32 devices in a mesh: seq: 4 (over x, core), blk: 8 (over z, y).
Axes of the slice: x: 2, y: 2, z: 4, core: 2. Of those that a mesh axis runs over, the one named last changes fastest.
Arguments:
- inputs: bfloat16 [32768, 1024], P(('seq', 'blk')), may hold values from -11 to 11
- cotangent: bfloat16 [32768, 1024], P(('seq', 'blk')), may hold values from -6 to 6
- timestep: int32 [4], P('seq'), may hold values from 0 to 4999
- lengths: int32 [4, 32], P('seq'), may hold values from 1 to 512, 8192 in all within a row
- padding: int32 [32768], P(('seq', 'blk')), may hold values 0 or 1
- time_weight: bfloat16 [1024], P(('seq', 'blk')), may hold values from -6 to 6
- time_bias: bfloat16 [1024], P(('seq', 'blk')), may hold values from -3 to 3
- inproj_weight: bfloat16 [1024, 3072], P(('seq', 'blk')), may hold values from -0.1875 to 0.1875
- query_bias: bfloat16 [1024], P(('seq', 'blk')), may hold values from -1.75 to 1.75
- value_bias: bfloat16 [1024], P(('seq', 'blk')), may hold values from -3 to 3
- outproj_weight: bfloat16 [1024, 1024], P(('seq', 'blk')), may hold values from -0.5 to 0.5
- outproj_bias: bfloat16 [1024], P(('seq', 'blk')), may hold values from -3 to 3
- first_gain: bfloat16 [1024], P(('seq', 'blk')), may hold values from 0.25 to 1.75
- first_shift: bfloat16 [1024], P(('seq', 'blk')), may hold values from -1.75 to 1.75
- upward_weight: bfloat16 [1024, 4096], P(('seq', 'blk')), may hold values from -0.1875 to 0.1875
- upward_bias: bfloat16 [4096], P(('seq', 'blk')), may hold values from -3 to 3
- downward_weight: bfloat16 [4096, 1024], P(('seq', 'blk')), may hold values from -0.09375 to 0.09375
- downward_bias: bfloat16 [1024], P(('seq', 'blk')), may hold values from -3 to 3
- second_gain: bfloat16 [1024], P(('seq', 'blk')), may hold values from 0.25 to 1.75
- second_shift: bfloat16 [1024], P(('seq', 'blk')), may hold values from -1.75 to 1.75
Outputs:
- layer_out: bfloat16 [32768, 1024], P(('seq', 'blk'))
- input_grad: bfloat16 [32768, 1024], P(('seq', 'blk'))
- time_weight_grad: float32 [1024], P(('seq', 'blk'))
- time_bias_grad: float32 [1024], P(('seq', 'blk'))
- inproj_weight_grad: float32 [1024, 3072], P(('seq', 'blk'))
- query_bias_grad: float32 [1024], P(('seq', 'blk'))
- value_bias_grad: float32 [1024], P(('seq', 'blk'))
- outproj_weight_grad: float32 [1024, 1024], P(('seq', 'blk'))
- outproj_bias_grad: float32 [1024], P(('seq', 'blk'))
- first_gain_grad: float32 [1024], P(('seq', 'blk'))
- first_shift_grad: float32 [1024], P(('seq', 'blk'))
- upward_weight_grad: float32 [1024, 4096], P(('seq', 'blk'))
- upward_bias_grad: float32 [4096], P(('seq', 'blk'))
- downward_weight_grad: float32 [4096, 1024], P(('seq', 'blk'))
- downward_bias_grad: float32 [1024], P(('seq', 'blk'))
- second_gain_grad: float32 [1024], P(('seq', 'blk'))
- second_shift_grad: float32 [1024], P(('seq', 'blk'))
- branch_rms: float32 [3], replicated
The draws below stay inside these ranges and needn't reach their ends.
Inputs may be any that keep to these rules, and one draw needn't show every extreme that they name: `lengths`: each row sums to 8192, and its longest item has exactly 512 tokens.
All inputs are finite; a program needn't handle non-finite values. No bound on the sum of `padding` on one device may be relied on, other than what follows from the above.
Results may differ from the reference program's by a relative error of at most 0.014.
The reference program's roundings to bfloat16 on the way count: a program that leaves them out, or rounds other values in their place, can miss the bound.
Values may be sent and summed in bfloat16 or wider, within the bound.
A program may use at most 384 MiB of HBM per device.

```python
import math
import jax
import jax.numpy as jnp
import numpy as np
from jax import lax

D = 1024
H = 16
HD = 64
FF = 4096
TOK_DEV = 1024
MAXLEN = 512
TSTEPS = 5000
LENGTH = 8192
SEQS = 4
TOKENS = 32768
ITEMS = 32
N_SEQ = 4
N_BLK = 8


def draw_inputs(key, part):
    key = jax.random.fold_in(key, 11)
    places = jnp.arange(TOKENS, dtype=jnp.float32)[:, None] / max(TOKENS - 1, 1)
    entries = jnp.clip(jax.random.normal(key, (TOKENS, D), jnp.float32), -6.0, 6.0)
    row_scale = 1.0 + 0.7320508 * places
    return (entries * row_scale).astype(jnp.bfloat16)


def touch_ends(values, rng, least, top_value):
    longest = values.shape.index(max(values.shape))
    spots = []
    for shift in (0, 1):
        where = [jax.random.randint(jax.random.fold_in(rng, axis), (), 0, length) for axis, length in enumerate(values.shape)]
        where[longest] = (where[longest] + shift) % values.shape[longest]
        spots.append(tuple(where))
    return values.at[spots[0]].set(least).at[spots[1]].set(top_value)


def steps_of(own_key, shape, split, least, top_value):
    level = 1.0
    for axis_at, parts in split:
        draws = jax.random.uniform(jax.random.fold_in(jax.random.fold_in(own_key, 6), axis_at), (parts,), jnp.float32, least / len(split), top_value / len(split))
        level = level * jnp.repeat(jnp.exp(draws), shape[axis_at] // parts).reshape((-1,) + (1,) * (len(shape) - 1 - axis_at))
    return level


def split_up(count, total, reach, slope):
    portions = [(1 << 20) // math.isqrt(grade ** slope) + 1 for grade in range(2, count + 1)]
    surplus, holding = total - reach - (count - 1), [1] * (count - 1)
    while surplus > 0:
        free = [i for i in range(count - 1) if holding[i] < reach]
        mass, budget = sum([portions[i] for i in free]), surplus
        for i in free:
            extra = min(reach - holding[i], max(1, budget * portions[i] // mass), surplus)
            holding[i] = holding[i] + extra
            surplus = surplus - extra
    return np.array([reach] + holding)


def uneven(own_key, amount, total, most, slope):
    if amount == 2:
        one = jax.random.randint(own_key, (), max(1, total - most), min(most, total - 1) + 1)
        return jnp.stack([one, total - one])
    sizes = jnp.asarray(split_up(amount, total, most, slope), jnp.int32)
    couples = (amount - 1) // 2
    giver, sink = sizes[1:1 + 2 * couples:2], sizes[2:2 + 2 * couples:2]
    room = jnp.minimum(giver - 1, most - sink)
    shifted = jax.random.randint(jax.random.fold_in(own_key, 1), (couples,), 0, 1 << 20) % (room + 1)
    sizes = sizes.at[1:1 + 2 * couples:2].set(giver - shifted).at[2:2 + 2 * couples:2].set(sink + shifted)
    return sizes[jax.random.permutation(jax.random.fold_in(own_key, 2), amount)]


def normal_values(rng, dims, width, bound, cuts=(), held_as=jnp.bfloat16):
    level = steps_of(rng, dims, cuts, -0.22, 0.18) if cuts else 1.0
    array = jax.random.normal(rng, dims, jnp.float32) * width * level
    return jnp.minimum(jnp.maximum(array, -bound), bound).astype(held_as)


def setup_inputs(seed: int = 0) -> dict:
    key_list = jax.random.split(jax.random.key(seed), 21)
    return {
        "inputs": draw_inputs(jax.random.fold_in(key_list[20], 71), 0),
        "cotangent": normal_values(key_list[1], (TOKENS, D), 1.0, 6.0, ((0, 32),)),
        "timestep": touch_ends(jax.random.randint(key_list[2], (SEQS,), 0, TSTEPS), jax.random.fold_in(key_list[2], 1), 0, TSTEPS - 1).astype(jnp.int32),
        "lengths": jax.vmap(lambda own: uneven(own, ITEMS, LENGTH, MAXLEN, 0))(jax.random.split(key_list[3], SEQS)).reshape((SEQS, ITEMS)).astype(jnp.int32),
        "padding": touch_ends((jax.random.randint(key_list[4], (TOKENS,), 0, 16) < 15).astype(jnp.int32), jax.random.fold_in(key_list[4], 1), 0, 1),
        "time_weight": normal_values(key_list[5], (D,), 1.0, 6.0, ((0, 32),)),
        "time_bias": normal_values(key_list[6], (D,), 0.5, 3.0, ((0, 32),)),
        "inproj_weight": normal_values(key_list[7], (D, 3 * D), D ** -0.5, 0.1875, ((0, 32),)),
        "query_bias": normal_values(key_list[8], (D,), 0.3, 1.75, ((0, 32),)),
        "value_bias": normal_values(key_list[9], (D,), 0.5, 3.0, ((0, 32),)),
        "outproj_weight": normal_values(key_list[10], (D, D), (D // 8) ** -0.5, 0.5, ((0, 32),)),
        "outproj_bias": normal_values(key_list[11], (D,), 0.5, 3.0, ((0, 32),)),
        "first_gain": jnp.clip(1.0 + 0.15 * jax.random.normal(key_list[12], (D,), jnp.float32), 0.25, 1.75).astype(jnp.bfloat16),
        "first_shift": normal_values(key_list[13], (D,), 0.3, 1.75, ((0, 32),)),
        "upward_weight": normal_values(key_list[14], (D, FF), D ** -0.5, 0.1875, ((0, 32),)),
        "upward_bias": normal_values(key_list[15], (FF,), 0.5, 3.0, ((0, 32),)),
        "downward_weight": normal_values(key_list[16], (FF, D), FF ** -0.5, 0.09375, ((0, 32),)),
        "downward_bias": normal_values(key_list[17], (D,), 0.5, 3.0, ((0, 32),)),
        "second_gain": jnp.clip(1.0 + 0.15 * jax.random.normal(key_list[18], (D,), jnp.float32), 0.25, 1.75).astype(jnp.bfloat16),
        "second_shift": normal_values(key_list[19], (D,), 0.3, 1.75, ((0, 32),)),
    }


HIGH = lax.Precision.HIGHEST
NEG_FILL = -1e+30

@jax.custom_vjp
def low(v):
    return lax.optimization_barrier(v.astype(jnp.bfloat16)).astype(jnp.float32)

@jax.custom_vjp
def low_back(v):
    return v

def low_keep(v):
    return (low(v), None)

def low_pass(kept, grad):
    return (grad,)

def back_keep(v):
    return (v, None)

def back_low(kept, grad):
    return (low(grad),)
low.defvjp(low_keep, low_pass)
low_back.defvjp(back_keep, back_low)

def matmul(left, right):
    return jnp.dot(left, right, precision=HIGH, preferred_element_type=jnp.float32)

def layer_norm(values, gain, shift):
    mean_val = lax.optimization_barrier(jnp.mean(values, axis=-1, keepdims=True))
    centered = values - mean_val
    spread_val = lax.optimization_barrier(jnp.mean(centered * centered, axis=-1, keepdims=True))
    return centered * lax.rsqrt(spread_val + 1e-05) * gain + shift

def attention(projected, item_row, keep_row):
    seq_len = projected.shape[0]
    query_all = projected[:, :D].reshape(seq_len, H, HD)
    key_all = jnp.pad(projected[:, D:2 * D], ((MAXLEN, MAXLEN), (0, 0))).reshape(seq_len + 2 * MAXLEN, H, HD)
    value_all = jnp.pad(projected[:, 2 * D:], ((MAXLEN, MAXLEN), (0, 0))).reshape(seq_len + 2 * MAXLEN, H, HD)
    item_pad = jnp.pad(item_row, (MAXLEN, MAXLEN), constant_values=-1)
    keep_pad = jnp.pad(keep_row, (MAXLEN, MAXLEN))
    blocks = seq_len // MAXLEN

    @jax.checkpoint
    def one_block(index):
        begin = (index * MAXLEN).astype(jnp.int32)
        query_blk = lax.dynamic_slice_in_dim(query_all, begin, MAXLEN, 0)
        key_win = lax.dynamic_slice_in_dim(key_all, begin, 3 * MAXLEN, 0)
        value_win = lax.dynamic_slice_in_dim(value_all, begin, 3 * MAXLEN, 0)
        query_item = lax.dynamic_slice_in_dim(item_row, begin, MAXLEN, 0)
        key_item = lax.dynamic_slice_in_dim(item_pad, begin, 3 * MAXLEN, 0)
        key_keep = lax.dynamic_slice_in_dim(keep_pad, begin, 3 * MAXLEN, 0)
        query_place = begin + jnp.arange(MAXLEN, dtype=jnp.int32)
        key_place = begin - MAXLEN + jnp.arange(3 * MAXLEN, dtype=jnp.int32)
        allowed = (query_item[:, None] == key_item[None, :]) & ((key_keep[None, :] == 1) | (query_place[:, None] == key_place[None, :]))
        score = jnp.einsum('qhd,khd->hqk', query_blk, key_win, precision=HIGH) * HD ** (-0.5)
        score = low_back(score)
        masked = jnp.where(allowed[None], score, NEG_FILL)
        row_top = lax.optimization_barrier(jnp.max(masked, axis=-1, keepdims=True))
        expo_vals = jnp.exp(masked - row_top)
        probs = low(expo_vals / lax.optimization_barrier(jnp.sum(expo_vals, axis=-1, keepdims=True)))
        result = jnp.einsum('hqk,khd->qhd', probs, value_win, precision=HIGH)
        return result.reshape(MAXLEN, D)
    outs = lax.map(one_block, jnp.arange(blocks, dtype=jnp.int32))
    return outs.reshape(seq_len, D)

def forward_seq(weights, values, time_value, ends, keep_row):
    time_weight, time_bias, inproj_weight, query_bias, value_bias, outproj_weight, outproj_bias, first_gain, first_shift, upward_weight, upward_bias, downward_weight, downward_bias, second_gain, second_shift = weights
    seq_len = values.shape[0]
    places = jnp.arange(seq_len, dtype=jnp.int32)
    item_row = lax.optimization_barrier(jnp.sum((ends[None, :] <= places[:, None]).astype(jnp.int32), axis=1)).astype(jnp.int32)
    start_vec = values + time_value * time_weight + time_bias
    zero_bias = jnp.zeros_like(query_bias)
    projected = matmul(low(start_vec), inproj_weight) + jnp.concatenate([query_bias, zero_bias, value_bias])
    projected = low(low_back(projected))
    attended = low(low_back(attention(projected, item_row, keep_row)))
    attn_branch = low_back(matmul(attended, outproj_weight) + outproj_bias)
    first_out = layer_norm(start_vec + attn_branch, first_gain, first_shift)
    upward = low_back(matmul(low(first_out), upward_weight) + upward_bias)
    hidden_low = low(jax.nn.gelu(upward, approximate=False))
    ffn_branch = low_back(matmul(hidden_low, downward_weight) + downward_bias)
    result = layer_norm(first_out + ffn_branch, second_gain, second_shift)
    sums = jnp.stack([jnp.sum(start_vec * start_vec), jnp.sum(attn_branch * attn_branch), jnp.sum(ffn_branch * ffn_branch)])
    return (result, sums)

def reference(inputs, cotangent, timestep, lengths, padding, time_weight, time_bias, inproj_weight, query_bias, value_bias, outproj_weight, outproj_bias, first_gain, first_shift, upward_weight, upward_bias, downward_weight, downward_bias, second_gain, second_shift):
    weights = tuple((item.astype(jnp.float32) for item in (time_weight, time_bias, inproj_weight, query_bias, value_bias, outproj_weight, outproj_bias, first_gain, first_shift, upward_weight, upward_bias, downward_weight, downward_bias, second_gain, second_shift)))
    seq_len = TOK_DEV * N_BLK
    seq_count = N_SEQ
    inputs_all = inputs.astype(jnp.float32).reshape(seq_count, seq_len, D)
    cot_all = cotangent.astype(jnp.float32).reshape(seq_count, seq_len, D)
    keep_all = padding.reshape(seq_count, seq_len)
    ends_all = jnp.cumsum(lengths, axis=1).astype(jnp.int32)
    times = timestep.astype(jnp.float32) / TSTEPS

    def per_sequence(carry, items):
        grad_total, sum_total = carry
        seq_in, seq_cot, time_value, ends, keep_row = items

        def forward(params, values):
            return forward_seq(params, values, time_value, ends, keep_row)
        result, pullback, sums = jax.vjp(forward, weights, seq_in, has_aux=True)
        grad_params, grad_values = pullback(seq_cot)
        grad_total = jax.tree.map(jnp.add, grad_total, grad_params)
        return ((grad_total, sum_total + sums), (result.astype(jnp.bfloat16), grad_values.astype(jnp.bfloat16)))
    start = (tuple((jnp.zeros_like(item) for item in weights)), jnp.zeros((3,), jnp.float32))
    (grad_total, sum_total), (results, grads_in) = lax.scan(per_sequence, start, (inputs_all, cot_all, times, ends_all, keep_all))
    branch_rms = jnp.sqrt(sum_total / (seq_count * seq_len * D))
    return (results.reshape(seq_count * seq_len, D), grads_in.reshape(seq_count * seq_len, D), grad_total[0], grad_total[1], grad_total[2], grad_total[3], grad_total[4], grad_total[5], grad_total[6], grad_total[7], grad_total[8], grad_total[9], grad_total[10], grad_total[11], grad_total[12], grad_total[13], grad_total[14], branch_rms)
```

```python
import functools

import jax
import jax.numpy as jnp
from jax import lax
from jax.experimental import pallas as pl
from jax.experimental.pallas import tpu as pltpu
from jax.sharding import PartitionSpec as P

HD=64
TQ = 256
NEG = -(2.0 ** 100)

def nt(a, b):
    return lax.dot_general(a, b, (((1,), (1,)), ((), ())), preferred_element_type=jnp.float32)

def nn(a, b):
    return jnp.dot(a, b, preferred_element_type=jnp.float32)

def fwd_kernel(tiles, lse_lane, lo_ref, n_ref, q_ref, k_ref, v_ref, qf_ref, kf_ref, o_ref, f_ref, ka, va, qa, sb, acc):
    step = pl.program_id(0)
    ext = k_ref.shape[0]
    half = (ext - tiles * TQ) // 2

    @pl.when(step == 0)
    def _():
        ka[:, 128:] = kf_ref[...]
        va[:, 128:] = jnp.ones((ext, 128), jnp.bfloat16)
        f_ref[...] = qf_ref[half : half + tiles * TQ, :]

    ka[:, :128] = k_ref[...]
    va[:, :128] = v_ref[...]
    lane = lax.broadcasted_iota(jnp.int32, (TQ, 128), 1)
    left = lane < HD
    for t in range(tiles):
        rows = slice(half + t * TQ, half + (t + 1) * TQ)
        q = q_ref[rows, :] * jnp.bfloat16(HD ** -0.5)
        zero = jnp.zeros_like(q)
        qa[:TQ, :128] = jnp.where(left, q, zero)
        qa[TQ:, :128] = jnp.where(left, zero, q)
        qa[:TQ, 128:] = qf_ref[rows, :]
        qa[TQ:, 128:] = qf_ref[rows, :]
        lo = lo_ref[t]
        count = n_ref[t]

        def scores(j, top):
            start = pl.multiple_of((lo + j) * TQ, TQ)
            s = nt(qa[...], ka[pl.ds(start, TQ), :])
            sb[j] = s
            return jnp.maximum(top, jnp.maximum(s[:, :128], s[:, 128:]))

        top = lax.fori_loop(0, count, scores, jnp.full((2 * TQ, 128), -jnp.inf, jnp.float32))
        top = jnp.max(top, axis=1, keepdims=True)
        acc[...] = jnp.zeros_like(acc)

        def weigh(j, carry):
            start = pl.multiple_of((lo + j) * TQ, TQ)
            p = jnp.exp(sb[j] - top).astype(jnp.bfloat16)
            acc[...] += nn(p, va[pl.ds(start, TQ), :])
            return carry

        lax.fori_loop(0, count, weigh, 0)
        total = acc[:, 128:]
        o = acc[:, :128] / total
        own = slice(t * TQ, (t + 1) * TQ)
        o_ref[own, :] = jnp.where(left, o[:TQ], o[TQ:]).astype(jnp.bfloat16)
        lse = top + jnp.log(total)
        feat = f_ref[own, :]
        for side in range(2):
            rest = lse[side * TQ : (side + 1) * TQ]
            for part in range(3):
                piece = rest.astype(jnp.bfloat16)
                rest = rest - piece.astype(jnp.float32)
                at = lse_lane + part * 16 + 2 * step + side
                feat = jnp.where(lane == at, piece, feat)
        f_ref[own, :] = feat


def attn_fwd(proj, qf, kf, lo, n, lse_lane, tok):
    ext, wide = proj.shape
    width = wide // 3
    pairs = width // 128
    tiles = tok // TQ
    col = lambda base: pl.BlockSpec((ext, 128), lambda i, *_: (0, base + i))
    fix = pl.BlockSpec((ext, 128), lambda i, *_: (0, 0))
    return pl.pallas_call(
        functools.partial(fwd_kernel, tiles, lse_lane),
        grid_spec=pltpu.PrefetchScalarGridSpec(
            num_scalar_prefetch=2,
            grid=(pairs,),
            in_specs=[col(0), col(pairs), col(2 * pairs), fix, fix],
            out_specs=[pl.BlockSpec((tok, 128), lambda i, *_: (0, i)), pl.BlockSpec((tok, 128), lambda i, *_: (0, 0))],
            scratch_shapes=[
                pltpu.VMEM((ext, 256), jnp.bfloat16),
                pltpu.VMEM((ext, 256), jnp.bfloat16),
                pltpu.VMEM((2 * TQ, 256), jnp.bfloat16),
                pltpu.VMEM((6, 2 * TQ, TQ), jnp.float32),
                pltpu.VMEM((2 * TQ, 256), jnp.float32),
            ],
        ),
        out_shape=[jax.ShapeDtypeStruct((tok, width), jnp.bfloat16), jax.ShapeDtypeStruct((tok, 128), jnp.bfloat16)],
        compiler_params=pltpu.CompilerParams(vmem_limit_bytes=48 << 20, dimension_semantics=("arbitrary",)),
        cost_estimate=pl.CostEstimate(flops=2 * 2 * tok * 768 * width * 2, bytes_accessed=8 << 20, transcendentals=tok * 768 * 16),
        name="attn_fwd",
    )(lo, n, proj, proj, proj, qf, kf)


def bwd_kernel(tiles, lse_lane, lo_ref, n_ref, q_ref, k_ref, v_ref, d_ref, qf_ref, kf_ref, df_ref, vf_ref, g_ref,
               ka, va, qa, da, acc, acc2):
    step = pl.program_id(0)
    ext = k_ref.shape[0]
    half = (ext - tiles * TQ) // 2

    @pl.when(step == 0)
    def _():
        ka[:, 128:] = kf_ref[...]
        va[:, 128:] = vf_ref[...]

    ka[:, :128] = k_ref[...]
    va[:, :128] = v_ref[...]
    lane = lax.broadcasted_iota(jnp.int32, (TQ, 128), 1)
    left = lane < HD
    for side in range(2):
        mine = left if side == 0 else ~left
        own_lane = (lane - lse_lane) % 16 == 2 * step + side
        for t in range(ext // TQ):
            rows = slice(t * TQ, (t + 1) * TQ)
            zero = jnp.zeros((TQ, 128), jnp.bfloat16)
            qa[t, side * TQ : (side + 1) * TQ, :128] = jnp.where(mine, q_ref[rows, :] * jnp.bfloat16(HD ** -0.5), zero)
            qa[t, side * TQ : (side + 1) * TQ, 128:] = jnp.where((lane < lse_lane) | own_lane, qf_ref[rows, :], zero)
            da[t, side * TQ : (side + 1) * TQ, :128] = jnp.where(mine, d_ref[rows, :], zero)
            da[t, side * TQ : (side + 1) * TQ, 128:] = jnp.where(own_lane, df_ref[rows, :], zero)
    first = half // TQ
    for t in range(tiles):
        rows = slice(half + t * TQ, half + (t + 1) * TQ)
        own = slice(t * TQ, (t + 1) * TQ)
        lo = lo_ref[t]
        count = n_ref[t]
        acc[...] = jnp.zeros_like(acc)
        acc2[...] = jnp.zeros_like(acc2)

        def query_pass(j, carry):
            start = pl.multiple_of((lo + j) * TQ, TQ)
            p = jnp.exp(nt(qa[first + t], ka[pl.ds(start, TQ), :]))
            g = (p * nt(da[first + t], va[pl.ds(start, TQ), :])).astype(jnp.bfloat16)
            acc[...] += nn(g, k_ref[pl.ds(start, TQ), :])
            return carry

        lax.fori_loop(0, count, query_pass, 0)
        g_ref[0, own, :] = (jnp.where(left, acc[:TQ], acc[TQ:]) * HD ** -0.5).astype(jnp.bfloat16)

        def key_pass(j, carry):
            at = lo + j
            p = jnp.exp(nt(ka[rows, :], qa[at]))
            g = (p * nt(va[rows, :], da[at])).astype(jnp.bfloat16)
            acc2[:, :128] += nn(g, qa[at, :, :128])
            acc2[:, 128:] += nn(p.astype(jnp.bfloat16), da[at, :, :128])
            return carry

        lax.fori_loop(0, count, key_pass, 0)
        g_ref[1, own, :] = acc2[:, :128].astype(jnp.bfloat16)
        g_ref[2, own, :] = acc2[:, 128:].astype(jnp.bfloat16)


def attn_bwd(proj, grad_ext, qf, kf, df, vf, lo, n, lse_lane, tok):
    ext, wide = proj.shape
    width = wide // 3
    pairs = width // 128
    tiles = tok // TQ
    col = lambda base: pl.BlockSpec((ext, 128), lambda i, *_: (0, base + i))
    fix = pl.BlockSpec((ext, 128), lambda i, *_: (0, 0))
    return pl.pallas_call(
        functools.partial(bwd_kernel, tiles, lse_lane),
        grid_spec=pltpu.PrefetchScalarGridSpec(
            num_scalar_prefetch=2,
            grid=(pairs,),
            in_specs=[col(0), col(pairs), col(2 * pairs), col(0), fix, fix, fix, fix],
            out_specs=pl.BlockSpec((3, tok, 128), lambda i, *_: (0, 0, i)),
            scratch_shapes=[
                pltpu.VMEM((ext, 256), jnp.bfloat16),
                pltpu.VMEM((ext, 256), jnp.bfloat16),
                pltpu.VMEM((ext // TQ, 2 * TQ, 256), jnp.bfloat16),
                pltpu.VMEM((ext // TQ, 2 * TQ, 256), jnp.bfloat16),
                pltpu.VMEM((2 * TQ, 128), jnp.float32),
                pltpu.VMEM((TQ, 256), jnp.float32),
            ],
        ),
        out_shape=jax.ShapeDtypeStruct((3, tok, width), jnp.bfloat16),
        compiler_params=pltpu.CompilerParams(vmem_limit_bytes=48 << 20, dimension_semantics=("arbitrary",)),
        cost_estimate=pl.CostEstimate(flops=2 * 4 * tok * 768 * width * 2, bytes_accessed=16 << 20, transcendentals=tok * 768 * 32),
        name="attn_bwd",
    )(lo, n, proj, proj, proj, grad_ext, qf, kf, df, vf)


def bits(values, count):
    planes = (values[:, None] >> jnp.arange(count, dtype=jnp.int32)[None, :]) & 1
    return planes.astype(jnp.float32)


def features(item, keep, tok, n_items):
    ext = item.shape[0]
    nb = (n_items + 1).bit_length()
    pb = (ext - 1).bit_length()
    lse_lane = 2 * (nb + pb)
    assert lse_lane + 48 <= 128
    ib = bits(item + 1, nb)
    ps = bits(jnp.arange(ext, dtype=jnp.int32), pb)
    kept = keep.astype(jnp.float32)[:, None]
    qf = jnp.concatenate([ib, 1 - ib, ps, 1 - ps, jnp.zeros((ext, 128 - lse_lane), jnp.float32)], axis=1)
    kf = jnp.concatenate([NEG * kept * (1 - ib), NEG * kept * ib, NEG * (1 - kept) * (1 - ps), NEG * (1 - kept) * ps,
                          -jnp.ones((ext, 48), jnp.float32), jnp.zeros((ext, 80 - lse_lane), jnp.float32)], axis=1)
    return qf.astype(jnp.bfloat16), kf.astype(jnp.bfloat16), lse_lane


def stat_lanes(ext, lse_lane):
    lane = jnp.arange(128)
    vf = jnp.where((lane >= lse_lane) & (lane < lse_lane + 48), -1.0, 0.0)
    return jnp.broadcast_to(vf[None], (ext, 128)).astype(jnp.bfloat16)


def delta_features(delta, lse_lane):
    parts = []
    rest = delta
    for _ in range(3):
        piece = rest.astype(jnp.bfloat16)
        parts.append(piece)
        rest = rest - piece.astype(jnp.float32)
    return jnp.pad(jnp.concatenate(parts, axis=1), ((0, 0), (lse_lane, 80 - lse_lane)))


def key_range(ends, offset, tok, half):
    tiles = tok // TQ
    ext = tok + 2 * half
    starts = jnp.concatenate([jnp.zeros((1,), ends.dtype), ends[:-1]])
    first = offset + jnp.arange(tiles, dtype=jnp.int32) * TQ
    last = first + TQ - 1
    begin = jnp.max(jnp.where(starts[None, :] <= first[:, None], starts[None, :], 0), axis=1)
    big = jnp.int32(1 << 30)
    stop = jnp.min(jnp.where(ends[None, :] > last[:, None], ends[None, :], big), axis=1)
    begin = jnp.maximum(begin - offset + half, 0)
    stop = jnp.minimum(stop - offset + half, ext)
    lo = begin // TQ
    return lo.astype(jnp.int32), ((stop + TQ - 1) // TQ - lo).astype(jnp.int32)


H = 16
MAXLEN = 512
TSTEPS = 5000
AXES = ("seq", "blk")
SMALL = 10


def as_float(value):
    return value.astype(jnp.float32)


def low(value):
    return value.astype(jnp.bfloat16)


def row_dot(left, right):
    return lax.dot_general(left, right, (((0,), (0,)), ((), ())), preferred_element_type=jnp.float32)


def place():
    seq, blk = lax.axis_index("seq"), lax.axis_index("blk")
    return seq // 2, seq % 2, blk // 2, blk % 2


def swap(value, dx=0, dc=0, dz=0, dy=0):
    pairs = []
    for i in range(32):
        seq, blk = i // 8, i % 8
        seq, blk = seq ^ (2 * dx + dc), blk ^ (2 * dz + dy)
        pairs.append((i, seq * 8 + blk))
    return lax.ppermute(value, AXES, pairs)


def ordered(bit, own, other, axis):
    return jnp.where(bit == 0, jnp.stack([own, other], axis), jnp.stack([other, own], axis))


def cut(columns):
    return columns // 256 * 128


def gather_rows(shard):
    x, c, z, y = place()
    parts = [shard] + [swap(shard, dz=k) for k in (1, 2, 3)]
    parts = [jnp.where(z % 2 == 0, parts[i], parts[i ^ 1]) for i in range(4)]
    line = jnp.stack([jnp.where(z < 2, parts[i], parts[i ^ 2]) for i in range(4)])
    at = cut(shard.shape[1])
    one, two = line[..., :at], line[..., at:]
    one = ordered(x, one, swap(one, dx=1), 0)
    two = ordered(y, two, swap(two, dy=1), 1)
    one = ordered(y, one, swap(one, dy=1), 2)
    two = ordered(x, two, swap(two, dx=1), 0)
    mine = jnp.concatenate([one, two], axis=-1)
    return mine, swap(mine, dc=1)


def gather(shard):
    mine, other = gather_rows(shard)
    full = ordered(place()[1], mine, other, 1)
    return full.reshape(-1, shard.shape[1])


def pick(value, index, axis):
    return lax.dynamic_index_in_dim(value, index, axis, keepdims=False)


def scatter_sum(value):
    x, c, z, y = place()
    value = value.reshape(2, 2, 4, 2, value.shape[0] // 32, value.shape[1])
    total = as_float(pick(value, c, 1)) + as_float(swap(pick(value, 1 - c, 1), dc=1))
    at = cut(value.shape[-1])
    one, two = low(total[..., :at]), low(total[..., at:])
    one = low(as_float(pick(one, y, 2)) + as_float(swap(pick(one, 1 - y, 2), dy=1)))
    two = low(as_float(pick(two, x, 0)) + as_float(swap(pick(two, 1 - x, 0), dx=1)))
    one = low(as_float(pick(one, x, 0)) + as_float(swap(pick(one, 1 - x, 0), dx=1)))
    two = low(as_float(pick(two, y, 1)) + as_float(swap(pick(two, 1 - y, 1), dy=1)))
    line = jnp.concatenate([one, two], axis=-1)
    total = as_float(pick(line, z, 0))
    for k in (1, 2, 3):
        total = total + as_float(swap(pick(line, z ^ k, 0), dz=k))
    return total


def total_of(values):
    for step in (dict(dc=1), dict(dx=1), dict(dy=1), dict(dz=1), dict(dz=2)):
        values = values + swap(values, **step)
    return values


def neighbours(low_part, high_part):
    count = lax.axis_size("blk")
    up = [(i, i + 1) for i in range(count - 1)]
    down = [(i + 1, i) for i in range(count - 1)]
    return lax.ppermute(high_part, "blk", up), lax.ppermute(low_part, "blk", down)


def norm_forward(values):
    mean_val = jnp.mean(values, axis=-1, keepdims=True)
    centered = values - mean_val
    inv = lax.rsqrt(jnp.mean(centered * centered, axis=-1, keepdims=True) + 1e-05)
    return centered * inv, inv


def norm_backward(grad, normal, inv, gain):
    scaled = grad * gain
    grad_in = inv * (
        scaled
        - jnp.mean(scaled, axis=-1, keepdims=True)
        - normal * jnp.mean(scaled * normal, axis=-1, keepdims=True)
    )
    return grad_in, jnp.sum(grad * normal, axis=0), jnp.sum(grad, axis=0)


def item_of(ends, places):
    return jnp.sum((ends[None, :] <= places[:, None]).astype(jnp.int32), axis=1)


def per_device(fast, inputs, cotangent, timestep, lengths, padding, *shards):
    (time_weight, time_bias, inproj, query_bias, value_bias, outproj, outproj_bias, first_gain, first_shift,
     upward_w, upward_bias, downward_w, downward_bias, second_gain, second_shift) = shards
    small = (time_weight, time_bias, query_bias, value_bias, outproj_bias, first_gain, first_shift,
             downward_bias, second_gain, second_shift)
    tok, width = inputs.shape
    half = MAXLEN
    ext = tok + 2 * half
    hidden = upward_w.shape[1]

    mark = jnp.zeros((16, width), jnp.bfloat16)
    keep_own = low(padding)
    edge_low = jnp.concatenate([inputs[:half], mark.at[0, :half].set(keep_own[:half])])
    edge_high = jnp.concatenate([inputs[tok - half :], mark.at[0, :half].set(keep_own[tok - half :])])
    from_low, from_high = neighbours(edge_low, edge_high)

    if fast:
        rows = time_weight.shape[0]
        cols = [v[:, None] for v in small] + [upward_bias.reshape(-1, rows).T]
        cols = jnp.concatenate(cols, axis=1)
        cols = jnp.pad(cols, ((0, 0), (0, 128 - cols.shape[1])))
        first = gather(jnp.concatenate([inproj, cols], axis=1))
        second = gather(jnp.concatenate([outproj, upward_w], axis=1))
        downward_f = gather(downward_w)
        inproj_f = first[:, : 3 * width]
        small_f = as_float(first[:, 3 * width :].T)
        upward_bias_f = small_f[SMALL : SMALL + hidden // width]
        upward_bias_f = upward_bias_f.reshape(-1, width // rows, rows).transpose(1, 0, 2).reshape(hidden)
        outproj_f, upward_f = second[:, :width], second[:, width:]
    else:
        whole = lambda v: lax.all_gather(v, AXES, axis=0, tiled=True)
        inproj_f, outproj_f, upward_f, downward_f = map(whole, (inproj, outproj, upward_w, downward_w))
        small_f = [as_float(whole(v)) for v in small]
        upward_bias_f = as_float(whole(upward_bias))
    (time_weight_f, time_bias_f, query_bias_f, value_bias_f, outproj_bias_f, first_gain_f, first_shift_f,
     downward_bias_f, second_gain_f, second_shift_f) = [small_f[i] for i in range(SMALL)]

    offset = lax.axis_index("blk") * tok
    ends = jnp.cumsum(lengths[0]).astype(jnp.int32)
    places = offset - half + jnp.arange(ext, dtype=jnp.int32)
    item = jnp.where(places >= 0, item_of(ends, places), -1)
    keep = jnp.concatenate([from_low[half, :half], keep_own, from_high[half, :half]])
    query_feat, key_feat, lane = features(item, as_float(keep) > 0.5, tok, lengths.shape[1])
    lo, count = key_range(ends, offset, tok, half)

    time_value = as_float(timestep[0]) / TSTEPS
    shift = time_value * time_weight_f + time_bias_f
    start_of = lambda v: as_float(v) + time_value * time_weight_f + time_bias_f
    start_vec = start_of(inputs)
    start_low = low(start_vec)
    start_ext = jnp.concatenate([low(start_of(from_low[:half])), start_low, low(start_of(from_high[:half]))])
    proj_bias = jnp.concatenate([query_bias_f, jnp.zeros_like(query_bias_f), value_bias_f])
    projected = low(jnp.dot(start_ext, inproj_f, preferred_element_type=jnp.float32) + proj_bias)

    attended, query_feat_own = attn_fwd(projected, query_feat, key_feat, lo, count, lane, tok)
    attn_branch = jnp.dot(attended, outproj_f, preferred_element_type=jnp.float32) + outproj_bias_f
    first_normal, first_inv = norm_forward(start_vec + attn_branch)
    first_out = first_normal * first_gain_f + first_shift_f
    first_low = low(first_out)
    upward = jnp.dot(first_low, upward_f, preferred_element_type=jnp.float32) + upward_bias_f
    phi = 0.5 * (1.0 + lax.erf(upward * 2.0**-0.5))
    hidden_low = low(upward * phi)
    slope = phi + upward * (jnp.exp(-0.5 * upward * upward) * 0.3989422804014327)
    ffn_branch = jnp.dot(hidden_low, downward_f, preferred_element_type=jnp.float32) + downward_bias_f
    second_normal, second_inv = norm_forward(first_out + ffn_branch)
    layer_out = low(second_normal * second_gain_f + second_shift_f)
    sums = jnp.stack([jnp.sum(v * v) for v in (start_vec, attn_branch, ffn_branch)])
    sums = total_of(sums) if fast else lax.psum(sums, AXES)
    branch_rms = jnp.sqrt(sums / (tok * width * lax.axis_size(AXES)))

    grad_second_in, grad_second_gain, grad_second_shift = norm_backward(
        as_float(cotangent), second_normal, second_inv, second_gain_f
    )
    grad_ffn_low = low(grad_second_in)
    grad_down_weight = row_dot(hidden_low, grad_ffn_low)
    grad_down_bias = jnp.sum(as_float(grad_ffn_low), axis=0)
    grad_up_low = low(nt(grad_ffn_low, downward_f) * slope)
    grad_up_weight = row_dot(first_low, grad_up_low)
    grad_up_bias = jnp.sum(as_float(grad_up_low), axis=0)
    grad_first = grad_second_in + nt(grad_up_low, upward_f)
    grad_first_in, grad_first_gain, grad_first_shift = norm_backward(grad_first, first_normal, first_inv, first_gain_f)
    grad_branch_low = low(grad_first_in)
    grad_out_weight = row_dot(attended, grad_branch_low)
    grad_out_bias = jnp.sum(as_float(grad_branch_low), axis=0)
    grad_attended = low(nt(grad_branch_low, outproj_f))

    head = jnp.arange(width)[:, None] // HD == jnp.arange(H)[None, :]
    delta = jnp.dot(
        as_float(grad_attended) * as_float(attended), as_float(head), precision=lax.Precision.HIGHEST
    )
    stats = jnp.concatenate(
        [query_feat_own[:, lane : lane + 48], delta_features(delta, 0)[:, :48], jnp.zeros((tok, 32), jnp.bfloat16)], axis=1
    )
    packed = jnp.concatenate([grad_attended, stats], axis=1)
    back_low, back_high = neighbours(packed[:half], packed[tok - half :])
    packed = jnp.concatenate([back_low, packed, back_high])
    grad_ext = packed[:, :width]
    query_feat = jnp.concatenate([query_feat[:, :lane], packed[:, width : width + 48], query_feat[:, lane + 48 :]], axis=1)
    delta_feat = jnp.pad(packed[:, width + 48 : width + 96], ((0, 0), (lane, 80 - lane)))
    grad_proj = attn_bwd(projected, grad_ext, query_feat, key_feat, delta_feat, stat_lanes(ext, lane), lo, count, lane, tok)

    grad_proj_low = jnp.concatenate([grad_proj[0], grad_proj[1], grad_proj[2]], axis=1)
    grad_in_weight = row_dot(start_low, grad_proj_low)
    grad_query_bias = jnp.sum(as_float(grad_proj[0]), axis=0)
    grad_value_bias = jnp.sum(as_float(grad_proj[2]), axis=0)
    grad_start = grad_first_in + nt(grad_proj_low, inproj_f)
    grad_time_bias = jnp.sum(grad_start, axis=0)
    grad_time_weight = time_value * grad_time_bias
    input_grad = low(grad_start)

    small_grads = (grad_time_weight, grad_time_bias, grad_query_bias, grad_value_bias, grad_out_bias, grad_first_gain,
                   grad_first_shift, grad_down_bias, grad_second_gain, grad_second_shift)
    if fast:
        down_share = scatter_sum(low(grad_down_weight))
        up_share = scatter_sum(low(grad_up_weight))
        out_share = scatter_sum(low(grad_out_weight))
        cols = grad_up_bias.reshape(width // rows, -1, rows).transpose(1, 0, 2).reshape(-1, width)
        cols = jnp.concatenate([jnp.stack(small_grads), cols]).T
        cols = jnp.pad(cols, ((0, 0), (0, 128 - cols.shape[1])))
        last = scatter_sum(low(jnp.concatenate([grad_in_weight, cols], axis=1)))
        in_share = last[:, : 3 * width]
        small_shares = [last[:, 3 * width + i] for i in range(SMALL)]
        up_bias_share = last[:, 3 * width + SMALL : 3 * width + SMALL + hidden // width].T.reshape(-1)
    else:
        share = lambda v: lax.psum_scatter(v, AXES, scatter_dimension=0, tiled=True)
        down_share, up_share, out_share, in_share, up_bias_share = map(
            share, (grad_down_weight, grad_up_weight, grad_out_weight, grad_in_weight, grad_up_bias)
        )
        small_shares = [share(v) for v in small_grads]
    (time_weight_s, time_bias_s, query_bias_s, value_bias_s, out_bias_s, first_gain_s, first_shift_s,
     down_bias_s, second_gain_s, second_shift_s) = small_shares
    return (layer_out, input_grad, time_weight_s, time_bias_s, in_share, query_bias_s, value_bias_s, out_share,
            out_bias_s, first_gain_s, first_shift_s, up_share, up_bias_share, down_share, down_bias_s,
            second_gain_s, second_shift_s, branch_rms)


def solution(mesh):
    both = P(AXES)
    matrix = P(AXES, None)
    in_specs = (matrix, matrix, P("seq"), P("seq", None), both,
                both, both, matrix, both, both, matrix, both, both, both, matrix, both, matrix, both, both, both)
    out_specs = (matrix, matrix, both, both, matrix, both, both, matrix, both, both, both, matrix, both, matrix,
                 both, both, both, P())
    fast = dict(mesh.shape) == {"seq": 4, "blk": 8}
    return jax.shard_map(
        functools.partial(per_device, fast), mesh=mesh, in_specs=in_specs, out_specs=out_specs, check_vma=False
    )
```

```python
import functools

import jax
import jax.numpy as jnp
from jax import lax
from jax.experimental import pallas as pl
from jax.experimental.pallas import tpu as pltpu
from jax.sharding import PartitionSpec as P

HD=64
TQ = 256
NEG = -(2.0 ** 100)

def nt(a, b):
    return lax.dot_general(a, b, (((1,), (1,)), ((), ())), preferred_element_type=jnp.float32)

def nn(a, b):
    return jnp.dot(a, b, preferred_element_type=jnp.float32)

def fwd_kernel(tiles, lse_lane, lo_ref, n_ref, q_ref, k_ref, v_ref, qf_ref, kf_ref, o_ref, f_ref, ka, va, qa, sb, acc):
    step = pl.program_id(0)
    ext = k_ref.shape[0]
    half = (ext - tiles * TQ) // 2

    @pl.when(step == 0)
    def _():
        ka[:, 128:] = kf_ref[...]
        va[:, 128:] = jnp.ones((ext, 128), jnp.bfloat16)
        f_ref[...] = qf_ref[half : half + tiles * TQ, :]

    ka[:, :128] = k_ref[...]
    va[:, :128] = v_ref[...]
    lane = lax.broadcasted_iota(jnp.int32, (TQ, 128), 1)
    left = lane < HD
    for t in range(tiles):
        rows = slice(half + t * TQ, half + (t + 1) * TQ)
        q = q_ref[rows, :] * jnp.bfloat16(HD ** -0.5)
        zero = jnp.zeros_like(q)
        qa[:TQ, :128] = jnp.where(left, q, zero)
        qa[TQ:, :128] = jnp.where(left, zero, q)
        qa[:TQ, 128:] = qf_ref[rows, :]
        qa[TQ:, 128:] = qf_ref[rows, :]
        lo = lo_ref[t]
        count = n_ref[t]

        def scores(j, top):
            start = pl.multiple_of((lo + j) * TQ, TQ)
            s = nt(qa[...], ka[pl.ds(start, TQ), :])
            sb[j] = s
            return jnp.maximum(top, jnp.maximum(s[:, :128], s[:, 128:]))

        top = lax.fori_loop(0, count, scores, jnp.full((2 * TQ, 128), -jnp.inf, jnp.float32))
        top = jnp.max(top, axis=1, keepdims=True)
        acc[...] = jnp.zeros_like(acc)

        def weigh(j, carry):
            start = pl.multiple_of((lo + j) * TQ, TQ)
            p = jnp.exp(sb[j] - top).astype(jnp.bfloat16)
            acc[...] += nn(p, va[pl.ds(start, TQ), :])
            return carry

        lax.fori_loop(0, count, weigh, 0)
        total = acc[:, 128:]
        o = acc[:, :128] / total
        own = slice(t * TQ, (t + 1) * TQ)
        o_ref[own, :] = jnp.where(left, o[:TQ], o[TQ:]).astype(jnp.bfloat16)
        lse = top + jnp.log(total)
        feat = f_ref[own, :]
        for side in range(2):
            rest = lse[side * TQ : (side + 1) * TQ]
            for part in range(3):
                piece = rest.astype(jnp.bfloat16)
                rest = rest - piece.astype(jnp.float32)
                at = lse_lane + part * 16 + 2 * step + side
                feat = jnp.where(lane == at, piece, feat)
        f_ref[own, :] = feat


def attn_fwd(proj, qf, kf, lo, n, lse_lane, tok):
    ext, wide = proj.shape
    width = wide // 3
    pairs = width // 128
    tiles = tok // TQ
    col = lambda base: pl.BlockSpec((ext, 128), lambda i, *_: (0, base + i))
    fix = pl.BlockSpec((ext, 128), lambda i, *_: (0, 0))
    return pl.pallas_call(
        functools.partial(fwd_kernel, tiles, lse_lane),
        grid_spec=pltpu.PrefetchScalarGridSpec(
            num_scalar_prefetch=2,
            grid=(pairs,),
            in_specs=[col(0), col(pairs), col(2 * pairs), fix, fix],
            out_specs=[pl.BlockSpec((tok, 128), lambda i, *_: (0, i)), pl.BlockSpec((tok, 128), lambda i, *_: (0, 0))],
            scratch_shapes=[
                pltpu.VMEM((ext, 256), jnp.bfloat16),
                pltpu.VMEM((ext, 256), jnp.bfloat16),
                pltpu.VMEM((2 * TQ, 256), jnp.bfloat16),
                pltpu.VMEM((6, 2 * TQ, TQ), jnp.float32),
                pltpu.VMEM((2 * TQ, 256), jnp.float32),
            ],
        ),
        out_shape=[jax.ShapeDtypeStruct((tok, width), jnp.bfloat16), jax.ShapeDtypeStruct((tok, 128), jnp.bfloat16)],
        compiler_params=pltpu.CompilerParams(vmem_limit_bytes=48 << 20, dimension_semantics=("arbitrary",)),
        cost_estimate=pl.CostEstimate(flops=2 * 2 * tok * 768 * width * 2, bytes_accessed=8 << 20, transcendentals=tok * 768 * 16),
        name="attn_fwd",
    )(lo, n, proj, proj, proj, qf, kf)


def bwd_kernel(tiles, lse_lane, lo_ref, n_ref, q_ref, k_ref, v_ref, d_ref, qf_ref, kf_ref, df_ref, vf_ref, g_ref,
               ka, va, qa, da, acc, acc2):
    step = pl.program_id(0)
    ext = k_ref.shape[0]
    half = (ext - tiles * TQ) // 2

    @pl.when(step == 0)
    def _():
        ka[:, 128:] = kf_ref[...]
        va[:, 128:] = vf_ref[...]

    ka[:, :128] = k_ref[...]
    va[:, :128] = v_ref[...]
    lane = lax.broadcasted_iota(jnp.int32, (TQ, 128), 1)
    left = lane < HD
    for side in range(2):
        mine = left if side == 0 else ~left
        own_lane = (lane - lse_lane) % 16 == 2 * step + side
        for t in range(ext // TQ):
            rows = slice(t * TQ, (t + 1) * TQ)
            zero = jnp.zeros((TQ, 128), jnp.bfloat16)
            qa[t, side * TQ : (side + 1) * TQ, :128] = jnp.where(mine, q_ref[rows, :] * jnp.bfloat16(HD ** -0.5), zero)
            qa[t, side * TQ : (side + 1) * TQ, 128:] = jnp.where((lane < lse_lane) | own_lane, qf_ref[rows, :], zero)
            da[t, side * TQ : (side + 1) * TQ, :128] = jnp.where(mine, d_ref[rows, :], zero)
            da[t, side * TQ : (side + 1) * TQ, 128:] = jnp.where(own_lane, df_ref[rows, :], zero)
    first = half // TQ
    for t in range(tiles):
        rows = slice(half + t * TQ, half + (t + 1) * TQ)
        own = slice(t * TQ, (t + 1) * TQ)
        lo = lo_ref[t]
        count = n_ref[t]
        acc[...] = jnp.zeros_like(acc)
        acc2[...] = jnp.zeros_like(acc2)

        def query_pass(j, carry):
            start = pl.multiple_of((lo + j) * TQ, TQ)
            p = jnp.exp(nt(qa[first + t], ka[pl.ds(start, TQ), :]))
            g = (p * nt(da[first + t], va[pl.ds(start, TQ), :])).astype(jnp.bfloat16)
            acc[...] += nn(g, k_ref[pl.ds(start, TQ), :])
            return carry

        lax.fori_loop(0, count, query_pass, 0)
        g_ref[0, own, :] = (jnp.where(left, acc[:TQ], acc[TQ:]) * HD ** -0.5).astype(jnp.bfloat16)

        def key_pass(j, carry):
            at = lo + j
            p = jnp.exp(nt(ka[rows, :], qa[at]))
            g = (p * nt(va[rows, :], da[at])).astype(jnp.bfloat16)
            acc2[:, :128] += nn(g, qa[at, :, :128])
            acc2[:, 128:] += nn(p.astype(jnp.bfloat16), da[at, :, :128])
            return carry

        lax.fori_loop(0, count, key_pass, 0)
        g_ref[1, own, :] = acc2[:, :128].astype(jnp.bfloat16)
        g_ref[2, own, :] = acc2[:, 128:].astype(jnp.bfloat16)


def attn_bwd(proj, grad_ext, qf, kf, df, vf, lo, n, lse_lane, tok):
    ext, wide = proj.shape
    width = wide // 3
    pairs = width // 128
    tiles = tok // TQ
    col = lambda base: pl.BlockSpec((ext, 128), lambda i, *_: (0, base + i))
    fix = pl.BlockSpec((ext, 128), lambda i, *_: (0, 0))
    return pl.pallas_call(
        functools.partial(bwd_kernel, tiles, lse_lane),
        grid_spec=pltpu.PrefetchScalarGridSpec(
            num_scalar_prefetch=2,
            grid=(pairs,),
            in_specs=[col(0), col(pairs), col(2 * pairs), col(0), fix, fix, fix, fix],
            out_specs=pl.BlockSpec((3, tok, 128), lambda i, *_: (0, 0, i)),
            scratch_shapes=[
                pltpu.VMEM((ext, 256), jnp.bfloat16),
                pltpu.VMEM((ext, 256), jnp.bfloat16),
                pltpu.VMEM((ext // TQ, 2 * TQ, 256), jnp.bfloat16),
                pltpu.VMEM((ext // TQ, 2 * TQ, 256), jnp.bfloat16),
                pltpu.VMEM((2 * TQ, 128), jnp.float32),
                pltpu.VMEM((TQ, 256), jnp.float32),
            ],
        ),
        out_shape=jax.ShapeDtypeStruct((3, tok, width), jnp.bfloat16),
        compiler_params=pltpu.CompilerParams(vmem_limit_bytes=48 << 20, dimension_semantics=("arbitrary",)),
        cost_estimate=pl.CostEstimate(flops=2 * 4 * tok * 768 * width * 2, bytes_accessed=16 << 20, transcendentals=tok * 768 * 32),
        name="attn_bwd",
    )(lo, n, proj, proj, proj, grad_ext, qf, kf, df, vf)


def bits(values, count):
    planes = (values[:, None] >> jnp.arange(count, dtype=jnp.int32)[None, :]) & 1
    return planes.astype(jnp.float32)


def features(item, keep, tok, n_items):
    ext = item.shape[0]
    nb = (n_items + 1).bit_length()
    pb = (ext - 1).bit_length()
    lse_lane = 2 * (nb + pb)
    assert lse_lane + 48 <= 128
    ib = bits(item + 1, nb)
    ps = bits(jnp.arange(ext, dtype=jnp.int32), pb)
    kept = keep.astype(jnp.float32)[:, None]
    qf = jnp.concatenate([ib, 1 - ib, ps, 1 - ps, jnp.zeros((ext, 128 - lse_lane), jnp.float32)], axis=1)
    kf = jnp.concatenate([NEG * kept * (1 - ib), NEG * kept * ib, NEG * (1 - kept) * (1 - ps), NEG * (1 - kept) * ps,
                          -jnp.ones((ext, 48), jnp.float32), jnp.zeros((ext, 80 - lse_lane), jnp.float32)], axis=1)
    return qf.astype(jnp.bfloat16), kf.astype(jnp.bfloat16), lse_lane


def stat_lanes(ext, lse_lane):
    lane = jnp.arange(128)
    vf = jnp.where((lane >= lse_lane) & (lane < lse_lane + 48), -1.0, 0.0)
    return jnp.broadcast_to(vf[None], (ext, 128)).astype(jnp.bfloat16)


def delta_features(delta, lse_lane):
    parts = []
    rest = delta
    for _ in range(3):
        piece = rest.astype(jnp.bfloat16)
        parts.append(piece)
        rest = rest - piece.astype(jnp.float32)
    return jnp.pad(jnp.concatenate(parts, axis=1), ((0, 0), (lse_lane, 80 - lse_lane)))


def key_range(ends, offset, tok, half):
    tiles = tok // TQ
    ext = tok + 2 * half
    starts = jnp.concatenate([jnp.zeros((1,), ends.dtype), ends[:-1]])
    first = offset + jnp.arange(tiles, dtype=jnp.int32) * TQ
    last = first + TQ - 1
    begin = jnp.max(jnp.where(starts[None, :] <= first[:, None], starts[None, :], 0), axis=1)
    big = jnp.int32(1 << 30)
    stop = jnp.min(jnp.where(ends[None, :] > last[:, None], ends[None, :], big), axis=1)
    begin = jnp.maximum(begin - offset + half, 0)
    stop = jnp.minimum(stop - offset + half, ext)
    lo = begin // TQ
    return lo.astype(jnp.int32), ((stop + TQ - 1) // TQ - lo).astype(jnp.int32)


MESH = pl.DeviceIdType.MESH


def coords():
    seq, blk = lax.axis_index("seq"), lax.axis_index("blk")
    return seq // 2, lax.rem(seq, 2), blk // 2, lax.rem(blk, 2)


def device_at(x, c, z, y):
    return (x * 2 + c, z * 2 + y)


def other_z(z, k):
    low_bit = lax.rem(z, 2)
    high_bit = z // 2
    if k & 1:
        low_bit = 1 - low_bit
    if k & 2:
        high_bit = 1 - high_bit
    return high_bit * 2 + low_bit


def partners():
    x, c, z, y = coords()
    return {
        "x": device_at(1 - x, c, z, y),
        "y": device_at(x, c, z, 1 - y),
        "c": device_at(x, 1 - c, z, y),
        1: device_at(x, c, other_z(z, 1), y),
        2: device_at(x, c, other_z(z, 2), y),
        3: device_at(x, c, other_z(z, 3), y),
    }


def meet(to):
    barrier = pltpu.get_barrier_semaphore()
    for device in to.values():
        pl.semaphore_signal(barrier, inc=1, device_id=device, device_id_type=MESH)
    pl.semaphore_wait(barrier, len(to))


class Sends:
    def __init__(self, send_sem, recv_sem, to):
        self.send_sem, self.recv_sem, self.to, self.used, self.live = send_sem, recv_sem, to, 0, []

    def start(self, src, dst, partner):
        copy = pltpu.make_async_remote_copy(
            src_ref=src, dst_ref=dst, send_sem=self.send_sem.at[self.used], recv_sem=self.recv_sem.at[self.used],
            device_id=self.to[partner], device_id_type=MESH,
        )
        copy.start()
        self.used += 1
        self.live.append(copy)
        return copy

    def finish(self):
        for copy in self.live:
            copy.wait_send()


def gather_plan(shard, full, sends, local, base, wide):
    x, c, z, y = coords()
    at = cut(wide)
    every, one, two = pl.ds(base, wide), pl.ds(base, at), pl.ds(base + at, wide - at)

    def send(partner, *index):
        return sends.start(full.at[index], full.at[index], partner)

    rows = slice(None)
    own = pltpu.make_async_copy(shard.at[:, every], full.at[x, c, z, y, :, every], local)
    own.start()
    line = [sends.start(shard.at[:, every], full.at[x, c, z, y, :, every], k) for k in (1, 2, 3)]
    yield
    own.wait()
    for copy in line:
        copy.wait_recv()
    if at:
        a = send("x", x, c, rows, y, rows, one)
    b = send("y", x, c, rows, y, rows, two)
    core = [send("c", x, c, rows, y, rows, every)]
    yield
    if at:
        a.wait_recv()
        a2 = send("y", rows, c, rows, y, rows, one)
        core.append(send("c", 1 - x, c, rows, y, rows, one))
    b.wait_recv()
    b2 = send("x", x, c, rows, rows, rows, two)
    core.append(send("c", x, c, rows, 1 - y, rows, two))
    yield
    if at:
        a2.wait_recv()
        core.append(send("c", rows, c, rows, 1 - y, rows, one))
    b2.wait_recv()
    core.append(send("c", 1 - x, c, rows, rows, rows, two))
    yield
    for copy in core:
        copy.wait_recv()
    yield


SENDS = 12


def cut(columns):
    return columns // 256 * 128


def run_staggered(plans):
    for turn in range(len(plans) + 4):
        for k in reversed(range(len(plans))):
            if 0 <= turn - k <= 4:
                next(plans[k])


def pieces(widths, parts):
    return [(k, p * (w // n), w // n) for k, (w, n) in enumerate(zip(widths, parts)) for p in range(n)]


def halo_start(edges, halo, sends, local):
    seq, blk = lax.axis_index("seq"), lax.axis_index("blk")
    last = lax.axis_size("blk") - 1
    s, r = sends.send_sem, sends.recv_sem
    at = sends.used
    sends.used += 2
    remote = functools.partial(pltpu.make_async_remote_copy, device_id_type=MESH)
    down = remote(src_ref=edges.at[0], dst_ref=halo.at[1], send_sem=s.at[at], recv_sem=r.at[at],
                  device_id=(seq, lax.max(blk - 1, 0)))
    up = remote(src_ref=edges.at[1], dst_ref=halo.at[0], send_sem=s.at[at + 1], recv_sem=r.at[at + 1],
                device_id=(seq, lax.min(blk + 1, last)))
    fill = [pltpu.make_async_copy(edges.at[k], halo.at[k], local) for k in (0, 1)]

    @pl.when(blk > 0)
    def _():
        down.start()

    @pl.when(blk < last)
    def _():
        up.start()

    @pl.when(blk == 0)
    def _():
        fill[0].start()

    @pl.when(blk == last)
    def _():
        fill[1].start()

    def finish():
        @pl.when(blk > 0)
        def _():
            down.wait_send()
            up.wait_recv()

        @pl.when(blk < last)
        def _():
            up.wait_send()
            down.wait_recv()

        @pl.when(blk == 0)
        def _():
            fill[0].wait()

        @pl.when(blk == last)
        def _():
            fill[1].wait()

    return finish


def meet_all(to):
    seq, blk = lax.axis_index("seq"), lax.axis_index("blk")
    last = lax.axis_size("blk") - 1
    barrier = pltpu.get_barrier_semaphore()
    for device in to.values():
        pl.semaphore_signal(barrier, inc=1, device_id=device, device_id_type=MESH)

    @pl.when(blk > 0)
    def _():
        pl.semaphore_signal(barrier, inc=1, device_id=(seq, lax.max(blk - 1, 0)), device_id_type=MESH)

    @pl.when(blk < last)
    def _():
        pl.semaphore_signal(barrier, inc=1, device_id=(seq, lax.min(blk + 1, last)), device_id_type=MESH)

    ends = jnp.where(blk == 0, 1, 0) + jnp.where(blk == last, 1, 0)
    pl.semaphore_wait(barrier, len(to) + 2 - ends)


def gather_kernel(plan, count, *refs):
    shards, edges, fulls, halo = refs[:count], refs[count], refs[count + 1 : 2 * count + 1], refs[2 * count + 1]
    send_sem, recv_sem, local_sem = refs[2 * count + 2 :]
    to = partners()
    meet_all(to)
    sends = Sends(send_sem, recv_sem, to)
    finish = halo_start(edges, halo, sends, local_sem.at[len(plan)])
    run_staggered([
        gather_plan(shards[k], fulls[k], sends, local_sem.at[i], base, wide) for i, (k, base, wide) in enumerate(plan)
    ])
    finish()
    sends.finish()


def gather_all(shards, parts, edges, collective):
    count = len(shards)
    plan = pieces([v.shape[1] for v in shards], parts)
    anywhere = pl.BlockSpec(memory_space=pl.ANY)
    shapes = [(2, 2, 4, 2) + v.shape for v in shards] + [edges.shape]
    return pl.pallas_call(
        functools.partial(gather_kernel, plan, count),
        in_specs=[anywhere] * (count + 1),
        out_specs=[anywhere] * (count + 1),
        out_shape=[jax.ShapeDtypeStruct(s, jnp.bfloat16) for s in shapes],
        scratch_shapes=[
            pltpu.SemaphoreType.DMA((len(plan) * SENDS + 2,)),
            pltpu.SemaphoreType.DMA((len(plan) * SENDS + 2,)),
            pltpu.SemaphoreType.DMA((len(plan) + 1,)),
        ],
        compiler_params=pltpu.CompilerParams(collective_id=collective, has_side_effects=True),
        name="gather_weights",
    )(*shards, edges)


def widen(value):
    return value.astype(jnp.float32)


def scatter_plan(grad, out, bufs, sends, local, base, wide):
    x, c, z, y = coords()
    at = cut(wide)
    own, got, one1, two1, one2, two2, line, ends = bufs if at else bufs[:2] + (None,) + bufs[2:3] + (None,) + bufs[3:]
    every, one, two = pl.ds(base, wide), pl.ds(0, at), pl.ds(at, wide - at)
    low = jnp.bfloat16
    load = pltpu.make_async_copy(grad.at[:, c, :, :, :, every], own, local)
    load.start()
    cross = sends.start(grad.at[:, 1 - c, :, :, :, every], got, "c")
    yield
    load.wait()
    cross.wait_recv()

    @pl.loop(0, 8)
    def _(i):
        own[i // 4, lax.rem(i, 4)] = (widen(own[i // 4, lax.rem(i, 4)]) + widen(got[i // 4, lax.rem(i, 4)])).astype(low)

    if at:
        a = sends.start(own.at[:, :, 1 - y, :, one], one1, "y")
    b = sends.start(own.at[1 - x, :, :, :, two], two1, "x")
    yield
    if at:
        a.wait_recv()

        @pl.loop(0, 8)
        def _(i):
            one1[i // 4, lax.rem(i, 4)] = (
                widen(own[i // 4, lax.rem(i, 4), y, :, :at]) + widen(one1[i // 4, lax.rem(i, 4)])
            ).astype(low)

        a2 = sends.start(one1.at[1 - x], one2, "x")
    b.wait_recv()

    @pl.loop(0, 4)
    def _(i):
        two1[i] = (widen(own[x, i, :, :, at:]) + widen(two1[i])).astype(low)

    b2 = sends.start(two1.at[:, 1 - y], two2, "y")
    yield
    if at:
        a2.wait_recv()
    b2.wait_recv()

    @pl.loop(0, 4)
    def _(i):
        if at:
            line[i, :, :at] = (widen(one1[x, i]) + widen(one2[i])).astype(low)
        line[i, :, at:] = (widen(two1[i, y]) + widen(two2[i])).astype(low)

    last = [sends.start(line.at[other_z(z, k)], ends.at[k - 1], k) for k in (1, 2, 3)]
    yield
    for copy in last:
        copy.wait_recv()
    out[:, base : base + wide] = widen(line[z]) + widen(ends[0]) + widen(ends[1]) + widen(ends[2])
    yield


def scatter_bufs(rows, wide):
    at = cut(wide)
    shapes = [(2, 4, 2, rows, wide), (2, 4, 2, rows, wide)]
    if at:
        shapes += [(2, 4, rows, at), (4, 2, rows, wide - at), (4, rows, at)]
    else:
        shapes += [(4, 2, rows, wide)]
    shapes += [(4, rows, wide - at), (4, rows, wide), (3, rows, wide)]
    return [pltpu.VMEM(s, jnp.bfloat16) for s in shapes]


def total_plan(values, result, bufs, sends):
    current = values
    for i, partner in enumerate(("c", "x", "y", 1, 2)):
        copy = sends.start(current, bufs.at[2 * i], partner)
        yield
        copy.wait_recv()
        target = result if i == 4 else bufs.at[2 * i + 1]
        target[...] = current[...] + bufs[2 * i]
        current = target
    yield


def scatter_kernel(plan, count, counts, extra, *refs):
    grads, refs = refs[:count], refs[count:]
    if extra:
        edges, values, refs = refs[0], refs[1], refs[2:]
    outs, refs = refs[:count], refs[count:]
    if extra:
        halo, result, refs = refs[0], refs[1], refs[2:]
    send_sem, recv_sem, local_sem = refs[:3]
    bufs = refs[3:]
    to = partners()
    sends = Sends(send_sem, recv_sem, to)
    plans = []
    if extra:
        meet_all(to)
        finish = halo_start(edges, halo, sends, local_sem.at[len(plan)])
        steps = total_plan(values, result, bufs[-1], sends)
    else:
        meet(to)
    for i, (k, base, wide) in enumerate(plan):
        first = sum(counts[:i])
        mine = bufs[first : first + counts[i]]
        plans.append(scatter_plan(grads[k], outs[k], mine, sends, local_sem.at[i], base, wide))
    run_staggered(plans)
    if extra:
        for _ in steps:
            pass
        finish()
    sends.finish()


def scatter_all(grads, parts, collective, extra=()):
    count = len(grads)
    grads = [v.reshape(2, 2, 4, 2, v.shape[0] // 32, v.shape[1]) for v in grads]
    plan = pieces([v.shape[-1] for v in grads], parts)
    bufs = [scatter_bufs(grads[k].shape[-2], wide) for k, base, wide in plan]
    counts = [len(b) for b in bufs]
    bufs = sum(bufs, [])
    anywhere, vmem = pl.BlockSpec(memory_space=pl.ANY), pl.BlockSpec(memory_space=pltpu.VMEM)
    shapes = [jax.ShapeDtypeStruct(v.shape[-2:], jnp.float32) for v in grads]
    in_specs, out_specs = [anywhere] * count, [vmem] * count
    number = len(plan) * SENDS
    if extra:
        in_specs, out_specs = in_specs + [anywhere, vmem], out_specs + [anywhere, vmem]
        shapes += [jax.ShapeDtypeStruct(v.shape, v.dtype) for v in extra]
        bufs.append(pltpu.VMEM((10, 8, 128), jnp.float32))
        number += 7
    return pl.pallas_call(
        functools.partial(scatter_kernel, plan, count, counts, bool(extra)),
        in_specs=in_specs,
        out_specs=out_specs,
        out_shape=shapes,
        scratch_shapes=[
            pltpu.SemaphoreType.DMA((number,)), pltpu.SemaphoreType.DMA((number,)), pltpu.SemaphoreType.DMA((len(plan) + 1,))
        ] + bufs,
        compiler_params=pltpu.CompilerParams(
            collective_id=collective, has_side_effects=True, vmem_limit_bytes=58 << 20
        ),
        name="sum_gradients",
    )(*grads, *extra)


H = 16
MAXLEN = 512
TSTEPS = 5000
AXES = ("seq", "blk")
SMALL = 10


def as_float(value):
    return value.astype(jnp.float32)


def low(value):
    return value.astype(jnp.bfloat16)


def row_dot(left, right):
    return lax.dot_general(left, right, (((0,), (0,)), ((), ())), preferred_element_type=jnp.float32)


def neighbours(low_part, high_part):
    count = lax.axis_size("blk")
    up = [(i, i + 1) for i in range(count - 1)]
    down = [(i + 1, i) for i in range(count - 1)]
    return lax.ppermute(high_part, "blk", up), lax.ppermute(low_part, "blk", down)


def norm_forward(values):
    mean_val = jnp.mean(values, axis=-1, keepdims=True)
    centered = values - mean_val
    inv = lax.rsqrt(jnp.mean(centered * centered, axis=-1, keepdims=True) + 1e-05)
    return centered * inv, inv


def norm_backward(grad, normal, inv, gain):
    scaled = grad * gain
    grad_in = inv * (
        scaled
        - jnp.mean(scaled, axis=-1, keepdims=True)
        - normal * jnp.mean(scaled * normal, axis=-1, keepdims=True)
    )
    return grad_in, jnp.sum(grad * normal, axis=0), jnp.sum(grad, axis=0)


def item_of(ends, places):
    return jnp.sum((ends[None, :] <= places[:, None]).astype(jnp.int32), axis=1)


def per_device(fast, inputs, cotangent, timestep, lengths, padding, *shards):
    (time_weight, time_bias, inproj, query_bias, value_bias, outproj, outproj_bias, first_gain, first_shift,
     upward_w, upward_bias, downward_w, downward_bias, second_gain, second_shift) = shards
    small = (time_weight, time_bias, query_bias, value_bias, outproj_bias, first_gain, first_shift,
             downward_bias, second_gain, second_shift)
    tok, width = inputs.shape
    half = MAXLEN
    ext = tok + 2 * half
    hidden = upward_w.shape[1]

    mark = jnp.zeros((16, width), jnp.bfloat16)
    keep_own = low(padding)
    edge_low = jnp.concatenate([inputs[:half], mark.at[0, :half].set(keep_own[:half])])
    edge_high = jnp.concatenate([inputs[tok - half :], mark.at[0, :half].set(keep_own[tok - half :])])

    if fast:
        rows = time_weight.shape[0]
        cols = [v[:, None] for v in small] + [upward_bias.reshape(-1, rows).T]
        cols = jnp.concatenate(cols, axis=1)
        cols = jnp.pad(cols, ((0, 0), (0, 128 - cols.shape[1])))
        *fulls, halo = gather_all(
            (inproj, cols, outproj, upward_w, downward_w), (1, 1, 1, 2, 2), jnp.stack([edge_low, edge_high]), 0
        )
        inproj_f, small_f, outproj_f, upward_f, downward_f = [v.reshape(-1, v.shape[-1]) for v in fulls]
        small_f = as_float(small_f.T)
        from_low, from_high = halo[0], halo[1]
        upward_bias_f = small_f[SMALL : SMALL + hidden // width]
        upward_bias_f = upward_bias_f.reshape(-1, width // rows, rows).transpose(1, 0, 2).reshape(hidden)
    else:
        from_low, from_high = neighbours(edge_low, edge_high)
        whole = lambda v: lax.all_gather(v, AXES, axis=0, tiled=True)
        inproj_f, outproj_f, upward_f, downward_f = map(whole, (inproj, outproj, upward_w, downward_w))
        small_f = [as_float(whole(v)) for v in small]
        upward_bias_f = as_float(whole(upward_bias))
    (time_weight_f, time_bias_f, query_bias_f, value_bias_f, outproj_bias_f, first_gain_f, first_shift_f,
     downward_bias_f, second_gain_f, second_shift_f) = [small_f[i] for i in range(SMALL)]

    offset = lax.axis_index("blk") * tok
    ends = jnp.cumsum(lengths[0]).astype(jnp.int32)
    places = offset - half + jnp.arange(ext, dtype=jnp.int32)
    item = jnp.where(places >= 0, item_of(ends, places), -1)
    keep = jnp.concatenate([from_low[half, :half], keep_own, from_high[half, :half]])
    query_feat, key_feat, lane = features(item, as_float(keep) > 0.5, tok, lengths.shape[1])
    lo, count = key_range(ends, offset, tok, half)

    time_value = as_float(timestep[0]) / TSTEPS
    shift = time_value * time_weight_f + time_bias_f
    start_of = lambda v: as_float(v) + time_value * time_weight_f + time_bias_f
    start_vec = start_of(inputs)
    start_low = low(start_vec)
    start_ext = jnp.concatenate([low(start_of(from_low[:half])), start_low, low(start_of(from_high[:half]))])
    proj_bias = jnp.concatenate([query_bias_f, jnp.zeros_like(query_bias_f), value_bias_f])
    projected = low(jnp.dot(start_ext, inproj_f, preferred_element_type=jnp.float32) + proj_bias)

    attended, query_feat_own = attn_fwd(projected, query_feat, key_feat, lo, count, lane, tok)
    attn_branch = jnp.dot(attended, outproj_f, preferred_element_type=jnp.float32) + outproj_bias_f
    first_normal, first_inv = norm_forward(start_vec + attn_branch)
    first_out = first_normal * first_gain_f + first_shift_f
    first_low = low(first_out)
    upward = jnp.dot(first_low, upward_f, preferred_element_type=jnp.float32) + upward_bias_f
    phi = 0.5 * (1.0 + lax.erf(upward * 2.0**-0.5))
    hidden_low = low(upward * phi)
    slope = phi + upward * (jnp.exp(-0.5 * upward * upward) * 0.3989422804014327)
    ffn_branch = jnp.dot(hidden_low, downward_f, preferred_element_type=jnp.float32) + downward_bias_f
    second_normal, second_inv = norm_forward(first_out + ffn_branch)
    layer_out = low(second_normal * second_gain_f + second_shift_f)
    sums = jnp.stack([jnp.sum(v * v) for v in (start_vec, attn_branch, ffn_branch)])

    grad_second_in, grad_second_gain, grad_second_shift = norm_backward(
        as_float(cotangent), second_normal, second_inv, second_gain_f
    )
    grad_ffn_low = low(grad_second_in)
    grad_down_weight = row_dot(hidden_low, grad_ffn_low)
    grad_down_bias = jnp.sum(as_float(grad_ffn_low), axis=0)
    grad_up_low = low(nt(grad_ffn_low, downward_f) * slope)
    grad_up_weight = row_dot(first_low, grad_up_low)
    grad_up_bias = jnp.sum(as_float(grad_up_low), axis=0)
    grad_first = grad_second_in + nt(grad_up_low, upward_f)
    grad_first_in, grad_first_gain, grad_first_shift = norm_backward(grad_first, first_normal, first_inv, first_gain_f)
    grad_branch_low = low(grad_first_in)
    grad_out_weight = row_dot(attended, grad_branch_low)
    grad_out_bias = jnp.sum(as_float(grad_branch_low), axis=0)
    grad_attended = low(nt(grad_branch_low, outproj_f))

    head = jnp.arange(width)[:, None] // HD == jnp.arange(H)[None, :]
    delta = jnp.dot(
        as_float(grad_attended) * as_float(attended), as_float(head), precision=lax.Precision.HIGHEST
    )
    stats = jnp.concatenate(
        [query_feat_own[:, lane : lane + 48], delta_features(delta, 0)[:, :48], jnp.zeros((tok, 32), jnp.bfloat16)], axis=1
    )
    packed = jnp.concatenate([grad_attended, stats], axis=1)
    if fast:
        grads = [low(v) for v in (grad_out_weight, grad_up_weight, grad_down_weight)]
        values = jnp.pad(sums[None], ((0, 7), (0, 125)))
        edges = jnp.stack([packed[:half], packed[tok - half :]])
        out_share, up_share, down_share, back, sums = scatter_all(grads, (1, 2, 2), 1, (edges, values))
        back_low, back_high, sums = back[0], back[1], sums[0, :3]
    else:
        back_low, back_high = neighbours(packed[:half], packed[tok - half :])
        sums = lax.psum(sums, AXES)
    branch_rms = jnp.sqrt(sums / (tok * width * lax.axis_size(AXES)))
    packed = jnp.concatenate([back_low, packed, back_high])
    grad_ext = packed[:, :width]
    query_feat = jnp.concatenate([query_feat[:, :lane], packed[:, width : width + 48], query_feat[:, lane + 48 :]], axis=1)
    delta_feat = jnp.pad(packed[:, width + 48 : width + 96], ((0, 0), (lane, 80 - lane)))
    grad_proj = attn_bwd(projected, grad_ext, query_feat, key_feat, delta_feat, stat_lanes(ext, lane), lo, count, lane, tok)

    grad_proj_low = jnp.concatenate([grad_proj[0], grad_proj[1], grad_proj[2]], axis=1)
    grad_in_weight = row_dot(start_low, grad_proj_low)
    grad_query_bias = jnp.sum(as_float(grad_proj[0]), axis=0)
    grad_value_bias = jnp.sum(as_float(grad_proj[2]), axis=0)
    grad_start = grad_first_in + nt(grad_proj_low, inproj_f)
    grad_time_bias = jnp.sum(grad_start, axis=0)
    grad_time_weight = time_value * grad_time_bias
    input_grad = low(grad_start)

    small_grads = (grad_time_weight, grad_time_bias, grad_query_bias, grad_value_bias, grad_out_bias, grad_first_gain,
                   grad_first_shift, grad_down_bias, grad_second_gain, grad_second_shift)
    if fast:
        cols = grad_up_bias.reshape(width // rows, -1, rows).transpose(1, 0, 2).reshape(-1, width)
        cols = jnp.concatenate([jnp.stack(small_grads), cols]).T
        cols = jnp.pad(cols, ((0, 0), (0, 128 - cols.shape[1])))
        in_share, last = scatter_all((low(grad_in_weight), low(cols)), (3, 1), 2)
        small_shares = [last[:, i] for i in range(SMALL)]
        up_bias_share = last[:, SMALL : SMALL + hidden // width].T.reshape(-1)
    else:
        share = lambda v: lax.psum_scatter(v, AXES, scatter_dimension=0, tiled=True)
        down_share, up_share, out_share, in_share, up_bias_share = map(
            share, (grad_down_weight, grad_up_weight, grad_out_weight, grad_in_weight, grad_up_bias)
        )
        small_shares = [share(v) for v in small_grads]
    (time_weight_s, time_bias_s, query_bias_s, value_bias_s, out_bias_s, first_gain_s, first_shift_s,
     down_bias_s, second_gain_s, second_shift_s) = small_shares
    return (layer_out, input_grad, time_weight_s, time_bias_s, in_share, query_bias_s, value_bias_s, out_share,
            out_bias_s, first_gain_s, first_shift_s, up_share, up_bias_share, down_share, down_bias_s,
            second_gain_s, second_shift_s, branch_rms)


def solution(mesh):
    both = P(AXES)
    matrix = P(AXES, None)
    in_specs = (matrix, matrix, P("seq"), P("seq", None), both,
                both, both, matrix, both, both, matrix, both, both, both, matrix, both, matrix, both, both, both)
    out_specs = (matrix, matrix, both, both, matrix, both, both, matrix, both, both, both, matrix, both, matrix,
                 both, both, both, P())
    fast = dict(mesh.shape) == {"seq": 4, "blk": 8}
    return jax.shard_map(
        functools.partial(per_device, fast), mesh=mesh, in_specs=in_specs, out_specs=out_specs, check_vma=False
    )
```

```python
import functools

import jax
import jax.numpy as jnp
from jax import lax
from jax.experimental import pallas as pl
from jax.experimental.pallas import tpu as pltpu
from jax.sharding import PartitionSpec as P

HD = 64
TQ = 256
PAIR = 2 * HD
NEG = -(2.0**100)


def nt(a, b):
    return lax.dot_general(a, b, (((1,), (1,)), ((), ())), preferred_element_type=jnp.float32)


def nn(a, b):
    return jnp.dot(a, b, preferred_element_type=jnp.float32)


def schedule(step, steps, job, length):
    at = [i * steps // length for i in range(length)]
    for s in range(steps):
        count = at.count(s)
        if count or s == steps - 1:

            @pl.when(step == s)
            def _():
                for _ in range(count):
                    next(job)


def fwd_kernel(plan, count, tok, lanes, *refs):
    shards, refs = refs[:count], refs[count:]
    start_ref, wq, wk, wv, bias_ref, qf_ref, kf_ref, refs = *refs[:7], refs[7:]
    fulls, refs = refs[:count], refs[count:]
    proj_ref, o_ref, f_ref, ka, va, qa = refs[:6]
    step = pl.program_id(0)
    ext = start_ref.shape[0]
    half = (ext - tok) // 2
    window = 2 * half + TQ
    if count:
        send_sem, recv_sem, local_sem = refs[6:]
        pos = Place()

        @pl.when(step == 0)
        def _():
            meet(pos, False)

        sends = Sends(send_sem, recv_sem, pos.to)
        schedule(step, FWD_STEPS, gather_job(pos, plan, shards, fulls, sends, local_sem), len(plan) + 4)

    @pl.when(step == 0)
    def _():
        ka[:, PAIR:] = kf_ref[...]
        va[:, PAIR:] = jnp.ones((ext, PAIR), jnp.bfloat16)
        f_ref[...] = qf_ref[half : half + tok, :]

    lane = lax.broadcasted_iota(jnp.int32, (TQ, PAIR), 1)
    left = lane < HD
    for t in range(ext // TQ):
        rows = slice(t * TQ, (t + 1) * TQ)
        start = start_ref[rows, :]
        q = (nn(start, wq[...]) + bias_ref[0:1, :]).astype(jnp.bfloat16)
        k = (nn(start, wk[...]) + bias_ref[1:2, :]).astype(jnp.bfloat16)
        v = (nn(start, wv[...]) + bias_ref[2:3, :]).astype(jnp.bfloat16)
        proj_ref[0, rows, :] = q
        proj_ref[1, rows, :] = k
        proj_ref[2, rows, :] = v
        ka[rows, :PAIR] = k
        va[rows, :PAIR] = v
        if half <= t * TQ < half + tok:
            own = t - half // TQ
            q = q * jnp.bfloat16(HD**-0.5)
            zero = jnp.zeros_like(q)
            qa[2 * own, :, :PAIR] = jnp.where(left, q, zero)
            qa[2 * own + 1, :, :PAIR] = jnp.where(left, zero, q)
            qa[2 * own, :, PAIR:] = qf_ref[rows, :]
            qa[2 * own + 1, :, PAIR:] = qf_ref[rows, :]
    for t in range(tok // TQ):
        win = slice(t * TQ, t * TQ + window)
        own = slice(t * TQ, (t + 1) * TQ)
        feat = f_ref[own, :]
        out = []
        for side in range(2):
            s = nt(qa[2 * t + side], ka[win, :])
            top = jnp.max(s, axis=1, keepdims=True)
            r = nn(jnp.exp(s - top).astype(jnp.bfloat16), va[win, :])
            total = r[:, PAIR:]
            out.append(r[:, :PAIR] / total)
            rest = top + jnp.log(total)
            for part in range(3):
                piece = rest.astype(jnp.bfloat16)
                rest = rest - piece.astype(jnp.float32)
                feat = jnp.where(lane == lanes + part * 16 + 2 * step + side, piece, feat)
        o_ref[own, :] = jnp.where(left, out[0], out[1]).astype(jnp.bfloat16)
        f_ref[own, :] = feat


FWD_STEPS = 8


def attn_fwd(start, inproj, bias, qf, kf, lanes, tok, shards=(), parts=(), share=0.0, collective=None):
    ext, width = start.shape
    pairs = width // PAIR
    count = len(shards)
    plan = pieces([v.shape[1] for v in shards], parts, share)
    anywhere = pl.BlockSpec(memory_space=pl.ANY)
    col = lambda base: pl.BlockSpec((width, PAIR), lambda i: (0, base + i))
    fix = pl.BlockSpec((ext, PAIR), lambda i: (0, 0))
    comm = dict(collective_id=collective, has_side_effects=True) if count else {}
    return pl.pallas_call(
        functools.partial(fwd_kernel, plan, count, tok, lanes),
        grid=(pairs,),
        in_specs=[anywhere] * count
        + [pl.BlockSpec((ext, width), lambda i: (0, 0)), col(0), col(pairs), col(2 * pairs),
           pl.BlockSpec((8, PAIR), lambda i: (0, i)), fix, fix],
        out_specs=[anywhere] * count
        + [pl.BlockSpec((3, ext, PAIR), lambda i: (0, 0, i)), pl.BlockSpec((tok, PAIR), lambda i: (0, i)),
           pl.BlockSpec((tok, PAIR), lambda i: (0, 0))],
        out_shape=full_shapes(shards)
        + [jax.ShapeDtypeStruct((3, ext, width), jnp.bfloat16), jax.ShapeDtypeStruct((tok, width), jnp.bfloat16),
           jax.ShapeDtypeStruct((tok, PAIR), jnp.bfloat16)],
        scratch_shapes=[
            pltpu.VMEM((ext, 2 * PAIR), jnp.bfloat16),
            pltpu.VMEM((ext, 2 * PAIR), jnp.bfloat16),
            pltpu.VMEM((2 * tok // TQ, TQ, 2 * PAIR), jnp.bfloat16),
        ] + (semaphores(len(plan) * SENDS, len(plan)) if count else []),
        compiler_params=pltpu.CompilerParams(
            vmem_limit_bytes=56 << 20, dimension_semantics=("arbitrary",), **comm
        ),
        name="attention",
    )(*shards, start, inproj, inproj, inproj, bias, qf, kf)


def bwd_kernel(plan, count, counts, tok, lanes, *refs):
    grads, refs = refs[:count], refs[count:]
    edges, values, refs = refs[0], refs[1], refs[2:]
    q_ref, k_ref, v_ref, d_ref, qf_ref, own_ref, kf_ref, vf_ref, refs = *refs[:8], refs[8:]
    outs, refs = refs[:count], refs[count:]
    result, gq_ref, gkv_ref, refs = *refs[:3], refs[3:]
    one, two, feats, halo, refs = *refs[:4], refs[4:]
    step = pl.program_id(0)
    ext = k_ref.shape[1]
    half = (ext - tok) // 2
    window = 2 * half + TQ
    pairs = BWD_STEPS // 2
    pair = lax.rem(step, pairs)
    if count:
        send_sem, recv_sem, local_sem, sums, refs = *refs[:4], refs[4:]
        pos = Place()

        @pl.when(step == 0)
        def _():
            meet(pos, True)

        sends = Sends(send_sem, recv_sem, pos.to)

        def work():
            neighbour = halo_plan(pos, edges, halo, sends, local_sem, len(plan))
            total = total_plan(values, result, sums, sends)
            next(neighbour)
            for i, _ in enumerate(scatter_job(pos, plan, counts, grads, outs, refs, sends, local_sem)):
                if i < 6:
                    next(total)
                if i == HALO_TURN:
                    next(neighbour)
                yield

        schedule(step, BWD_STEPS, work(), len(plan) + 4)
    else:

        @pl.when(step == 0)
        def _():
            halo[...] = edges[...]
            result[...] = values[...]

    lane = lax.broadcasted_iota(jnp.int32, (TQ, PAIR), 1)
    left = lane < HD

    @pl.when(step == 0)
    def _():
        one[2, :, PAIR:] = kf_ref[...]
        two[2, :, PAIR:] = vf_ref[...]
        feats[half : half + tok, :] = own_ref[...]

    @pl.when(step == pairs)
    def _():
        for t in range(half // TQ):
            for side, base in ((0, 0), (1, half + tok)):
                rows = slice(base + t * TQ, base + (t + 1) * TQ)
                got = halo[side, t * TQ : (t + 1) * TQ, PAIR * pairs :]
                feats[rows, :] = jnp.where(lane < lanes, qf_ref[rows, :], got)

    def sides(tile, rows, d):
        q = q_ref[0, rows, :] * jnp.bfloat16(HD**-0.5)
        feat = feats[rows, :]
        zero = jnp.zeros_like(q)
        for side in range(2):
            mine = left if side == 0 else ~left
            kept = jnp.where((lane < lanes) | (lax.rem(lane - lanes + 128, 16) == 2 * pair + side), feat, zero)
            one[side, rows, :PAIR] = jnp.where(mine, q, zero)
            one[side, rows, PAIR:] = kept
            two[side, rows, :PAIR] = jnp.where(mine, d, zero)
            two[side, rows, PAIR:] = kept

    one[2, :, :PAIR] = k_ref[0]
    two[2, :, :PAIR] = v_ref[0]
    for t in range(tok // TQ):
        sides(t, slice(half + t * TQ, half + (t + 1) * TQ), d_ref[t * TQ : (t + 1) * TQ, :])

    @pl.when(step < pairs)
    def _():
        for t in range(tok // TQ):
            win = slice(t * TQ, t * TQ + window)
            rows = slice(half + t * TQ, half + (t + 1) * TQ)
            parts = []
            for side in range(2):
                p = jnp.exp(nt(one[side, rows, :], one[2, win, :]))
                g = (p * nt(two[side, rows, :], two[2, win, :])).astype(jnp.bfloat16)
                parts.append(nn(g, k_ref[0, win, :]))
            gq_ref[t * TQ : (t + 1) * TQ, :] = (jnp.where(left, *parts) * HD**-0.5).astype(jnp.bfloat16)

    @pl.when(step >= pairs)
    def _():
        at = pl.ds(pl.multiple_of(pair * PAIR, PAIR), PAIR)
        for t in range(half // TQ):
            for side, base in ((0, 0), (1, half + tok)):
                sides(t, slice(base + t * TQ, base + (t + 1) * TQ), halo[side, t * TQ : (t + 1) * TQ, at])
        for t in range(tok // TQ):
            win = slice(t * TQ, t * TQ + window)
            rows = slice(half + t * TQ, half + (t + 1) * TQ)
            dk, dv = 0.0, 0.0
            for side in range(2):
                p = jnp.exp(nt(one[2, rows, :], one[side, win, :]))
                g = (p * nt(two[2, rows, :], two[side, win, :])).astype(jnp.bfloat16)
                dk = dk + nn(g, one[side, win, :PAIR])
                dv = dv + nn(p.astype(jnp.bfloat16), two[side, win, :PAIR])
            gkv_ref[0, t * TQ : (t + 1) * TQ, :] = dk.astype(jnp.bfloat16)
            gkv_ref[1, t * TQ : (t + 1) * TQ, :] = dv.astype(jnp.bfloat16)


BWD_STEPS = 16
HALO_TURN = 3


def attn_bwd(proj, grad, qf, own_feat, kf, vf, lanes, tok, edges, values, grads=(), parts=(), share=0.0, collective=None):
    _, ext, width = proj.shape
    pairs = width // PAIR
    half = (ext - tok) // 2
    grads, plan, counts, bufs, shapes = scatter_layout(grads, parts, share)
    count = len(grads)
    anywhere, vmem = pl.BlockSpec(memory_space=pl.ANY), pl.BlockSpec(memory_space=pltpu.VMEM)
    third = lambda k: pl.BlockSpec((1, ext, PAIR), lambda i: (k, 0, lax.rem(i, pairs)))
    fix = lambda rows: pl.BlockSpec((rows, PAIR), lambda i: (0, 0))
    comm = dict(collective_id=collective, has_side_effects=True) if count else {}
    scratch = [
        pltpu.VMEM((3, ext, 2 * PAIR), jnp.bfloat16),
        pltpu.VMEM((3, ext, 2 * PAIR), jnp.bfloat16),
        pltpu.VMEM((ext, PAIR), jnp.bfloat16),
        pltpu.VMEM((2, half, width + PAIR), jnp.bfloat16),
    ]
    if count:
        scratch += semaphores(len(plan) * SENDS + 7, len(plan) + 1) + [pltpu.VMEM((10, 8, 128), jnp.float32)] + bufs
    return pl.pallas_call(
        functools.partial(bwd_kernel, plan, count, counts, tok, lanes),
        grid=(2 * pairs,),
        in_specs=[anywhere] * count
        + [anywhere if count else vmem, vmem, third(0), third(1), third(2),
           pl.BlockSpec((tok, PAIR), lambda i: (0, lax.rem(i, pairs))), fix(ext), fix(tok), fix(ext), fix(ext)],
        out_specs=[vmem] * count
        + [vmem, pl.BlockSpec((tok, PAIR), lambda i: (0, lax.min(i, pairs - 1))),
           pl.BlockSpec((2, tok, PAIR), lambda i: (0, 0, lax.max(i - pairs, 0)))],
        out_shape=shapes
        + [jax.ShapeDtypeStruct(values.shape, jnp.float32), jax.ShapeDtypeStruct((tok, width), jnp.bfloat16),
           jax.ShapeDtypeStruct((2, tok, width), jnp.bfloat16)],
        scratch_shapes=scratch,
        compiler_params=pltpu.CompilerParams(
            vmem_limit_bytes=62 << 20, dimension_semantics=("arbitrary",), **comm
        ),
        name="attention_gradients",
    )(*grads, edges, values, proj, proj, proj, grad, qf, own_feat, kf, vf)


def bits(values, count):
    planes = (values[:, None] >> jnp.arange(count, dtype=jnp.int32)[None, :]) & 1
    return planes.astype(jnp.float32)


def features(item, places, keep, n_items):
    ext = item.shape[0]
    nb = (n_items + 1).bit_length()
    pb = (ext - 1).bit_length()
    lanes = 2 * (nb + pb)
    assert lanes + 80 <= PAIR and ext == 1 << pb
    ib = bits(item + 1, nb)
    ps = bits(places, pb)
    kept = keep.astype(jnp.float32)[:, None]
    lost = 1 - kept
    qf = jnp.concatenate([ib, 1 - ib, ps, 1 - ps, jnp.zeros((ext, PAIR - lanes))], axis=1)
    kf = jnp.concatenate([NEG * kept * (1 - ib), NEG * kept * ib, NEG * lost * (1 - ps), NEG * lost * ps,
                          -jnp.ones((ext, 48)), jnp.zeros((ext, PAIR - 48 - lanes))], axis=1)
    return qf.astype(jnp.bfloat16), kf.astype(jnp.bfloat16), lanes


def delta_key(ext, lanes):
    lane = jnp.arange(PAIR)
    vf = jnp.where((lane >= lanes + 48) & (lane < lanes + 80), -1.0, 0.0)
    return jnp.broadcast_to(vf[None], (ext, PAIR)).astype(jnp.bfloat16)


def delta_lanes(delta, lanes):
    first = delta.astype(jnp.bfloat16)
    second = (delta - first.astype(jnp.float32)).astype(jnp.bfloat16)
    return jnp.pad(jnp.concatenate([first, second], axis=1), ((0, 0), (lanes + 48, PAIR - 80 - lanes)))


MESH = pl.DeviceIdType.MESH


class Place:
    def __init__(self):
        seq, blk = lax.axis_index("seq"), lax.axis_index("blk")
        self.seq, self.blk, self.last = seq, blk, lax.axis_size("blk") - 1
        self.x, self.c, self.z, self.y = x, c, z, y = seq // 2, lax.rem(seq, 2), blk // 2, lax.rem(blk, 2)
        self.nx, self.nc, self.ny = nx, nc, ny = 1 - x, 1 - c, 1 - y
        low_bit, high_bit = lax.rem(z, 2), z // 2
        flips = {1: (1 - low_bit, high_bit), 2: (low_bit, 1 - high_bit), 3: (1 - low_bit, 1 - high_bit)}
        self.nz = {k: high * 2 + bit for k, (bit, high) in flips.items()}
        device = lambda x, c, z, y: (x * 2 + c, z * 2 + y)
        self.to = {"x": device(nx, c, z, y), "y": device(x, c, z, ny), "c": device(x, nc, z, y)}
        for k in (1, 2, 3):
            self.to[k] = device(x, c, self.nz[k], y)
        self.below = (seq, lax.max(blk - 1, 0))
        self.above = (seq, lax.min(blk + 1, self.last))


class Copy:
    def __init__(self, make):
        self.make = make

    def start(self):
        self.make().start()
        return self

    def wait(self):
        self.make().wait()

    def wait_send(self):
        self.make().wait_send()

    def wait_recv(self):
        self.make().wait_recv()


def local_copy(src, dst, sems, at):
    return Copy(lambda: pltpu.make_async_copy(src(), dst(), sems.at[at])).start()


class Sends:
    def __init__(self, send_sem, recv_sem, to):
        self.send_sem, self.recv_sem, self.to, self.used, self.live = send_sem, recv_sem, to, 0, []

    def describe(self, src, dst, device):
        at = self.used
        self.used += 1
        return Copy(
            lambda: pltpu.make_async_remote_copy(
                src_ref=src(), dst_ref=dst(), send_sem=self.send_sem.at[at], recv_sem=self.recv_sem.at[at],
                device_id=device, device_id_type=MESH,
            )
        )

    def start(self, src, dst, partner):
        copy = self.describe(src, dst, self.to[partner]).start()
        self.live.append(copy)
        return copy

    def finish(self):
        for copy in self.live:
            copy.wait_send()


def gather_plan(pos, shard, full, sends, local, number, base, wide, at):
    x, c, z, y, nx, nc, ny = pos.x, pos.c, pos.z, pos.y, pos.nx, pos.nc, pos.ny
    every, one, two = pl.ds(base, wide), pl.ds(base, at), pl.ds(base + at, wide - at)

    def send(partner, *index):
        return sends.start(lambda: full.at[index], lambda: full.at[index], partner)

    rows = slice(None)
    source, target = lambda: shard.at[:, every], lambda: full.at[x, c, z, y, :, every]
    own = local_copy(source, target, local, number)
    line = [sends.start(source, target, k) for k in (1, 2, 3)]
    yield
    own.wait()
    for copy in line:
        copy.wait_recv()
    if at:
        a = send("x", x, c, rows, y, rows, one)
    b = send("y", x, c, rows, y, rows, two)
    core = [send("c", x, c, rows, y, rows, every)]
    yield
    if at:
        a.wait_recv()
        a2 = send("y", rows, c, rows, y, rows, one)
        core.append(send("c", nx, c, rows, y, rows, one))
    b.wait_recv()
    b2 = send("x", x, c, rows, rows, rows, two)
    core.append(send("c", x, c, rows, ny, rows, two))
    yield
    if at:
        a2.wait_recv()
        core.append(send("c", rows, c, rows, ny, rows, one))
    b2.wait_recv()
    core.append(send("c", nx, c, rows, rows, rows, two))
    yield
    for copy in core:
        copy.wait_recv()
    yield


SENDS = 12


def turns(plans, last):
    for turn in range(len(plans) + 4):
        for k in reversed(range(len(plans))):
            if 0 <= turn - k <= 4:
                next(plans[k])
        if turn == len(plans) + 3:
            last()
        yield


def pieces(widths, parts, share):
    plan = []
    for k, (whole, count) in enumerate(zip(widths, parts)):
        wide = whole // count
        plan += [(k, p * wide, wide, int(wide * share) // 128 * 128) for p in range(count)]
    return plan


def halo_plan(pos, edges, halo, sends, local, number):
    blk, last = pos.blk, pos.last
    down = sends.describe(lambda: edges.at[0], lambda: halo.at[1], pos.below)
    up = sends.describe(lambda: edges.at[1], lambda: halo.at[0], pos.above)
    fill = [
        Copy(lambda k=k: pltpu.make_async_copy(edges.at[k], halo.at[k], local.at[number])) for k in (0, 1)
    ]

    def where(test, *acts):
        @pl.when(test)
        def _():
            for act in acts:
                act()

    where(blk > 0, down.start)
    where(blk < last, up.start)
    where(blk == 0, fill[0].start)
    where(blk == last, fill[1].start)
    yield
    where(blk > 0, down.wait_send, up.wait_recv)
    where(blk < last, up.wait_send, down.wait_recv)
    where(blk == 0, fill[0].wait)
    where(blk == last, fill[1].wait)
    yield


def meet(pos, halo):
    barrier = pltpu.get_barrier_semaphore()
    for device in pos.to.values():
        pl.semaphore_signal(barrier, inc=1, device_id=device, device_id_type=MESH)
    count = len(pos.to)
    if halo:

        @pl.when(pos.blk > 0)
        def _():
            pl.semaphore_signal(barrier, inc=1, device_id=pos.below, device_id_type=MESH)

        @pl.when(pos.blk < pos.last)
        def _():
            pl.semaphore_signal(barrier, inc=1, device_id=pos.above, device_id_type=MESH)

        count = count + 2 - jnp.where(pos.blk == 0, 1, 0) - jnp.where(pos.blk == pos.last, 1, 0)
    pl.semaphore_wait(barrier, count)


def gather_job(pos, plan, shards, fulls, sends, local):
    yield from turns([
        gather_plan(pos, shards[k], fulls[k], sends, local, i, base, wide, at) for i, (k, base, wide, at) in enumerate(plan)
    ], sends.finish)


def gather_kernel(plan, count, *refs):
    shards, edges, fulls, halo = refs[:count], refs[count], refs[count + 1 : 2 * count + 1], refs[2 * count + 1]
    send_sem, recv_sem, local_sem = refs[2 * count + 2 :]
    pos = Place()
    meet(pos, True)
    sends = Sends(send_sem, recv_sem, pos.to)
    neighbour = halo_plan(pos, edges, halo, sends, local_sem, len(plan))
    next(neighbour)
    for _ in gather_job(pos, plan, shards, fulls, sends, local_sem):
        pass
    next(neighbour)


def semaphores(number, local):
    return [pltpu.SemaphoreType.DMA((number,)), pltpu.SemaphoreType.DMA((number,)), pltpu.SemaphoreType.DMA((local,))]


def full_shapes(shards):
    return [jax.ShapeDtypeStruct((2, 2, 4, 2) + v.shape, jnp.bfloat16) for v in shards]


def gather_all(shards, parts, share, edges, collective):
    count = len(shards)
    plan = pieces([v.shape[1] for v in shards], parts, share)
    anywhere = pl.BlockSpec(memory_space=pl.ANY)
    return pl.pallas_call(
        functools.partial(gather_kernel, plan, count),
        in_specs=[anywhere] * (count + 1),
        out_specs=[anywhere] * (count + 1),
        out_shape=full_shapes(shards) + [jax.ShapeDtypeStruct(edges.shape, edges.dtype)],
        scratch_shapes=semaphores(len(plan) * SENDS + 2, len(plan) + 1),
        compiler_params=pltpu.CompilerParams(collective_id=collective, has_side_effects=True),
        name="gather_weights",
    )(*shards, edges)


def widen(value):
    return value.astype(jnp.float32)


def scatter_plan(pos, grad, out, bufs, sends, local, number, base, wide, at):
    x, c, z, y, nx, nc, ny = pos.x, pos.c, pos.z, pos.y, pos.nx, pos.nc, pos.ny
    own, got, one1, two1, one2, two2, line, ends = bufs if at else bufs[:2] + (None,) + bufs[2:3] + (None,) + bufs[3:]
    every, one, two = pl.ds(base, wide), pl.ds(0, at), pl.ds(at, wide - at)
    low = jnp.bfloat16
    load = local_copy(lambda: grad.at[:, c, :, :, :, every], lambda: own, local, number)
    cross = sends.start(lambda: grad.at[:, nc, :, :, :, every], lambda: got, "c")
    yield
    load.wait()
    cross.wait_recv()

    @pl.loop(0, 8)
    def _(i):
        own[i // 4, lax.rem(i, 4)] = (widen(own[i // 4, lax.rem(i, 4)]) + widen(got[i // 4, lax.rem(i, 4)])).astype(low)

    if at:
        a = sends.start(lambda: own.at[:, :, ny, :, one], lambda: one1, "y")
    b = sends.start(lambda: own.at[nx, :, :, :, two], lambda: two1, "x")
    yield
    if at:
        a.wait_recv()

        @pl.loop(0, 8)
        def _(i):
            one1[i // 4, lax.rem(i, 4)] = (
                widen(own[i // 4, lax.rem(i, 4), y, :, :at]) + widen(one1[i // 4, lax.rem(i, 4)])
            ).astype(low)

        a2 = sends.start(lambda: one1.at[nx], lambda: one2, "x")
    b.wait_recv()

    @pl.loop(0, 4)
    def _(i):
        two1[i] = (widen(own[x, i, :, :, at:]) + widen(two1[i])).astype(low)

    b2 = sends.start(lambda: two1.at[:, ny], lambda: two2, "y")
    yield
    if at:
        a2.wait_recv()
    b2.wait_recv()

    @pl.loop(0, 4)
    def _(i):
        if at:
            line[i, :, :at] = (widen(one1[x, i]) + widen(one2[i])).astype(low)
        line[i, :, at:] = (widen(two1[i, y]) + widen(two2[i])).astype(low)

    last = [
        sends.start(lambda k=k: line.at[pos.nz[k]], lambda k=k: ends.at[k - 1], k) for k in (1, 2, 3)
    ]
    yield
    for copy in last:
        copy.wait_recv()
    out[:, base : base + wide] = widen(line[z]) + widen(ends[0]) + widen(ends[1]) + widen(ends[2])
    yield


def scatter_bufs(rows, wide, at):
    shapes = [(2, 4, 2, rows, wide), (2, 4, 2, rows, wide)]
    if at:
        shapes += [(2, 4, rows, at), (4, 2, rows, wide - at), (4, rows, at)]
    else:
        shapes += [(4, 2, rows, wide)]
    shapes += [(4, rows, wide - at), (4, rows, wide), (3, rows, wide)]
    return [pltpu.VMEM(s, jnp.bfloat16) for s in shapes]


def total_plan(values, result, bufs, sends):
    partners = ("c", "x", "y", 1, 2)
    for i, partner in enumerate(partners):
        source = (lambda i=i: bufs.at[2 * i - 1]) if i else (lambda: values)
        copy = sends.start(source, lambda i=i: bufs.at[2 * i], partner)
        yield
        copy.wait_recv()
        total = source()[...] + bufs[2 * i]
        if i + 1 < len(partners):
            bufs[2 * i + 1] = total
        else:
            result[...] = total
    yield


def scatter_job(pos, plan, counts, grads, outs, bufs, sends, local):
    plans = []
    for i, (k, base, wide, at) in enumerate(plan):
        first = sum(counts[:i])
        mine = bufs[first : first + counts[i]]
        plans.append(scatter_plan(pos, grads[k], outs[k], mine, sends, local, i, base, wide, at))
    yield from turns(plans, sends.finish)


def scatter_layout(grads, parts, share):
    grads = [v.reshape(2, 2, 4, 2, v.shape[0] // 32, v.shape[1]) for v in grads]
    plan = pieces([v.shape[-1] for v in grads], parts, share)
    bufs = [scatter_bufs(grads[k].shape[-2], wide, at) for k, base, wide, at in plan]
    shapes = [jax.ShapeDtypeStruct(v.shape[-2:], jnp.float32) for v in grads]
    return grads, plan, [len(b) for b in bufs], sum(bufs, []), shapes


def scatter_kernel(plan, count, counts, *refs):
    grads, outs, refs = refs[:count], refs[count : 2 * count], refs[2 * count :]
    send_sem, recv_sem, local_sem = refs[:3]
    pos = Place()
    meet(pos, False)
    sends = Sends(send_sem, recv_sem, pos.to)
    for _ in scatter_job(pos, plan, counts, grads, outs, refs[3:], sends, local_sem):
        pass


def scatter_all(grads, parts, share, collective):
    count = len(grads)
    grads, plan, counts, bufs, shapes = scatter_layout(grads, parts, share)
    anywhere, vmem = pl.BlockSpec(memory_space=pl.ANY), pl.BlockSpec(memory_space=pltpu.VMEM)
    return pl.pallas_call(
        functools.partial(scatter_kernel, plan, count, counts),
        in_specs=[anywhere] * count,
        out_specs=[vmem] * count,
        out_shape=shapes,
        scratch_shapes=semaphores(len(plan) * SENDS, len(plan)) + bufs,
        compiler_params=pltpu.CompilerParams(
            collective_id=collective, has_side_effects=True, vmem_limit_bytes=58 << 20
        ),
        name="sum_gradients",
    )(*grads)


H = 16
MAXLEN = 512
TSTEPS = 5000
AXES = ("seq", "blk")
SMALL = 10


def as_float(value):
    return value.astype(jnp.float32)


def low(value):
    return value.astype(jnp.bfloat16)


def row_dot(left, right):
    return lax.dot_general(left, right, (((0,), (0,)), ((), ())), preferred_element_type=jnp.float32)


def neighbours(low_part, high_part):
    count = lax.axis_size("blk")
    up = [(i, i + 1) for i in range(count - 1)]
    down = [(i + 1, i) for i in range(count - 1)]
    return lax.ppermute(high_part, "blk", up), lax.ppermute(low_part, "blk", down)


def norm_forward(values):
    mean_val = jnp.mean(values, axis=-1, keepdims=True)
    centered = values - mean_val
    inv = lax.rsqrt(jnp.mean(centered * centered, axis=-1, keepdims=True) + 1e-05)
    return centered * inv, inv


def norm_backward(grad, normal, inv, gain):
    scaled = grad * gain
    grad_in = inv * (
        scaled
        - jnp.mean(scaled, axis=-1, keepdims=True)
        - normal * jnp.mean(scaled * normal, axis=-1, keepdims=True)
    )
    return grad_in, jnp.sum(grad * normal, axis=0), jnp.sum(grad, axis=0)


def item_of(ends, places):
    return jnp.sum((ends[None, :] <= places[:, None]).astype(jnp.int32), axis=1)


def per_device(fast, inputs, cotangent, timestep, lengths, padding, *shards):
    (time_weight, time_bias, inproj, query_bias, value_bias, outproj, outproj_bias, first_gain, first_shift,
     upward_w, upward_bias, downward_w, downward_bias, second_gain, second_shift) = shards
    small = (time_weight, time_bias, query_bias, value_bias, outproj_bias, first_gain, first_shift,
             downward_bias, second_gain, second_shift)
    tok, width = inputs.shape
    half = MAXLEN
    ext = tok + 2 * half
    hidden = upward_w.shape[1]

    mark = jnp.zeros((16, width), jnp.bfloat16)
    keep_own = low(padding)
    edge_low = jnp.concatenate([inputs[:half], mark.at[0, :half].set(keep_own[:half])])
    edge_high = jnp.concatenate([inputs[tok - half :], mark.at[0, :half].set(keep_own[tok - half :])])

    if fast:
        rows = time_weight.shape[0]
        cols = [v[:, None] for v in small] + [upward_bias.reshape(-1, rows).T]
        cols = jnp.concatenate(cols, axis=1)
        cols = jnp.pad(cols, ((0, 0), (0, 128 - cols.shape[1])))
        *fulls, halo = gather_all(
            (inproj, cols), (1, 1), 0.0, jnp.stack([edge_low, edge_high]), 0
        )
        inproj_f, small_f = [v.reshape(-1, v.shape[-1]) for v in fulls]
        small_f = as_float(small_f.T)
        from_low, from_high = halo[0], halo[1]
        upward_bias_f = small_f[SMALL : SMALL + hidden // width]
        upward_bias_f = upward_bias_f.reshape(-1, width // rows, rows).transpose(1, 0, 2).reshape(hidden)
    else:
        from_low, from_high = neighbours(edge_low, edge_high)
        whole = lambda v: lax.all_gather(v, AXES, axis=0, tiled=True)
        inproj_f, outproj_f, upward_f, downward_f = map(whole, (inproj, outproj, upward_w, downward_w))
        small_f = [as_float(whole(v)) for v in small]
        upward_bias_f = as_float(whole(upward_bias))
    (time_weight_f, time_bias_f, query_bias_f, value_bias_f, outproj_bias_f, first_gain_f, first_shift_f,
     downward_bias_f, second_gain_f, second_shift_f) = [small_f[i] for i in range(SMALL)]

    offset = lax.axis_index("blk") * tok
    ends = jnp.cumsum(lengths[0]).astype(jnp.int32)
    places = offset - half + jnp.arange(ext, dtype=jnp.int32)
    item = jnp.where(places >= 0, item_of(ends, places), -1)
    keep = jnp.concatenate([from_low[half, :half], keep_own, from_high[half, :half]])
    query_feat, key_feat, lane = features(item, places, as_float(keep) > 0.5, lengths.shape[1])

    time_value = as_float(timestep[0]) / TSTEPS
    shift = time_value * time_weight_f + time_bias_f
    start_of = lambda v: as_float(v) + time_value * time_weight_f + time_bias_f
    start_vec = start_of(inputs)
    start_low = low(start_vec)
    start_ext = jnp.concatenate([low(start_of(from_low[:half])), start_low, low(start_of(from_high[:half]))])
    bias = jnp.pad(jnp.stack([query_bias_f, jnp.zeros_like(query_bias_f), value_bias_f]), ((0, 5), (0, 0)))
    if fast:
        *fulls, projected, attended, feat_own = attn_fwd(
            start_ext, inproj_f, bias, query_feat, key_feat, lane, tok, (outproj, upward_w, downward_w), (1, 2, 2), 0.5, 1
        )
        outproj_f, upward_f, downward_f = [v.reshape(-1, v.shape[-1]) for v in fulls]
    else:
        projected, attended, feat_own = attn_fwd(start_ext, inproj_f, bias, query_feat, key_feat, lane, tok)
    attn_branch = jnp.dot(attended, outproj_f, preferred_element_type=jnp.float32) + outproj_bias_f
    first_normal, first_inv = norm_forward(start_vec + attn_branch)
    first_out = first_normal * first_gain_f + first_shift_f
    first_low = low(first_out)
    upward = jnp.dot(first_low, upward_f, preferred_element_type=jnp.float32) + upward_bias_f
    phi = 0.5 * (1.0 + lax.erf(upward * 2.0**-0.5))
    hidden_low = low(upward * phi)
    slope = phi + upward * (jnp.exp(-0.5 * upward * upward) * 0.3989422804014327)
    ffn_branch = jnp.dot(hidden_low, downward_f, preferred_element_type=jnp.float32) + downward_bias_f
    second_normal, second_inv = norm_forward(first_out + ffn_branch)
    layer_out = low(second_normal * second_gain_f + second_shift_f)
    sums = jnp.stack([jnp.sum(v * v) for v in (start_vec, attn_branch, ffn_branch)])

    grad_second_in, grad_second_gain, grad_second_shift = norm_backward(
        as_float(cotangent), second_normal, second_inv, second_gain_f
    )
    grad_ffn_low = low(grad_second_in)
    grad_down_weight = row_dot(hidden_low, grad_ffn_low)
    grad_down_bias = jnp.sum(as_float(grad_ffn_low), axis=0)
    grad_up_low = low(nt(grad_ffn_low, downward_f) * slope)
    grad_up_weight = row_dot(first_low, grad_up_low)
    grad_up_bias = jnp.sum(as_float(grad_up_low), axis=0)
    grad_first = grad_second_in + nt(grad_up_low, upward_f)
    grad_first_in, grad_first_gain, grad_first_shift = norm_backward(grad_first, first_normal, first_inv, first_gain_f)
    grad_branch_low = low(grad_first_in)
    grad_out_weight = row_dot(attended, grad_branch_low)
    grad_out_bias = jnp.sum(as_float(grad_branch_low), axis=0)
    grad_attended = low(nt(grad_branch_low, outproj_f))

    head = jnp.arange(width)[:, None] // HD == jnp.arange(H)[None, :]
    delta = jnp.dot(
        as_float(grad_attended) * as_float(attended), as_float(head), precision=lax.Precision.HIGHEST
    )
    feat_own = jnp.where(jnp.arange(PAIR) < lane + 48, feat_own, delta_lanes(delta, lane))
    packed = jnp.concatenate([grad_attended, feat_own], axis=1)
    values = jnp.pad(sums[None], ((0, 7), (0, 125)))
    backward = functools.partial(
        attn_bwd, projected, grad_attended, query_feat, feat_own, key_feat, delta_key(ext, lane), lane, tok
    )
    if fast:
        grads = [low(v) for v in (grad_out_weight, grad_up_weight, grad_down_weight)]
        edges = jnp.stack([packed[:half], packed[tok - half :]])
        out_share, up_share, down_share, sums, grad_q, grad_kv = backward(edges, values, grads, (1, 2, 2), 0.0, 2)
    else:
        edges = jnp.stack(neighbours(packed[:half], packed[tok - half :]))
        sums, grad_q, grad_kv = backward(edges, lax.psum(values, AXES))
    sums = sums[0, :3]
    branch_rms = jnp.sqrt(sums / (tok * width * lax.axis_size(AXES)))
    grad_proj_low = jnp.concatenate([grad_q, grad_kv[0], grad_kv[1]], axis=1)
    grad_in_weight = row_dot(start_low, grad_proj_low)
    grad_query_bias = jnp.sum(as_float(grad_q), axis=0)
    grad_value_bias = jnp.sum(as_float(grad_kv[1]), axis=0)
    grad_start = grad_first_in + nt(grad_proj_low, inproj_f)
    grad_time_bias = jnp.sum(grad_start, axis=0)
    grad_time_weight = time_value * grad_time_bias
    input_grad = low(grad_start)

    small_grads = (grad_time_weight, grad_time_bias, grad_query_bias, grad_value_bias, grad_out_bias, grad_first_gain,
                   grad_first_shift, grad_down_bias, grad_second_gain, grad_second_shift)
    if fast:
        cols = grad_up_bias.reshape(width // rows, -1, rows).transpose(1, 0, 2).reshape(-1, width)
        cols = jnp.concatenate([jnp.stack(small_grads), cols]).T
        cols = jnp.pad(cols, ((0, 0), (0, 128 - cols.shape[1])))
        in_share, last = scatter_all((low(grad_in_weight), low(cols)), (3, 1), 0.5, 3)
        small_shares = [last[:, i] for i in range(SMALL)]
        up_bias_share = last[:, SMALL : SMALL + hidden // width].T.reshape(-1)
    else:
        share = lambda v: lax.psum_scatter(v, AXES, scatter_dimension=0, tiled=True)
        down_share, up_share, out_share, in_share, up_bias_share = map(
            share, (grad_down_weight, grad_up_weight, grad_out_weight, grad_in_weight, grad_up_bias)
        )
        small_shares = [share(v) for v in small_grads]
    (time_weight_s, time_bias_s, query_bias_s, value_bias_s, out_bias_s, first_gain_s, first_shift_s,
     down_bias_s, second_gain_s, second_shift_s) = small_shares
    return (layer_out, input_grad, time_weight_s, time_bias_s, in_share, query_bias_s, value_bias_s, out_share,
            out_bias_s, first_gain_s, first_shift_s, up_share, up_bias_share, down_share, down_bias_s,
            second_gain_s, second_shift_s, branch_rms)


def solution(mesh):
    both = P(AXES)
    matrix = P(AXES, None)
    in_specs = (matrix, matrix, P("seq"), P("seq", None), both,
                both, both, matrix, both, both, matrix, both, both, both, matrix, both, matrix, both, both, both)
    out_specs = (matrix, matrix, both, both, matrix, both, both, matrix, both, both, both, matrix, both, matrix,
                 both, both, both, P())
    fast = dict(mesh.shape) == {"seq": 4, "blk": 8}
    return jax.shard_map(
        functools.partial(per_device, fast), mesh=mesh, in_specs=in_specs, out_specs=out_specs, check_vma=False
    )
```

```python
import functools

import jax
import jax.numpy as jnp
from jax import lax
from jax.experimental import pallas as pl
from jax.experimental.pallas import tpu as pltpu
from jax.sharding import PartitionSpec as P

HD = 64
TQ = 256
PAIR = 2 * HD
NEG = -(2.0**100)


def nt(a, b):
    return lax.dot_general(a, b, (((1,), (1,)), ((), ())), preferred_element_type=jnp.float32)


def nn(a, b):
    return jnp.dot(a, b, preferred_element_type=jnp.float32)


def schedule(step, first, last, job, length):
    at = [first + (2 * i * (last - first) + length - 1) // (2 * (length - 1)) for i in range(length)]
    for s in range(last + 1):
        count = at.count(s)
        if count:

            @pl.when(step == s)
            def _():
                for _ in range(count):
                    next(job)


def fwd_kernel(plan, count, tok, lanes, *refs):
    shards, refs = refs[:count], refs[count:]
    edges, shift_ref, start_ref, wq, wk, wv, bias_ref, qf_ref, kf_ref, refs = *refs[:9], refs[9:]
    fulls, refs = refs[:count], refs[count:]
    proj_ref, o_ref, f_ref, ka, va, qa, halo = refs[:7]
    step = pl.program_id(0)
    half = halo.shape[1]
    ext = tok + 2 * half
    window = 2 * half + TQ
    if count:
        send_sem, recv_sem, local_sem = refs[7:]
        pos = Place()

        @pl.when(step == 0)
        def _():
            meet(pos, False)

        sends = Sends(send_sem, recv_sem, pos.to)
        schedule(step, 0, FWD_STEPS - 1, gather_job(pos, plan, shards, fulls, sends, local_sem), len(plan) + 4)

    @pl.when(step == 0)
    def _():
        for side in range(2):
            for t in range(half // TQ):
                rows = slice(t * TQ, (t + 1) * TQ)
                moved = edges[side, rows, :].astype(jnp.float32) + shift_ref[0:1, :] + shift_ref[1:2, :]
                halo[side, rows, :] = moved.astype(jnp.bfloat16)
        ka[:, PAIR:] = kf_ref[...]
        va[:, PAIR:] = jnp.ones((ext, PAIR), jnp.bfloat16)
        f_ref[...] = qf_ref[half : half + tok, :]

    lane = lax.broadcasted_iota(jnp.int32, (TQ, PAIR), 1)
    left = lane < HD
    for t in range(ext // TQ):
        rows = slice(t * TQ, (t + 1) * TQ)
        if t * TQ < half:
            start = halo[0, rows, :]
        elif t * TQ < half + tok:
            start = start_ref[t * TQ - half : (t + 1) * TQ - half, :]
        else:
            start = halo[1, t * TQ - half - tok : (t + 1) * TQ - half - tok, :]
        q = (nn(start, wq[...]) + bias_ref[0:1, :]).astype(jnp.bfloat16)
        k = (nn(start, wk[...]) + bias_ref[1:2, :]).astype(jnp.bfloat16)
        v = (nn(start, wv[...]) + bias_ref[2:3, :]).astype(jnp.bfloat16)
        proj_ref[0, rows, :] = q
        proj_ref[1, rows, :] = k
        proj_ref[2, rows, :] = v
        ka[rows, :PAIR] = k
        va[rows, :PAIR] = v
        if half <= t * TQ < half + tok:
            own = t - half // TQ
            q = q * jnp.bfloat16(HD**-0.5)
            zero = jnp.zeros_like(q)
            qa[2 * own, :, :PAIR] = jnp.where(left, q, zero)
            qa[2 * own + 1, :, :PAIR] = jnp.where(left, zero, q)
            qa[2 * own, :, PAIR:] = qf_ref[rows, :]
            qa[2 * own + 1, :, PAIR:] = qf_ref[rows, :]
    for t in range(tok // TQ):
        win = slice(t * TQ, t * TQ + window)
        own = slice(t * TQ, (t + 1) * TQ)
        feat = f_ref[own, :]
        out = []
        for side in range(2):
            s = nt(qa[2 * t + side], ka[win, :])
            top = jnp.max(s, axis=1, keepdims=True)
            r = nn(jnp.exp(s - top).astype(jnp.bfloat16), va[win, :])
            total = r[:, PAIR:]
            out.append(r[:, :PAIR] / total)
            rest = top + jnp.log(total)
            for part in range(3):
                piece = rest.astype(jnp.bfloat16)
                rest = rest - piece.astype(jnp.float32)
                feat = jnp.where(lane == lanes + part * 16 + 2 * step + side, piece, feat)
        o_ref[own, :] = jnp.where(left, out[0], out[1]).astype(jnp.bfloat16)
        f_ref[own, :] = feat


FWD_STEPS = 8


def attn_fwd(edges, shift, start, inproj, bias, qf, kf, lanes, shards=(), parts=(), share=0.0, collective=None):
    tok, width = start.shape
    half = edges.shape[1]
    ext = tok + 2 * half
    pairs = width // PAIR
    count = len(shards)
    plan = pieces([v.shape[1] for v in shards], parts, share)
    anywhere, vmem = pl.BlockSpec(memory_space=pl.ANY), pl.BlockSpec(memory_space=pltpu.VMEM)
    col = lambda base: pl.BlockSpec((width, PAIR), lambda i: (0, base + i))
    fix = pl.BlockSpec((ext, PAIR), lambda i: (0, 0))
    comm = dict(collective_id=collective, has_side_effects=True) if count else {}
    return pl.pallas_call(
        functools.partial(fwd_kernel, plan, count, tok, lanes),
        grid=(pairs,),
        in_specs=[anywhere] * count
        + [vmem, vmem, vmem, col(0), col(pairs), col(2 * pairs),
           pl.BlockSpec((8, PAIR), lambda i: (0, i)), fix, fix],
        out_specs=[anywhere] * count
        + [pl.BlockSpec((3, ext, PAIR), lambda i: (0, 0, i)), pl.BlockSpec((tok, PAIR), lambda i: (0, i)),
           pl.BlockSpec((tok, PAIR), lambda i: (0, 0))],
        out_shape=full_shapes(shards)
        + [jax.ShapeDtypeStruct((3, ext, width), jnp.bfloat16), jax.ShapeDtypeStruct((tok, width), jnp.bfloat16),
           jax.ShapeDtypeStruct((tok, PAIR), jnp.bfloat16)],
        scratch_shapes=[
            pltpu.VMEM((ext, 2 * PAIR), jnp.bfloat16),
            pltpu.VMEM((ext, 2 * PAIR), jnp.bfloat16),
            pltpu.VMEM((2 * tok // TQ, TQ, 2 * PAIR), jnp.bfloat16),
            pltpu.VMEM((2, half, width), jnp.bfloat16),
        ] + (semaphores(len(plan) * SENDS, len(plan)) if count else []),
        compiler_params=pltpu.CompilerParams(
            vmem_limit_bytes=56 << 20, dimension_semantics=("arbitrary",), **comm
        ),
        name="attention",
    )(*shards, edges, shift, start, inproj, inproj, inproj, bias, qf, kf)


def bwd_kernel(plan, count, counts, tok, lanes, *refs):
    grads, refs = refs[:count], refs[count:]
    edges, values, refs = refs[0], refs[1], refs[2:]
    q_ref, k_ref, v_ref, d_ref, qf_ref, own_ref, kf_ref, vf_ref, refs = *refs[:8], refs[8:]
    outs, refs = refs[:count], refs[count:]
    result, gq_ref, gkv_ref, refs = *refs[:3], refs[3:]
    one, two, feats, halo, refs = *refs[:4], refs[4:]
    step = pl.program_id(0)
    ext = k_ref.shape[1]
    half = (ext - tok) // 2
    window = 2 * half + TQ
    pairs = BWD_STEPS // 2
    pair = lax.rem(step, pairs)
    if count:
        send_sem, recv_sem, local_sem, sums, refs = *refs[:4], refs[4:]
        pos = Place()

        @pl.when(step == 0)
        def _():
            meet(pos, True)

        sends = Sends(send_sem, recv_sem, pos.to)

        def work():
            neighbour = halo_plan(pos, edges, halo, sends, local_sem, len(plan))
            total = total_plan(values, result, sums, sends)
            next(neighbour)
            for i, _ in enumerate(scatter_job(pos, plan, counts, grads, outs, refs, sends, local_sem)):
                if i < 6:
                    next(total)
                if i == HALO_TURN:
                    next(neighbour)
                yield

        schedule(step, 0, BWD_STEPS - 1, work(), len(plan) + 4)
    else:

        @pl.when(step == 0)
        def _():
            halo[...] = edges[...]
            result[...] = values[...]

    lane = lax.broadcasted_iota(jnp.int32, (TQ, PAIR), 1)
    left = lane < HD

    @pl.when(step == 0)
    def _():
        one[2, :, PAIR:] = kf_ref[...]
        two[2, :, PAIR:] = vf_ref[...]
        feats[half : half + tok, :] = own_ref[...]

    @pl.when(step == pairs)
    def _():
        for t in range(half // TQ):
            for side, base in ((0, 0), (1, half + tok)):
                rows = slice(base + t * TQ, base + (t + 1) * TQ)
                got = halo[side, t * TQ : (t + 1) * TQ, PAIR * pairs :]
                feats[rows, :] = jnp.where(lane < lanes, qf_ref[rows, :], got)

    def sides(tile, rows, d):
        q = q_ref[0, rows, :] * jnp.bfloat16(HD**-0.5)
        feat = feats[rows, :]
        zero = jnp.zeros_like(q)
        for side in range(2):
            mine = left if side == 0 else ~left
            kept = jnp.where((lane < lanes) | (lax.rem(lane - lanes + 128, 16) == 2 * pair + side), feat, zero)
            one[side, rows, :PAIR] = jnp.where(mine, q, zero)
            one[side, rows, PAIR:] = kept
            two[side, rows, :PAIR] = jnp.where(mine, d, zero)
            two[side, rows, PAIR:] = kept

    one[2, :, :PAIR] = k_ref[0]
    two[2, :, :PAIR] = v_ref[0]
    for t in range(tok // TQ):
        sides(t, slice(half + t * TQ, half + (t + 1) * TQ), d_ref[t * TQ : (t + 1) * TQ, :])

    @pl.when(step < pairs)
    def _():
        for t in range(tok // TQ):
            win = slice(t * TQ, t * TQ + window)
            rows = slice(half + t * TQ, half + (t + 1) * TQ)
            parts = []
            for side in range(2):
                p = jnp.exp(nt(one[side, rows, :], one[2, win, :]))
                g = (p * nt(two[side, rows, :], two[2, win, :])).astype(jnp.bfloat16)
                parts.append(nn(g, k_ref[0, win, :]))
            gq_ref[t * TQ : (t + 1) * TQ, :] = (jnp.where(left, *parts) * HD**-0.5).astype(jnp.bfloat16)

    @pl.when(step >= pairs)
    def _():
        at = pl.ds(pl.multiple_of(pair * PAIR, PAIR), PAIR)
        for t in range(half // TQ):
            for side, base in ((0, 0), (1, half + tok)):
                sides(t, slice(base + t * TQ, base + (t + 1) * TQ), halo[side, t * TQ : (t + 1) * TQ, at])
        for t in range(tok // TQ):
            win = slice(t * TQ, t * TQ + window)
            rows = slice(half + t * TQ, half + (t + 1) * TQ)
            dk, dv = 0.0, 0.0
            for side in range(2):
                p = jnp.exp(nt(one[2, rows, :], one[side, win, :]))
                g = (p * nt(two[2, rows, :], two[side, win, :])).astype(jnp.bfloat16)
                dk = dk + nn(g, one[side, win, :PAIR])
                dv = dv + nn(p.astype(jnp.bfloat16), two[side, win, :PAIR])
            gkv_ref[0, t * TQ : (t + 1) * TQ, :] = dk.astype(jnp.bfloat16)
            gkv_ref[1, t * TQ : (t + 1) * TQ, :] = dv.astype(jnp.bfloat16)


BWD_STEPS = 16
HALO_TURN = 3


def attn_bwd(proj, grad, qf, own_feat, kf, vf, lanes, tok, edges, values, grads=(), parts=(), share=0.0, collective=None):
    _, ext, width = proj.shape
    pairs = width // PAIR
    half = (ext - tok) // 2
    grads, plan, counts, bufs, shapes = scatter_layout(grads, parts, share)
    count = len(grads)
    anywhere, vmem = pl.BlockSpec(memory_space=pl.ANY), pl.BlockSpec(memory_space=pltpu.VMEM)
    third = lambda k: pl.BlockSpec((1, ext, PAIR), lambda i: (k, 0, lax.rem(i, pairs)))
    fix = lambda rows: pl.BlockSpec((rows, PAIR), lambda i: (0, 0))
    comm = dict(collective_id=collective, has_side_effects=True) if count else {}
    scratch = [
        pltpu.VMEM((3, ext, 2 * PAIR), jnp.bfloat16),
        pltpu.VMEM((3, ext, 2 * PAIR), jnp.bfloat16),
        pltpu.VMEM((ext, PAIR), jnp.bfloat16),
        pltpu.VMEM((2, half, width + PAIR), jnp.bfloat16),
    ]
    if count:
        scratch += semaphores(len(plan) * SENDS + 7, len(plan) + 1) + [pltpu.VMEM((10, 8, 128), jnp.float32)] + bufs
    return pl.pallas_call(
        functools.partial(bwd_kernel, plan, count, counts, tok, lanes),
        grid=(2 * pairs,),
        in_specs=[anywhere] * count
        + [anywhere if count else vmem, vmem, third(0), third(1), third(2),
           pl.BlockSpec((tok, PAIR), lambda i: (0, lax.rem(i, pairs))), fix(ext), fix(tok), fix(ext), fix(ext)],
        out_specs=[vmem] * count
        + [vmem, pl.BlockSpec((tok, PAIR), lambda i: (0, lax.min(i, pairs - 1))),
           pl.BlockSpec((2, tok, PAIR), lambda i: (0, 0, lax.max(i - pairs, 0)))],
        out_shape=shapes
        + [jax.ShapeDtypeStruct(values.shape, jnp.float32), jax.ShapeDtypeStruct((tok, width), jnp.bfloat16),
           jax.ShapeDtypeStruct((2, tok, width), jnp.bfloat16)],
        scratch_shapes=scratch,
        compiler_params=pltpu.CompilerParams(
            vmem_limit_bytes=62 << 20, dimension_semantics=("arbitrary",), **comm
        ),
        name="attention_gradients",
    )(*grads, edges, values, proj, proj, proj, grad, qf, own_feat, kf, vf)


def bits(values, count):
    planes = (values[:, None] >> jnp.arange(count, dtype=jnp.int32)[None, :]) & 1
    return planes.astype(jnp.float32)


def features(item, places, keep, n_items):
    ext = item.shape[0]
    nb = (n_items + 1).bit_length()
    pb = (ext - 1).bit_length()
    lanes = 2 * (nb + pb)
    assert lanes + 80 <= PAIR and ext == 1 << pb
    ib = bits(item + 1, nb)
    ps = bits(places, pb)
    kept = keep.astype(jnp.float32)[:, None]
    lost = 1 - kept
    qf = jnp.concatenate([ib, 1 - ib, ps, 1 - ps, jnp.zeros((ext, PAIR - lanes))], axis=1)
    kf = jnp.concatenate([NEG * kept * (1 - ib), NEG * kept * ib, NEG * lost * (1 - ps), NEG * lost * ps,
                          -jnp.ones((ext, 48)), jnp.zeros((ext, PAIR - 48 - lanes))], axis=1)
    return qf.astype(jnp.bfloat16), kf.astype(jnp.bfloat16), lanes


def delta_key(ext, lanes):
    lane = jnp.arange(PAIR)
    vf = jnp.where((lane >= lanes + 48) & (lane < lanes + 80), -1.0, 0.0)
    return jnp.broadcast_to(vf[None], (ext, PAIR)).astype(jnp.bfloat16)


MESH = pl.DeviceIdType.MESH


class Place:
    def __init__(self):
        seq, blk = lax.axis_index("seq"), lax.axis_index("blk")
        self.seq, self.blk, self.last = seq, blk, lax.axis_size("blk") - 1
        self.x, self.c, self.z, self.y = x, c, z, y = seq // 2, lax.rem(seq, 2), blk // 2, lax.rem(blk, 2)
        self.nx, self.nc, self.ny = nx, nc, ny = 1 - x, 1 - c, 1 - y
        low_bit, high_bit = lax.rem(z, 2), z // 2
        flips = {1: (1 - low_bit, high_bit), 2: (low_bit, 1 - high_bit), 3: (1 - low_bit, 1 - high_bit)}
        self.nz = {k: high * 2 + bit for k, (bit, high) in flips.items()}
        device = lambda x, c, z, y: (x * 2 + c, z * 2 + y)
        self.to = {"x": device(nx, c, z, y), "y": device(x, c, z, ny), "c": device(x, nc, z, y)}
        for k in (1, 2, 3):
            self.to[k] = device(x, c, self.nz[k], y)
        self.below = (seq, lax.max(blk - 1, 0))
        self.above = (seq, lax.min(blk + 1, self.last))


class Copy:
    def __init__(self, make):
        self.make = make

    def start(self):
        self.make().start()
        return self

    def wait(self):
        self.make().wait()

    def wait_send(self):
        self.make().wait_send()

    def wait_recv(self):
        self.make().wait_recv()


def local_copy(src, dst, sems, at):
    return Copy(lambda: pltpu.make_async_copy(src(), dst(), sems.at[at])).start()


class Sends:
    def __init__(self, send_sem, recv_sem, to):
        self.send_sem, self.recv_sem, self.to, self.used, self.live = send_sem, recv_sem, to, 0, []

    def describe(self, src, dst, device):
        at = self.used
        self.used += 1
        return Copy(
            lambda: pltpu.make_async_remote_copy(
                src_ref=src(), dst_ref=dst(), send_sem=self.send_sem.at[at], recv_sem=self.recv_sem.at[at],
                device_id=device, device_id_type=MESH,
            )
        )

    def start(self, src, dst, partner):
        copy = self.describe(src, dst, self.to[partner]).start()
        self.live.append(copy)
        return copy

    def finish(self):
        for copy in self.live:
            copy.wait_send()


def gather_plan(pos, shard, full, sends, local, number, base, wide, at):
    x, c, z, y, nx, nc, ny = pos.x, pos.c, pos.z, pos.y, pos.nx, pos.nc, pos.ny
    every, one, two = pl.ds(base, wide), pl.ds(base, at), pl.ds(base + at, wide - at)

    def send(partner, *index):
        return sends.start(lambda: full.at[index], lambda: full.at[index], partner)

    rows = slice(None)
    source, target = lambda: shard.at[:, every], lambda: full.at[x, c, z, y, :, every]
    own = local_copy(source, target, local, number)
    line = [sends.start(source, target, k) for k in (1, 2, 3)]
    yield
    own.wait()
    for copy in line:
        copy.wait_recv()
    if at:
        a = send("x", x, c, rows, y, rows, one)
    b = send("y", x, c, rows, y, rows, two)
    core = [send("c", x, c, rows, y, rows, every)]
    yield
    if at:
        a.wait_recv()
        a2 = send("y", rows, c, rows, y, rows, one)
        core.append(send("c", nx, c, rows, y, rows, one))
    b.wait_recv()
    b2 = send("x", x, c, rows, rows, rows, two)
    core.append(send("c", x, c, rows, ny, rows, two))
    yield
    if at:
        a2.wait_recv()
        core.append(send("c", rows, c, rows, ny, rows, one))
    b2.wait_recv()
    core.append(send("c", nx, c, rows, rows, rows, two))
    yield
    for copy in core:
        copy.wait_recv()
    yield


SENDS = 12


def turns(plans, last):
    for turn in range(len(plans) + 4):
        for k in reversed(range(len(plans))):
            if 0 <= turn - k <= 4:
                next(plans[k])
        if turn == len(plans) + 3:
            last()
        yield


def pieces(widths, parts, share):
    plan = []
    for k, (whole, count) in enumerate(zip(widths, parts)):
        wide = whole // count
        plan += [(k, p * wide, wide, int(wide * share) // 128 * 128) for p in range(count)]
    return plan


def halo_plan(pos, edges, halo, sends, local, number):
    blk, last = pos.blk, pos.last
    down = sends.describe(lambda: edges.at[0], lambda: halo.at[1], pos.below)
    up = sends.describe(lambda: edges.at[1], lambda: halo.at[0], pos.above)
    fill = [
        Copy(lambda k=k: pltpu.make_async_copy(edges.at[k], halo.at[k], local.at[number])) for k in (0, 1)
    ]

    def where(test, *acts):
        @pl.when(test)
        def _():
            for act in acts:
                act()

    where(blk > 0, down.start)
    where(blk < last, up.start)
    where(blk == 0, fill[0].start)
    where(blk == last, fill[1].start)
    yield
    where(blk > 0, down.wait_send, up.wait_recv)
    where(blk < last, up.wait_send, down.wait_recv)
    where(blk == 0, fill[0].wait)
    where(blk == last, fill[1].wait)
    yield


def meet(pos, halo):
    barrier = pltpu.get_barrier_semaphore()
    for device in pos.to.values():
        pl.semaphore_signal(barrier, inc=1, device_id=device, device_id_type=MESH)
    count = len(pos.to)
    if halo:

        @pl.when(pos.blk > 0)
        def _():
            pl.semaphore_signal(barrier, inc=1, device_id=pos.below, device_id_type=MESH)

        @pl.when(pos.blk < pos.last)
        def _():
            pl.semaphore_signal(barrier, inc=1, device_id=pos.above, device_id_type=MESH)

        count = count + 2 - jnp.where(pos.blk == 0, 1, 0) - jnp.where(pos.blk == pos.last, 1, 0)
    pl.semaphore_wait(barrier, count)


def gather_job(pos, plan, shards, fulls, sends, local):
    yield from turns([
        gather_plan(pos, shards[k], fulls[k], sends, local, i, base, wide, at) for i, (k, base, wide, at) in enumerate(plan)
    ], sends.finish)


def gather_kernel(plan, count, *refs):
    shards, edges, fulls, halo = refs[:count], refs[count], refs[count + 1 : 2 * count + 1], refs[2 * count + 1]
    send_sem, recv_sem, local_sem = refs[2 * count + 2 :]
    pos = Place()
    meet(pos, True)
    sends = Sends(send_sem, recv_sem, pos.to)
    neighbour = halo_plan(pos, edges, halo, sends, local_sem, len(plan))
    next(neighbour)
    for _ in gather_job(pos, plan, shards, fulls, sends, local_sem):
        pass
    next(neighbour)


def semaphores(number, local):
    return [pltpu.SemaphoreType.DMA((number,)), pltpu.SemaphoreType.DMA((number,)), pltpu.SemaphoreType.DMA((local,))]


def full_shapes(shards):
    return [jax.ShapeDtypeStruct((2, 2, 4, 2) + v.shape, jnp.bfloat16) for v in shards]


def gather_all(shards, parts, share, edges, collective):
    count = len(shards)
    plan = pieces([v.shape[1] for v in shards], parts, share)
    anywhere = pl.BlockSpec(memory_space=pl.ANY)
    return pl.pallas_call(
        functools.partial(gather_kernel, plan, count),
        in_specs=[anywhere] * (count + 1),
        out_specs=[anywhere] * (count + 1),
        out_shape=full_shapes(shards) + [jax.ShapeDtypeStruct(edges.shape, edges.dtype)],
        scratch_shapes=semaphores(len(plan) * SENDS + 2, len(plan) + 1),
        compiler_params=pltpu.CompilerParams(collective_id=collective, has_side_effects=True),
        name="gather_weights",
    )(*shards, edges)


def widen(value):
    return value.astype(jnp.float32)


def scatter_plan(pos, grad, out, bufs, sends, local, number, base, wide, at, held=False):
    x, c, z, y, nx, nc, ny = pos.x, pos.c, pos.z, pos.y, pos.nx, pos.nc, pos.ny
    every, one, two = pl.ds(base, wide), pl.ds(0, at), pl.ds(at, wide - at)
    if held:
        own, bufs = lambda: grad.at[:, c, :, :, :, every], (None,) + tuple(bufs)
    else:
        own = lambda: bufs[0]
    got, one1, two1, one2, two2, line, ends = bufs[1:] if at else bufs[1:2] + (None,) + bufs[2:3] + (None,) + bufs[3:]
    low = jnp.bfloat16
    if not held:
        load = local_copy(lambda: grad.at[:, c, :, :, :, every], own, local, number)
    cross = sends.start(lambda: grad.at[:, nc, :, :, :, every], lambda: got, "c")
    yield
    if not held:
        load.wait()
    cross.wait_recv()

    @pl.loop(0, 8)
    def _(i):
        mine = own().at[i // 4, lax.rem(i, 4)]
        mine[...] = (widen(mine[...]) + widen(got[i // 4, lax.rem(i, 4)])).astype(low)

    if at:
        a = sends.start(lambda: own().at[:, :, ny, :, one], lambda: one1, "y")
    b = sends.start(lambda: own().at[nx, :, :, :, two], lambda: two1, "x")
    yield
    if at:
        a.wait_recv()

        @pl.loop(0, 8)
        def _(i):
            one1[i // 4, lax.rem(i, 4)] = (
                widen(own().at[i // 4, lax.rem(i, 4), y, :, one][...]) + widen(one1[i // 4, lax.rem(i, 4)])
            ).astype(low)

        a2 = sends.start(lambda: one1.at[nx], lambda: one2, "x")
    b.wait_recv()

    @pl.loop(0, 4)
    def _(i):
        two1[i] = (widen(own().at[x, i, :, :, two][...]) + widen(two1[i])).astype(low)

    b2 = sends.start(lambda: two1.at[:, ny], lambda: two2, "y")
    yield
    if at:
        a2.wait_recv()
    b2.wait_recv()

    @pl.loop(0, 4)
    def _(i):
        if at:
            line[i, :, :at] = (widen(one1[x, i]) + widen(one2[i])).astype(low)
        line[i, :, at:] = (widen(two1[i, y]) + widen(two2[i])).astype(low)

    last = [
        sends.start(lambda k=k: line.at[pos.nz[k]], lambda k=k: ends.at[k - 1], k) for k in (1, 2, 3)
    ]
    yield
    for copy in last:
        copy.wait_recv()
    out[:, base : base + wide] = widen(line[z]) + widen(ends[0]) + widen(ends[1]) + widen(ends[2])
    yield


def scatter_bufs(rows, wide, at, held=False):
    shapes = [(2, 4, 2, rows, wide)] * (1 if held else 2)
    if at:
        shapes += [(2, 4, rows, at), (4, 2, rows, wide - at), (4, rows, at)]
    else:
        shapes += [(4, 2, rows, wide)]
    shapes += [(4, rows, wide - at), (4, rows, wide), (3, rows, wide)]
    return [pltpu.VMEM(s, jnp.bfloat16) for s in shapes]


def total_plan(values, result, bufs, sends):
    partners = ("c", "x", "y", 1, 2)
    for i, partner in enumerate(partners):
        source = (lambda i=i: bufs.at[2 * i - 1]) if i else (lambda: values)
        copy = sends.start(source, lambda i=i: bufs.at[2 * i], partner)
        yield
        copy.wait_recv()
        total = source()[...] + bufs[2 * i]
        if i + 1 < len(partners):
            bufs[2 * i + 1] = total
        else:
            result[...] = total
    yield


def scatter_job(pos, plan, counts, grads, outs, bufs, sends, local, held=False):
    plans = []
    for i, (k, base, wide, at) in enumerate(plan):
        first = sum(counts[:i])
        mine = bufs[first : first + counts[i]]
        plans.append(scatter_plan(pos, grads[k], outs[k], mine, sends, local, i, base, wide, at, held))
    yield from turns(plans, sends.finish)


def scatter_layout(grads, parts, share):
    grads = [v.reshape(2, 2, 4, 2, v.shape[0] // 32, v.shape[1]) for v in grads]
    plan = pieces([v.shape[-1] for v in grads], parts, share)
    bufs = [scatter_bufs(grads[k].shape[-2], wide, at) for k, base, wide, at in plan]
    shapes = [jax.ShapeDtypeStruct(v.shape[-2:], jnp.float32) for v in grads]
    return grads, plan, [len(b) for b in bufs], sum(bufs, []), shapes


def scatter_kernel(plan, count, counts, *refs):
    grads, outs, refs = refs[:count], refs[count : 2 * count], refs[2 * count :]
    send_sem, recv_sem, local_sem = refs[:3]
    pos = Place()
    meet(pos, False)
    sends = Sends(send_sem, recv_sem, pos.to)
    for _ in scatter_job(pos, plan, counts, grads, outs, refs[3:], sends, local_sem):
        pass


def scatter_all(grads, parts, share, collective):
    count = len(grads)
    grads, plan, counts, bufs, shapes = scatter_layout(grads, parts, share)
    anywhere, vmem = pl.BlockSpec(memory_space=pl.ANY), pl.BlockSpec(memory_space=pltpu.VMEM)
    return pl.pallas_call(
        functools.partial(scatter_kernel, plan, count, counts),
        in_specs=[anywhere] * count,
        out_specs=[vmem] * count,
        out_shape=shapes,
        scratch_shapes=semaphores(len(plan) * SENDS, len(plan)) + bufs,
        compiler_params=pltpu.CompilerParams(
            collective_id=collective, has_side_effects=True, vmem_limit_bytes=58 << 20
        ),
        name="sum_gradients",
    )(*grads)


FT = 512
ROWS = 256


def normalize(values):
    centered = values - jnp.mean(values, axis=1, keepdims=True)
    inv = lax.rsqrt(jnp.mean(centered * centered, axis=1, keepdims=True) + 1e-05)
    return centered * inv, inv


def normalize_back(grad, normal, inv):
    return inv * (
        grad - jnp.mean(grad, axis=1, keepdims=True) - normal * jnp.mean(grad * normal, axis=1, keepdims=True)
    )


def column_sum(values):
    return jnp.sum(values, axis=0, keepdims=True)


def ffn_kernel(plan, count, ups, *refs):
    source, att, inp, wo, wu, vec, ub, cot = refs[:8]
    if count:
        full, refs = refs[8], refs[9:]
    else:
        full, refs = source, refs[8:]
    hid, slope, normal_ref, inv_ref, low_ref, out_ref, grad_ref, grad_low_ref, sums, keep, wd, load = refs[:12]
    step = pl.program_id(0)
    tok = att.shape[0]
    if count:
        send_sem, recv_sem, local_sem = refs[12:]
        pos = Place()

        @pl.when(step == 0)
        def _():
            meet(pos, False)

        sends = Sends(send_sem, recv_sem, pos.to)
        schedule(step, 0, ups, gather_job(pos, plan, [source], [full], sends, local_sem), len(plan) + 4)
    @pl.when(step == 0)
    def _():
        sums[...] = jnp.zeros_like(sums)
        for r in range(tok // ROWS):
            rows = slice(r * ROWS, (r + 1) * ROWS)
            branch = nn(att[rows, :], wo[...]) + vec[2:3, :]
            start = inp[rows, :].astype(jnp.float32) + vec[0:1, :] + vec[1:2, :]
            normal, inv = normalize(start + branch)
            normal_ref[rows, :] = normal
            inv_ref[rows, :] = jnp.broadcast_to(inv, (ROWS, 128))
            low_ref[rows, :] = (normal * vec[3:4, :] + vec[4:5, :]).astype(jnp.bfloat16)
            sums[3:4, :] += column_sum(start * start)
            sums[4:5, :] += column_sum(branch * branch)

    @pl.when(step < ups)
    def _():
        at = pl.ds(pl.multiple_of(step * FT, FT), FT)
        for r in range(tok // ROWS):
            rows = slice(r * ROWS, (r + 1) * ROWS)
            up = nn(low_ref[rows, :], wu[...]) + ub[0:1, :]
            phi = 0.5 * (1.0 + lax.erf(up * 2.0**-0.5))
            h = (up * phi).astype(jnp.bfloat16)
            hid[rows, :] = h
            keep[rows, at] = h
            slope[rows, :] = (phi + up * (jnp.exp(-0.5 * up * up) * 0.3989422804014327)).astype(jnp.bfloat16)

    @pl.when(step == ups)
    def _():
        copy = pltpu.make_async_copy(full, wd, load)
        copy.start()
        copy.wait()

    @pl.when(step >= ups)
    def _():
        rows = pl.ds(pl.multiple_of((step - ups) * ROWS, ROWS), ROWS)
        weight = wd[...].reshape(-1, wd.shape[-1])
        branch = nn(keep[rows, :], weight) + vec[5:6, :]
        first = normal_ref[rows, :] * vec[3:4, :] + vec[4:5, :]
        normal, inv = normalize(first + branch)
        out_ref[...] = (normal * vec[6:7, :] + vec[7:8, :]).astype(jnp.bfloat16)
        g = cot[...].astype(jnp.float32)
        grad = normalize_back(g * vec[6:7, :], normal, inv)
        grad_ref[...] = grad
        low_grad = grad.astype(jnp.bfloat16)
        grad_low_ref[...] = low_grad
        sums[0:1, :] += column_sum(g * normal)
        sums[1:2, :] += column_sum(g)
        sums[2:3, :] += column_sum(low_grad.astype(jnp.float32))
        sums[5:6, :] += column_sum(branch * branch)


def ffn_forward(source, att, inp, wo, wu, vec, ub, cot, parts=(), share=0.0, collective=None):
    tok, width = att.shape
    wide = wu.shape[1]
    ups, downs = wide // FT, tok // ROWS
    count = 1 if parts else 0
    plan = pieces([source.shape[1]], parts, share) if count else []
    anywhere, vmem = pl.BlockSpec(memory_space=pl.ANY), pl.BlockSpec(memory_space=pltpu.VMEM)
    tile = pl.BlockSpec((tok, FT), lambda i: (0, lax.min(i, ups - 1)))
    row = pl.BlockSpec((ROWS, width), lambda i: (lax.max(i - ups, 0), 0))
    comm = dict(collective_id=collective, has_side_effects=True) if count else {}
    f32, low = jnp.float32, jnp.bfloat16
    shape = jax.ShapeDtypeStruct
    wd_shape = (2, 2, 4, 2) + source.shape if count else source.shape
    return pl.pallas_call(
        functools.partial(ffn_kernel, plan, count, ups),
        grid=(ups + downs,),
        in_specs=[anywhere, vmem, vmem, vmem, pl.BlockSpec((width, FT), lambda i: (0, lax.min(i, ups - 1))), vmem,
                  pl.BlockSpec((8, FT), lambda i: (0, lax.min(i, ups - 1))), row],
        out_specs=[anywhere] * count + [tile, tile, vmem, vmem, vmem, row, row, row, vmem],
        out_shape=(full_shapes([source]) if count else [])
        + [shape((tok, wide), low), shape((tok, wide), low), shape((tok, width), f32), shape((tok, 128), f32),
           shape((tok, width), low), shape((tok, width), low), shape((tok, width), f32), shape((tok, width), low),
           shape((8, width), f32)],
        scratch_shapes=[pltpu.VMEM((tok, wide), low), pltpu.VMEM(wd_shape, low), pltpu.SemaphoreType.DMA]
        + (semaphores(len(plan) * SENDS, len(plan)) if count else []),
        compiler_params=pltpu.CompilerParams(vmem_limit_bytes=62 << 20, dimension_semantics=("arbitrary",), **comm),
        name="feed_forward",
    )(source, att, inp, wo, wu, vec, ub, cot)


def tn(a, b):
    return lax.dot_general(a, b, (((0,), (0,)), ((), ())), preferred_element_type=jnp.float32)


def back_kernel(plan, count, counts, ups, lanes, *refs):
    hid, gffn, wd, slope, wu, first_low, gsecond, normal_ref, inv_ref, vec, att, wo, feat_ref = refs[:13]
    down, up_grad, out_grad, up_sum, sums, gin_ref, gatt_ref, feat_out, acc, piece, low_grad = refs[13:24]
    refs = refs[24:]
    step = pl.program_id(0)
    tok, width = gffn.shape
    last = 2 * ups + tok // ROWS - 1
    if count:
        dwd, send_sem, recv_sem, local_sem, bufs = *refs[:4], refs[4:]
        pos = Place()

        @pl.when(step == ups)
        def _():
            meet(pos, False)

        sends = Sends(send_sem, recv_sem, pos.to)
        job = scatter_job(pos, plan, counts, [dwd], [down], bufs, sends, local_sem, True)
        schedule(step, ups, last, job, len(plan) + 4)

    @pl.when(step < ups)
    def _():
        grad = tn(hid[...], gffn[...]).astype(jnp.bfloat16)
        if count:
            each = dwd.shape[4]
            for k in range(FT // each):
                at = step * (FT // each) + k
                dwd[at // 16, lax.rem(at // 8, 2), lax.rem(at // 2, 4), lax.rem(at, 2)] = grad[k * each : (k + 1) * each]
        else:
            down[pl.ds(pl.multiple_of(step * FT, FT), FT), :] = grad

    @pl.when((step >= ups) & (step < 2 * ups))
    def _():
        total = jnp.zeros((1, FT), jnp.float32)
        for r in range(tok // ROWS):
            rows = slice(r * ROWS, (r + 1) * ROWS)
            g = (nt(gffn[rows, :], wd[...]) * slope[rows, :].astype(jnp.float32)).astype(jnp.bfloat16)
            piece[rows, :] = g
            total += column_sum(g.astype(jnp.float32))
            more = nt(g, wu[...])

            @pl.when(step == ups)
            def _():
                acc[rows, :] = more

            @pl.when(step > ups)
            def _():
                acc[rows, :] += more

        up_sum[...] = jnp.broadcast_to(total, (8, FT))
        up_grad[...] = tn(first_low[...], piece[...]).astype(jnp.bfloat16)

    @pl.when(step == 2 * ups)
    def _():
        sums[...] = jnp.zeros_like(sums)

    @pl.when(step >= 2 * ups)
    def _():
        rows = pl.ds(pl.multiple_of((step - 2 * ups) * ROWS, ROWS), ROWS)
        g = gsecond[...] + acc[rows, :]
        normal = normal_ref[...]
        grad = normalize_back(g * vec[3:4, :], normal, inv_ref[:, :1])
        gin_ref[...] = grad
        low = grad.astype(jnp.bfloat16)
        low_grad[rows, :] = low
        sums[0:1, :] += column_sum(g * normal)
        sums[1:2, :] += column_sum(g)
        sums[2:3, :] += column_sum(low.astype(jnp.float32))
        gatt = nt(low, wo[...]).astype(jnp.bfloat16)
        gatt_ref[...] = gatt
        both = gatt.astype(jnp.float32) * att[rows, :].astype(jnp.float32)
        lane = lax.broadcasted_iota(jnp.int32, (width, PAIR), 1)
        head = lax.broadcasted_iota(jnp.int32, (width, PAIR), 0) // HD
        pick = (lane >= lanes + 48) & (lane < lanes + 80) & (lax.rem(lane - lanes + 128, 16) == head)
        pick = jnp.where(pick, 1.0, 0.0).astype(jnp.bfloat16)
        high = both.astype(jnp.bfloat16)
        delta = nn(high, pick) + nn((both - high.astype(jnp.float32)).astype(jnp.bfloat16), pick)
        first = delta.astype(jnp.bfloat16)
        second = (delta - first.astype(jnp.float32)).astype(jnp.bfloat16)
        lane = lax.broadcasted_iota(jnp.int32, (ROWS, PAIR), 1)
        feat = feat_ref[...]
        feat = jnp.where((lane >= lanes + 48) & (lane < lanes + 64), first, feat)
        feat_out[...] = jnp.where((lane >= lanes + 64) & (lane < lanes + 80), second, feat)

    @pl.when(step == last)
    def _():
        for k in range(2):
            cols = slice(k * width // 2, (k + 1) * width // 2)
            out_grad[cols, :] = tn(att[:, cols], low_grad[...]).astype(jnp.bfloat16)


def ffn_backward(hid, gffn, wd, slope, wu, first_low, gsecond, normal, inv, vec, att, wo, feat, lanes, parts=(), share=0.0,
                 collective=None):
    tok, wide = hid.shape
    width = gffn.shape[1]
    ups, downs = wide // FT, tok // ROWS
    count = 1 if parts else 0
    f32, low = jnp.float32, jnp.bfloat16
    shape = jax.ShapeDtypeStruct
    vmem = pl.BlockSpec(memory_space=pltpu.VMEM)
    whole = lambda r, c: pl.BlockSpec((r, c), lambda i: (0, 0), pipeline_mode=pl.Buffered(1))
    middle = lambda i: lax.max(lax.min(i - ups, ups - 1), 0)
    tile = pl.BlockSpec((tok, FT), lambda i: (0, middle(i)))
    row = lambda c: pl.BlockSpec((ROWS, c), lambda i: (lax.max(i - 2 * ups, 0), 0))
    scratch = [pltpu.VMEM((tok, width), f32), pltpu.VMEM((tok, FT), low), pltpu.VMEM((tok, width), low)]
    plan, counts, down, comm = [], [], shape((wide, width), low), {}
    if count:
        rows = wide // 32
        plan = pieces([width], parts, share)
        bufs = [scatter_bufs(rows, w, at, True) for _, _, w, at in plan]
        counts = [len(b) for b in bufs]
        scratch += [pltpu.VMEM((2, 2, 4, 2, rows, width), low)] + semaphores(len(plan) * SENDS, len(plan)) + sum(bufs, [])
        down, comm = shape((rows, width), f32), dict(collective_id=collective, has_side_effects=True)
    return pl.pallas_call(
        functools.partial(back_kernel, plan, count, counts, ups, lanes),
        grid=(2 * ups + downs,),
        in_specs=[pl.BlockSpec((tok, FT), lambda i: (0, lax.min(i, ups - 1))), whole(tok, width),
                  pl.BlockSpec((FT, width), lambda i: (middle(i), 0)), tile,
                  pl.BlockSpec((width, FT), lambda i: (0, middle(i))), whole(tok, width), row(width), row(width), row(128),
                  whole(8, width), whole(tok, width), whole(width, width), row(PAIR)],
        out_specs=[vmem, pl.BlockSpec((width, FT), lambda i: (0, middle(i))), whole(width, width),
                   pl.BlockSpec((8, FT), lambda i: (0, middle(i))), whole(8, width), row(width), row(width), row(PAIR)],
        out_shape=[down, shape((width, wide), low), shape((width, width), low), shape((8, wide), f32),
                   shape((8, width), f32), shape((tok, width), f32), shape((tok, width), low), shape((tok, PAIR), low)],
        scratch_shapes=scratch,
        compiler_params=pltpu.CompilerParams(vmem_limit_bytes=62 << 20, dimension_semantics=("arbitrary",), **comm),
        name="feed_forward_gradients",
    )(hid, gffn, wd, slope, wu, first_low, gsecond, normal, inv, vec, att, wo, feat)


H = 16
MAXLEN = 512
TSTEPS = 5000
AXES = ("seq", "blk")
SMALL = 10


def as_float(value):
    return value.astype(jnp.float32)


def low(value):
    return value.astype(jnp.bfloat16)


def row_dot(left, right):
    return lax.dot_general(left, right, (((0,), (0,)), ((), ())), preferred_element_type=jnp.float32)


def neighbours(low_part, high_part):
    count = lax.axis_size("blk")
    up = [(i, i + 1) for i in range(count - 1)]
    down = [(i + 1, i) for i in range(count - 1)]
    return lax.ppermute(high_part, "blk", up), lax.ppermute(low_part, "blk", down)


def item_of(ends, places):
    return jnp.sum((ends[None, :] <= places[:, None]).astype(jnp.int32), axis=1)


def per_device(fast, inputs, cotangent, timestep, lengths, padding, *shards):
    (time_weight, time_bias, inproj, query_bias, value_bias, outproj, outproj_bias, first_gain, first_shift,
     upward_w, upward_bias, downward_w, downward_bias, second_gain, second_shift) = shards
    small = (time_weight, time_bias, query_bias, value_bias, outproj_bias, first_gain, first_shift,
             downward_bias, second_gain, second_shift)
    tok, width = inputs.shape
    half = MAXLEN
    ext = tok + 2 * half
    hidden = upward_w.shape[1]

    keep_own = low(padding)
    mark = jnp.pad(keep_own.reshape(1, tok), ((0, 15), (0, width - tok)))
    edges = jnp.stack([jnp.concatenate([inputs[:half], mark]), jnp.concatenate([inputs[tok - half :], mark])])

    if fast:
        rows = time_weight.shape[0]
        cols = [v[:, None] for v in small] + [upward_bias.reshape(-1, rows).T]
        cols = jnp.concatenate(cols, axis=1)
        cols = jnp.pad(cols, ((0, 0), (0, 128 - cols.shape[1])))
        *fulls, halo = gather_all(
            (inproj, cols), (1, 1), 0.5, edges, 0
        )
        inproj_f, small_f = [v.reshape(-1, v.shape[-1]) for v in fulls]
        small_f = as_float(small_f.T)
        edges = halo
        upward_bias_f = small_f[SMALL : SMALL + hidden // width]
        upward_bias_f = upward_bias_f.reshape(-1, width // rows, rows).transpose(1, 0, 2).reshape(hidden)
    else:
        edges = jnp.stack(neighbours(*edges))
        whole = lambda v: lax.all_gather(v, AXES, axis=0, tiled=True)
        inproj_f, outproj_f, upward_f, downward_f = map(whole, (inproj, outproj, upward_w, downward_w))
        small_f = [as_float(whole(v)) for v in small]
        upward_bias_f = as_float(whole(upward_bias))
    (time_weight_f, time_bias_f, query_bias_f, value_bias_f, outproj_bias_f, first_gain_f, first_shift_f,
     downward_bias_f, second_gain_f, second_shift_f) = [small_f[i] for i in range(SMALL)]

    offset = lax.axis_index("blk") * tok
    ends = jnp.cumsum(lengths[0]).astype(jnp.int32)
    places = offset - half + jnp.arange(ext, dtype=jnp.int32)
    item = jnp.where(places >= 0, item_of(ends, places), -1)
    keep = jnp.concatenate([edges[0, half, tok - half :], keep_own, edges[1, half, :half]])
    edges = edges[:, :half]
    query_feat, key_feat, lane = features(item, places, as_float(keep) > 0.5, lengths.shape[1])

    time_value = as_float(timestep[0]) / TSTEPS
    move = time_value * time_weight_f
    start_vec = as_float(inputs) + move + time_bias_f
    start_low = low(start_vec)
    shift = jnp.pad(jnp.stack([move, time_bias_f]), ((0, 6), (0, 0)))
    bias = jnp.pad(jnp.stack([query_bias_f, jnp.zeros_like(query_bias_f), value_bias_f]), ((0, 5), (0, 0)))
    if fast:
        *fulls, projected, attended, feat_own = attn_fwd(
            edges, shift, start_low, inproj_f, bias, query_feat, key_feat, lane, (outproj, upward_w), (1, 4),
            0.5, 1,
        )
        outproj_f, upward_f = [v.reshape(-1, v.shape[-1]) for v in fulls]
    else:
        projected, attended, feat_own = attn_fwd(
            edges, shift, start_low, inproj_f, bias, query_feat, key_feat, lane
        )
    vec = jnp.stack([move, time_bias_f, outproj_bias_f, first_gain_f, first_shift_f, downward_bias_f, second_gain_f,
                     second_shift_f])
    up_bias = jnp.broadcast_to(upward_bias_f, (8, hidden))
    forward = (attended, inputs, outproj_f, upward_f, vec, up_bias, cotangent)
    if fast:
        downward_f, *results = ffn_forward(downward_w, *forward, (4,), 0.5, 2)
        downward_f = downward_f.reshape(-1, width)
    else:
        results = ffn_forward(downward_f, *forward)
    hidden_low, slope, first_normal, first_inv, first_low, layer_out, grad_second_in, grad_ffn_low, sums = results
    grad_second_gain, grad_second_shift, grad_down_bias = sums[0], sums[1], sums[2]
    sums = jnp.sum(sums[3:6], axis=1)
    backward = functools.partial(
        ffn_backward, hidden_low, grad_ffn_low, downward_f, slope, upward_f, first_low, grad_second_in, first_normal,
        first_inv, vec, attended, outproj_f, feat_own, lane
    )
    (grad_down, grad_up_weight, grad_out_weight, grad_up_bias, sums_back, grad_first_in, grad_attended,
     feat_own) = backward((4,), 0.5, 3) if fast else backward()
    grad_up_bias = grad_up_bias[0]
    grad_first_gain, grad_first_shift, grad_out_bias = sums_back[0], sums_back[1], sums_back[2]
    packed = jnp.concatenate([grad_attended, feat_own], axis=1)
    values = jnp.pad(sums[None], ((0, 7), (0, 125)))
    backward = functools.partial(
        attn_bwd, projected, grad_attended, query_feat, feat_own, key_feat, delta_key(ext, lane), lane, tok
    )
    if fast:
        edges = jnp.stack([packed[:half], packed[tok - half :]])
        down_share = grad_down
        out_share, up_share, sums, grad_q, grad_kv = backward(
            edges, values, (grad_out_weight, grad_up_weight), (1, 4), 0.0, 4
        )
    else:
        edges = jnp.stack(neighbours(packed[:half], packed[tok - half :]))
        sums, grad_q, grad_kv = backward(edges, lax.psum(values, AXES))
    sums = sums[0, :3]
    branch_rms = jnp.sqrt(sums / (tok * width * lax.axis_size(AXES)))
    grad_proj_low = jnp.concatenate([grad_q, grad_kv[0], grad_kv[1]], axis=1)
    grad_in_weight = row_dot(start_low, grad_proj_low)
    grad_query_bias = jnp.sum(as_float(grad_q), axis=0)
    grad_value_bias = jnp.sum(as_float(grad_kv[1]), axis=0)
    grad_start = grad_first_in + nt(grad_proj_low, inproj_f)
    grad_time_bias = jnp.sum(grad_start, axis=0)
    grad_time_weight = time_value * grad_time_bias
    input_grad = low(grad_start)

    small_grads = (grad_time_weight, grad_time_bias, grad_query_bias, grad_value_bias, grad_out_bias, grad_first_gain,
                   grad_first_shift, grad_down_bias, grad_second_gain, grad_second_shift)
    if fast:
        cols = grad_up_bias.reshape(width // rows, -1, rows).transpose(1, 0, 2).reshape(-1, width)
        cols = jnp.concatenate([jnp.stack(small_grads), cols]).T
        cols = jnp.pad(cols, ((0, 0), (0, 128 - cols.shape[1])))
        in_share, last = scatter_all((low(grad_in_weight), low(cols)), (3, 1), 0.5, 5)
        small_shares = [last[:, i] for i in range(SMALL)]
        up_bias_share = last[:, SMALL : SMALL + hidden // width].T.reshape(-1)
    else:
        share = lambda v: lax.psum_scatter(v, AXES, scatter_dimension=0, tiled=True)
        down_share, up_share, out_share, in_share, up_bias_share = map(
            share, map(as_float, (grad_down, grad_up_weight, grad_out_weight, grad_in_weight, grad_up_bias))
        )
        small_shares = [share(v) for v in small_grads]
    (time_weight_s, time_bias_s, query_bias_s, value_bias_s, out_bias_s, first_gain_s, first_shift_s,
     down_bias_s, second_gain_s, second_shift_s) = small_shares
    return (layer_out, input_grad, time_weight_s, time_bias_s, in_share, query_bias_s, value_bias_s, out_share,
            out_bias_s, first_gain_s, first_shift_s, up_share, up_bias_share, down_share, down_bias_s,
            second_gain_s, second_shift_s, branch_rms)


def solution(mesh):
    both = P(AXES)
    matrix = P(AXES, None)
    in_specs = (matrix, matrix, P("seq"), P("seq", None), both,
                both, both, matrix, both, both, matrix, both, both, both, matrix, both, matrix, both, both, both)
    out_specs = (matrix, matrix, both, both, matrix, both, both, matrix, both, both, both, matrix, both, matrix,
                 both, both, both, P())
    fast = dict(mesh.shape) == {"seq": 4, "blk": 8}
    return jax.shard_map(
        functools.partial(per_device, fast), mesh=mesh, in_specs=in_specs, out_specs=out_specs, check_vma=False
    )
```

```python
import functools

import jax
import jax.numpy as jnp
from jax import lax
from jax.experimental import pallas as pl
from jax.experimental.pallas import tpu as pltpu
from jax.sharding import PartitionSpec as P

HD = 64
TQ = 256
PAIR = 2 * HD
NEG = -(2.0**100)


def nt(a, b):
    return lax.dot_general(a, b, (((1,), (1,)), ((), ())), preferred_element_type=jnp.float32)


def nn(a, b):
    return jnp.dot(a, b, preferred_element_type=jnp.float32)


def spread(first, last, length):
    return [first + (2 * i * (last - first) + length - 1) // (2 * (length - 1)) for i in range(length)]


def place(step, at, job):
    for s in range(at[-1] + 1):
        count = at.count(s)
        if count:

            @pl.when(step == s)
            def _():
                for _ in range(count):
                    next(job)


def attention_body(step, tok, lanes, edges, shift_ref, start_ref, wq, wk, wv, bias_ref, qf_ref, kf_ref,
                   proj_ref, o_ref, f_ref, ka, va, qa, halo):
    half = halo.shape[1]
    ext = tok + 2 * half
    window = 2 * half + TQ
    columns = pl.ds(pl.multiple_of(step * PAIR, PAIR), PAIR)

    @pl.when(step == 0)
    def _():
        for side in range(2):
            for t in range(half // TQ):
                rows = slice(t * TQ, (t + 1) * TQ)
                moved = edges[side, rows, :].astype(jnp.float32) + shift_ref[0:1, :] + shift_ref[1:2, :]
                halo[side, rows, :] = moved.astype(jnp.bfloat16)
        ka[:, PAIR:] = kf_ref[...]
        va[:, PAIR:] = jnp.ones((ext, PAIR), jnp.bfloat16)
        f_ref[...] = qf_ref[half : half + tok, :]

    lane = lax.broadcasted_iota(jnp.int32, (TQ, PAIR), 1)
    left = lane < HD
    for t in range(ext // TQ):
        rows = slice(t * TQ, (t + 1) * TQ)
        if t * TQ < half:
            start = halo[0, rows, :]
        elif t * TQ < half + tok:
            start = start_ref[t * TQ - half : (t + 1) * TQ - half, :]
        else:
            start = halo[1, t * TQ - half - tok : (t + 1) * TQ - half - tok, :]
        q = (nn(start, wq[...]) + bias_ref[0:1, :]).astype(jnp.bfloat16)
        k = (nn(start, wk[...]) + bias_ref[1:2, :]).astype(jnp.bfloat16)
        v = (nn(start, wv[...]) + bias_ref[2:3, :]).astype(jnp.bfloat16)
        proj_ref[0, rows, :] = q
        proj_ref[1, rows, :] = k
        proj_ref[2, rows, :] = v
        ka[rows, :PAIR] = k
        va[rows, :PAIR] = v
        if half <= t * TQ < half + tok:
            own = t - half // TQ
            q = q * jnp.bfloat16(HD**-0.5)
            zero = jnp.zeros_like(q)
            qa[2 * own, :, :PAIR] = jnp.where(left, q, zero)
            qa[2 * own + 1, :, :PAIR] = jnp.where(left, zero, q)
            qa[2 * own, :, PAIR:] = qf_ref[rows, :]
            qa[2 * own + 1, :, PAIR:] = qf_ref[rows, :]
    for t in range(tok // TQ):
        win = slice(t * TQ, t * TQ + window)
        own = slice(t * TQ, (t + 1) * TQ)
        feat = f_ref[own, :]
        out = []
        for side in range(2):
            s = nt(qa[2 * t + side], ka[win, :])
            top = jnp.max(s, axis=1, keepdims=True)
            r = nn(jnp.exp(s - top).astype(jnp.bfloat16), va[win, :])
            total = r[:, PAIR:]
            out.append(r[:, :PAIR] / total)
            rest = top + jnp.log(total)
            for part in range(3):
                piece = rest.astype(jnp.bfloat16)
                rest = rest - piece.astype(jnp.float32)
                feat = jnp.where(lane == lanes + part * 16 + 2 * step + side, piece, feat)
        o_ref[own, columns] = jnp.where(left, out[0], out[1]).astype(jnp.bfloat16)
        f_ref[own, :] = feat


def fwd_kernel(tok, lanes, *refs):
    attention_body(pl.program_id(0), tok, lanes, *refs)


def fixed(*shape):
    return pl.BlockSpec(shape, lambda i: (0,) * len(shape), pipeline_mode=pl.Buffered(1))


def attention_specs(tok, ext, width):
    half, last = (ext - tok) // 2, width // PAIR - 1
    col = lambda base: pl.BlockSpec((width, PAIR), lambda i: (0, base * (last + 1) + lax.min(i, last)))
    ins = [fixed(2, half, width), fixed(8, width), fixed(tok, width), col(0), col(1), col(2),
           pl.BlockSpec((8, PAIR), lambda i: (0, lax.min(i, last))), fixed(ext, PAIR), fixed(ext, PAIR)]
    outs = [pl.BlockSpec((3, ext, PAIR), lambda i: (0, 0, lax.min(i, last))), fixed(tok, width), fixed(tok, PAIR)]
    shape, low = jax.ShapeDtypeStruct, jnp.bfloat16
    shapes = [shape((3, ext, width), low), shape((tok, width), low), shape((tok, PAIR), low)]
    scratch = [pltpu.VMEM((ext, 2 * PAIR), low), pltpu.VMEM((ext, 2 * PAIR), low),
               pltpu.VMEM((2 * tok // TQ, TQ, 2 * PAIR), low), pltpu.VMEM((2, half, width), low)]
    return ins, outs, shapes, scratch


def attn_fwd(edges, shift, start, inproj, bias, qf, kf, lanes):
    tok, width = start.shape
    ins, outs, shapes, scratch = attention_specs(tok, tok + 2 * (edges.shape[1] - 16), width)
    return pl.pallas_call(
        functools.partial(fwd_kernel, tok, lanes),
        grid=(width // PAIR,), in_specs=ins, out_specs=outs, out_shape=shapes, scratch_shapes=scratch,
        compiler_params=pltpu.CompilerParams(vmem_limit_bytes=56 << 20, dimension_semantics=("arbitrary",)),
        name="attention",
    )(edges, shift, start, inproj, inproj, inproj, bias, qf, kf)


def bwd_kernel(plan, count, counts, tok, lanes, *refs):
    grads, refs = refs[:count], refs[count:]
    edges, values, refs = refs[0], refs[1], refs[2:]
    q_ref, k_ref, v_ref, d_ref, qf_ref, own_ref, kf_ref, vf_ref, refs = *refs[:8], refs[8:]
    outs, refs = refs[:count], refs[count:]
    result, gq_ref, gkv_ref, refs = *refs[:3], refs[3:]
    one, two, feats, halo, refs = *refs[:4], refs[4:]
    step = pl.program_id(0)
    ext = k_ref.shape[1]
    half = (ext - tok) // 2
    window = 2 * half + TQ
    pairs = BWD_STEPS // 2
    pair = lax.rem(step, pairs)
    if count:
        send_sem, recv_sem, local_sem, sums, refs = *refs[:4], refs[4:]
        pos = Place()

        @pl.when(step == 0)
        def _():
            meet(pos, True)

        sends = Sends(send_sem, recv_sem, pos.to)

        at = spread(0, BWD_STEPS - 1, len(plan) + 4)
        ready = max(i for i, s in enumerate(at) if s <= pairs)

        def work():
            neighbour = halo_plan(pos, edges, halo, sends, local_sem, len(plan))
            total = total_plan(values, result, sums, sends)
            next(neighbour)
            for i, _ in enumerate(scatter_job(pos, plan, counts, grads, outs, refs, sends, local_sem)):
                if i < 6:
                    next(total)
                if i == ready:
                    next(neighbour)
                yield

        place(step, at, work())
    else:

        @pl.when(step == 0)
        def _():
            halo[...] = edges[...]
            result[...] = values[...]

    lane = lax.broadcasted_iota(jnp.int32, (TQ, PAIR), 1)
    left = lane < HD

    @pl.when(step == 0)
    def _():
        one[2, :, PAIR:] = kf_ref[...]
        two[2, :, PAIR:] = vf_ref[...]
        feats[half : half + tok, :] = own_ref[...]

    @pl.when(step == pairs)
    def _():
        for t in range(half // TQ):
            for side, base in ((0, 0), (1, half + tok)):
                rows = slice(base + t * TQ, base + (t + 1) * TQ)
                got = halo[side, t * TQ : (t + 1) * TQ, PAIR * pairs :]
                feats[rows, :] = jnp.where(lane < lanes, qf_ref[rows, :], got)

    def sides(tile, rows, d):
        q = q_ref[0, rows, :] * jnp.bfloat16(HD**-0.5)
        feat = feats[rows, :]
        zero = jnp.zeros_like(q)
        for side in range(2):
            mine = left if side == 0 else ~left
            kept = jnp.where((lane < lanes) | (lax.rem(lane - lanes + 128, 16) == 2 * pair + side), feat, zero)
            one[side, rows, :PAIR] = jnp.where(mine, q, zero)
            one[side, rows, PAIR:] = kept
            two[side, rows, :PAIR] = jnp.where(mine, d, zero)
            two[side, rows, PAIR:] = kept

    one[2, :, :PAIR] = k_ref[0]
    two[2, :, :PAIR] = v_ref[0]
    for t in range(tok // TQ):
        sides(t, slice(half + t * TQ, half + (t + 1) * TQ), d_ref[t * TQ : (t + 1) * TQ, :])

    @pl.when(step < pairs)
    def _():
        for t in range(tok // TQ):
            win = slice(t * TQ, t * TQ + window)
            rows = slice(half + t * TQ, half + (t + 1) * TQ)
            parts = []
            for side in range(2):
                p = jnp.exp(nt(one[side, rows, :], one[2, win, :]))
                g = (p * nt(two[side, rows, :], two[2, win, :])).astype(jnp.bfloat16)
                parts.append(nn(g, k_ref[0, win, :]))
            gq_ref[t * TQ : (t + 1) * TQ, :] = (jnp.where(left, *parts) * HD**-0.5).astype(jnp.bfloat16)

    @pl.when(step >= pairs)
    def _():
        at = pl.ds(pl.multiple_of(pair * PAIR, PAIR), PAIR)
        for t in range(half // TQ):
            for side, base in ((0, 0), (1, half + tok)):
                sides(t, slice(base + t * TQ, base + (t + 1) * TQ), halo[side, t * TQ : (t + 1) * TQ, at])
        for t in range(tok // TQ):
            win = slice(t * TQ, t * TQ + window)
            rows = slice(half + t * TQ, half + (t + 1) * TQ)
            dk, dv = 0.0, 0.0
            for side in range(2):
                p = jnp.exp(nt(one[2, rows, :], one[side, win, :]))
                g = (p * nt(two[2, rows, :], two[side, win, :])).astype(jnp.bfloat16)
                dk = dk + nn(g, one[side, win, :PAIR])
                dv = dv + nn(p.astype(jnp.bfloat16), two[side, win, :PAIR])
            gkv_ref[0, t * TQ : (t + 1) * TQ, :] = dk.astype(jnp.bfloat16)
            gkv_ref[1, t * TQ : (t + 1) * TQ, :] = dv.astype(jnp.bfloat16)


BWD_STEPS = 16


def attn_bwd(proj, packed, qf, kf, vf, lanes, tok, edges, values, grads=(), parts=(), share=0.0, collective=None):
    _, ext, width = proj.shape
    pairs = width // PAIR
    half = (ext - tok) // 2
    grads, plan, counts, bufs, shapes = scatter_layout(grads, parts, share)
    count = len(grads)
    anywhere, vmem = pl.BlockSpec(memory_space=pl.ANY), pl.BlockSpec(memory_space=pltpu.VMEM)
    third = lambda k: pl.BlockSpec((1, ext, PAIR), lambda i: (k, 0, lax.rem(i, pairs)))
    fix = lambda rows: pl.BlockSpec((rows, PAIR), lambda i: (0, 0))
    comm = dict(collective_id=collective, has_side_effects=True) if count else {}
    scratch = [
        pltpu.VMEM((3, ext, 2 * PAIR), jnp.bfloat16),
        pltpu.VMEM((3, ext, 2 * PAIR), jnp.bfloat16),
        pltpu.VMEM((ext, PAIR), jnp.bfloat16),
        pltpu.VMEM((2, half, width + PAIR), jnp.bfloat16),
    ]
    if count:
        scratch += semaphores(len(plan) * SENDS + 7, len(plan) + 1) + [pltpu.VMEM((10, 8, 128), jnp.float32)] + bufs
    return pl.pallas_call(
        functools.partial(bwd_kernel, plan, count, counts, tok, lanes),
        grid=(2 * pairs,),
        in_specs=[anywhere] * count
        + [anywhere if count else vmem, vmem, third(0), third(1), third(2),
           pl.BlockSpec((tok, PAIR), lambda i: (0, lax.rem(i, pairs))), fix(ext),
           pl.BlockSpec((tok, PAIR), lambda i: (0, pairs)), fix(ext), fix(ext)],
        out_specs=[vmem] * count
        + [vmem, pl.BlockSpec((tok, PAIR), lambda i: (0, lax.min(i, pairs - 1))),
           pl.BlockSpec((2, tok, PAIR), lambda i: (0, 0, lax.max(i - pairs, 0)))],
        out_shape=shapes
        + [jax.ShapeDtypeStruct(values.shape, jnp.float32), jax.ShapeDtypeStruct((tok, width), jnp.bfloat16),
           jax.ShapeDtypeStruct((2, tok, width), jnp.bfloat16)],
        scratch_shapes=scratch,
        compiler_params=pltpu.CompilerParams(
            vmem_limit_bytes=62 << 20, dimension_semantics=("arbitrary",), **comm
        ),
        name="attention_gradients",
    )(*grads, edges, values, proj, proj, proj, packed, qf, packed, kf, vf)


def features(item, places, keep, n_items):
    ext = item.shape[0]
    nb = (n_items + 1).bit_length()
    pb = (ext - 1).bit_length()
    lanes = 2 * (nb + pb)
    assert lanes + 80 <= PAIR and ext == 1 << pb
    lane = jnp.arange(PAIR, dtype=jnp.int32)
    of_item = lane < 2 * nb
    shift = jnp.where(of_item, lane % nb, (lane - 2 * nb) % pb)
    turned = jnp.where(of_item, lane // nb, (lane - 2 * nb) // pb)
    bit = ((jnp.where(of_item, (item + 1)[:, None], places[:, None]) >> shift) ^ turned) & 1
    used = lane < lanes
    active = of_item == keep[:, None]
    qf = jnp.where(used, bit, 0)
    kf = jnp.where(used, jnp.where(active & (bit == 0), NEG, 0.0), jnp.where(lane < lanes + 48, -1.0, 0.0))
    return qf.astype(jnp.bfloat16), kf.astype(jnp.bfloat16), lanes


def delta_key(ext, lanes):
    lane = jnp.arange(PAIR)
    vf = jnp.where((lane >= lanes + 48) & (lane < lanes + 80), -1.0, 0.0)
    return jnp.broadcast_to(vf[None], (ext, PAIR)).astype(jnp.bfloat16)


MESH = pl.DeviceIdType.MESH


class Place:
    def __init__(self):
        seq, blk = lax.axis_index("seq"), lax.axis_index("blk")
        self.seq, self.blk, self.last = seq, blk, lax.axis_size("blk") - 1
        self.x, self.c, self.z, self.y = x, c, z, y = seq // 2, lax.rem(seq, 2), blk // 2, lax.rem(blk, 2)
        self.nx, self.nc, self.ny = nx, nc, ny = 1 - x, 1 - c, 1 - y
        low_bit, high_bit = lax.rem(z, 2), z // 2
        flips = {1: (1 - low_bit, high_bit), 2: (low_bit, 1 - high_bit), 3: (1 - low_bit, 1 - high_bit)}
        self.nz = {k: high * 2 + bit for k, (bit, high) in flips.items()}
        device = lambda x, c, z, y: (x * 2 + c, z * 2 + y)
        self.to = {"x": device(nx, c, z, y), "y": device(x, c, z, ny), "c": device(x, nc, z, y)}
        for k in (1, 2, 3):
            self.to[k] = device(x, c, self.nz[k], y)
        self.below = (seq, lax.max(blk - 1, 0))
        self.above = (seq, lax.min(blk + 1, self.last))


class Copy:
    def __init__(self, make):
        self.make = make

    def start(self):
        self.make().start()
        return self

    def wait(self):
        self.make().wait()

    def wait_send(self):
        self.make().wait_send()

    def wait_recv(self):
        self.make().wait_recv()


def local_copy(src, dst, sems, at):
    return Copy(lambda: pltpu.make_async_copy(src(), dst(), sems.at[at])).start()


class Sends:
    def __init__(self, send_sem, recv_sem, to):
        self.send_sem, self.recv_sem, self.to, self.used, self.live = send_sem, recv_sem, to, 0, []

    def describe(self, src, dst, device):
        at = self.used
        self.used += 1
        return Copy(
            lambda: pltpu.make_async_remote_copy(
                src_ref=src(), dst_ref=dst(), send_sem=self.send_sem.at[at], recv_sem=self.recv_sem.at[at],
                device_id=device, device_id_type=MESH,
            )
        )

    def start(self, src, dst, partner):
        copy = self.describe(src, dst, self.to[partner]).start()
        self.live.append(copy)
        return copy

    def finish(self):
        for copy in self.live:
            copy.wait_send()


def gather_plan(pos, shard, full, sends, local, number, base, wide, at):
    x, c, z, y, nx, nc, ny = pos.x, pos.c, pos.z, pos.y, pos.nx, pos.nc, pos.ny
    every, one, two = pl.ds(base, wide), pl.ds(base, at), pl.ds(base + at, wide - at)

    def send(partner, *index):
        return sends.start(lambda: full.at[index], lambda: full.at[index], partner)

    rows = slice(None)
    source, target = lambda: shard.at[:, every], lambda: full.at[x, c, z, y, :, every]
    own = local_copy(source, target, local, number)
    line = [sends.start(source, target, k) for k in (1, 2, 3)]
    yield
    own.wait()
    for copy in line:
        copy.wait_recv()
    if at:
        a = send("x", x, c, rows, y, rows, one)
    b = send("y", x, c, rows, y, rows, two)
    core = [send("c", x, c, rows, y, rows, every)]
    yield
    if at:
        a.wait_recv()
        a2 = send("y", rows, c, rows, y, rows, one)
        core.append(send("c", nx, c, rows, y, rows, one))
    b.wait_recv()
    b2 = send("x", x, c, rows, rows, rows, two)
    core.append(send("c", x, c, rows, ny, rows, two))
    yield
    if at:
        a2.wait_recv()
        core.append(send("c", rows, c, rows, ny, rows, one))
    b2.wait_recv()
    core.append(send("c", nx, c, rows, rows, rows, two))
    yield
    for copy in core:
        copy.wait_recv()
    yield


SENDS = 12


def turns(plans, last, begin=None):
    begin = begin or list(range(len(plans)))
    for turn in range(begin[-1] + 5):
        for k in reversed(range(len(plans))):
            if 0 <= turn - begin[k] <= 4:
                next(plans[k])
        if turn == begin[-1] + 4:
            last()
        yield


def pieces(widths, parts, share):
    plan = []
    for k, (whole, count) in enumerate(zip(widths, parts)):
        wide = whole // count
        plan += [(k, p * wide, wide, int(wide * share) // 128 * 128) for p in range(count)]
    return plan


def halo_plan(pos, edges, halo, sends, local, number):
    blk, last = pos.blk, pos.last
    down = sends.describe(lambda: edges.at[0], lambda: halo.at[1], pos.below)
    up = sends.describe(lambda: edges.at[1], lambda: halo.at[0], pos.above)
    fill = [
        Copy(lambda k=k: pltpu.make_async_copy(edges.at[k], halo.at[k], local.at[number])) for k in (0, 1)
    ]

    def where(test, *acts):
        @pl.when(test)
        def _():
            for act in acts:
                act()

    where(blk > 0, down.start)
    where(blk < last, up.start)
    where(blk == 0, fill[0].start)
    where(blk == last, fill[1].start)
    yield
    where(blk > 0, down.wait_send, up.wait_recv)
    where(blk < last, up.wait_send, down.wait_recv)
    where(blk == 0, fill[0].wait)
    where(blk == last, fill[1].wait)
    yield


def meet(pos, halo):
    barrier = pltpu.get_barrier_semaphore()
    for device in pos.to.values():
        pl.semaphore_signal(barrier, inc=1, device_id=device, device_id_type=MESH)
    count = len(pos.to)
    if halo:

        @pl.when(pos.blk > 0)
        def _():
            pl.semaphore_signal(barrier, inc=1, device_id=pos.below, device_id_type=MESH)

        @pl.when(pos.blk < pos.last)
        def _():
            pl.semaphore_signal(barrier, inc=1, device_id=pos.above, device_id_type=MESH)

        count = count + 2 - jnp.where(pos.blk == 0, 1, 0) - jnp.where(pos.blk == pos.last, 1, 0)
    pl.semaphore_wait(barrier, count)


def gather_job(pos, plan, shards, fulls, sends, local):
    yield from turns([
        gather_plan(pos, shards[k], fulls[k], sends, local, i, base, wide, at) for i, (k, base, wide, at) in enumerate(plan)
    ], sends.finish)


def gather_kernel(plan, count, *refs):
    shards, edges, fulls, halo = refs[:count], refs[count], refs[count + 1 : 2 * count + 1], refs[2 * count + 1]
    send_sem, recv_sem, local_sem = refs[2 * count + 2 :]
    pos = Place()
    meet(pos, True)
    sends = Sends(send_sem, recv_sem, pos.to)
    neighbour = halo_plan(pos, edges, halo, sends, local_sem, len(plan))
    next(neighbour)
    for _ in gather_job(pos, plan, shards, fulls, sends, local_sem):
        pass
    next(neighbour)


def semaphores(number, local):
    return [pltpu.SemaphoreType.DMA((number,)), pltpu.SemaphoreType.DMA((number,)), pltpu.SemaphoreType.DMA((local,))]


def full_shapes(shards):
    return [jax.ShapeDtypeStruct((2, 2, 4, 2) + v.shape, jnp.bfloat16) for v in shards]


def gather_all(shards, parts, share, edges, collective):
    count = len(shards)
    plan = pieces([v.shape[1] for v in shards], parts, share)
    anywhere = pl.BlockSpec(memory_space=pl.ANY)
    return pl.pallas_call(
        functools.partial(gather_kernel, plan, count),
        in_specs=[anywhere] * (count + 1),
        out_specs=[anywhere] * (count + 1),
        out_shape=full_shapes(shards) + [jax.ShapeDtypeStruct(edges.shape, edges.dtype)],
        scratch_shapes=semaphores(len(plan) * SENDS + 2, len(plan) + 1),
        compiler_params=pltpu.CompilerParams(collective_id=collective, has_side_effects=True),
        name="gather_weights",
    )(*shards, edges)


def widen(value):
    return value.astype(jnp.float32)


def scatter_plan(pos, grad, out, bufs, sends, local, number, base, wide, at, held=False):
    x, c, z, y, nx, nc, ny = pos.x, pos.c, pos.z, pos.y, pos.nx, pos.nc, pos.ny
    every, one, two = pl.ds(base, wide), pl.ds(0, at), pl.ds(at, wide - at)
    if held:
        own, bufs = lambda: grad.at[:, c, :, :, :, every], (None,) + tuple(bufs)
    else:
        own = lambda: bufs[0]
    got, one1, two1, one2, two2, line, ends = bufs[1:] if at else bufs[1:2] + (None,) + bufs[2:3] + (None,) + bufs[3:]
    if not held:
        load = local_copy(lambda: grad.at[:, c, :, :, :, every], own, local, number)
    cross = sends.start(lambda: grad.at[:, nc, :, :, :, every], lambda: got, "c")
    yield
    if not held:
        load.wait()
    cross.wait_recv()

    @pl.loop(0, 8)
    def _(i):
        mine = own().at[i // 4, lax.rem(i, 4)]
        mine[...] = mine[...] + got[i // 4, lax.rem(i, 4)]

    if at:
        a = sends.start(lambda: own().at[:, :, ny, :, one], lambda: one1, "y")
    b = sends.start(lambda: own().at[nx, :, :, :, two], lambda: two1, "x")
    yield
    if at:
        a.wait_recv()

        @pl.loop(0, 8)
        def _(i):
            one1[i // 4, lax.rem(i, 4)] = own().at[i // 4, lax.rem(i, 4), y, :, one][...] + one1[i // 4, lax.rem(i, 4)]

        a2 = sends.start(lambda: one1.at[nx], lambda: one2, "x")
    b.wait_recv()

    @pl.loop(0, 4)
    def _(i):
        two1[i] = own().at[x, i, :, :, two][...] + two1[i]

    b2 = sends.start(lambda: two1.at[:, ny], lambda: two2, "y")
    yield
    if at:
        a2.wait_recv()
    b2.wait_recv()

    @pl.loop(0, 4)
    def _(i):
        if at:
            line[i, :, :at] = one1[x, i] + one2[i]
        line[i, :, at:] = two1[i, y] + two2[i]

    last = [
        sends.start(lambda k=k: line.at[pos.nz[k]], lambda k=k: ends.at[k - 1], k) for k in (1, 2, 3)
    ]
    yield
    for copy in last:
        copy.wait_recv()
    out[:, base : base + wide] = widen(line[z]) + widen(ends[0]) + widen(ends[1]) + widen(ends[2])
    yield


def scatter_bufs(rows, wide, at, held=False):
    shapes = [(2, 4, 2, rows, wide)] * (1 if held else 2)
    if at:
        shapes += [(2, 4, rows, at), (4, 2, rows, wide - at), (4, rows, at)]
    else:
        shapes += [(4, 2, rows, wide)]
    shapes += [(4, rows, wide - at), (4, rows, wide), (3, rows, wide)]
    return [pltpu.VMEM(s, jnp.bfloat16) for s in shapes]


def total_plan(values, result, bufs, sends):
    partners = ("c", "x", "y", 1, 2)
    for i, partner in enumerate(partners):
        source = (lambda i=i: bufs.at[2 * i - 1]) if i else (lambda: values)
        copy = sends.start(source, lambda i=i: bufs.at[2 * i], partner)
        yield
        copy.wait_recv()
        total = source()[...] + bufs[2 * i]
        if i + 1 < len(partners):
            bufs[2 * i + 1] = total
        else:
            result[...] = total
    yield


def scatter_job(pos, plan, counts, grads, outs, bufs, sends, local, held=False, begin=None):
    plans = []
    for i, (k, base, wide, at) in enumerate(plan):
        first = sum(counts[:i])
        mine = bufs[first : first + counts[i]]
        plans.append(scatter_plan(pos, grads[k], outs[k], mine, sends, local, i, base, wide, at, held))
    yield from turns(plans, sends.finish, begin)


def scatter_layout(grads, parts, share):
    grads = [v.reshape(2, 2, 4, 2, v.shape[0] // 32, v.shape[1]) for v in grads]
    plan = pieces([v.shape[-1] for v in grads], parts, share)
    bufs = [scatter_bufs(grads[k].shape[-2], wide, at) for k, base, wide, at in plan]
    shapes = [jax.ShapeDtypeStruct(v.shape[-2:], jnp.float32) for v in grads]
    return grads, plan, [len(b) for b in bufs], sum(bufs, []), shapes


def scatter_kernel(plan, count, counts, *refs):
    grads, outs, refs = refs[:count], refs[count : 2 * count], refs[2 * count :]
    send_sem, recv_sem, local_sem = refs[:3]
    pos = Place()
    meet(pos, False)
    sends = Sends(send_sem, recv_sem, pos.to)
    for _ in scatter_job(pos, plan, counts, grads, outs, refs[3:], sends, local_sem):
        pass


def scatter_all(grads, parts, share, collective):
    count = len(grads)
    grads, plan, counts, bufs, shapes = scatter_layout(grads, parts, share)
    anywhere, vmem = pl.BlockSpec(memory_space=pl.ANY), pl.BlockSpec(memory_space=pltpu.VMEM)
    return pl.pallas_call(
        functools.partial(scatter_kernel, plan, count, counts),
        in_specs=[anywhere] * count,
        out_specs=[vmem] * count,
        out_shape=shapes,
        scratch_shapes=semaphores(len(plan) * SENDS, len(plan)) + bufs,
        compiler_params=pltpu.CompilerParams(
            collective_id=collective, has_side_effects=True, vmem_limit_bytes=58 << 20
        ),
        name="sum_gradients",
    )(*grads)


FT = 512
ROWS = 256


def normalize(values):
    centered = values - jnp.mean(values, axis=1, keepdims=True)
    inv = lax.rsqrt(jnp.mean(centered * centered, axis=1, keepdims=True) + 1e-05)
    return centered * inv, inv


def normalize_back(grad, normal, inv):
    return inv * (
        grad - jnp.mean(grad, axis=1, keepdims=True) - normal * jnp.mean(grad * normal, axis=1, keepdims=True)
    )


def column_sum(values):
    return jnp.sum(values, axis=0, keepdims=True)


def ffn_body(step, ups, whole_weight, up_weight, att, inp, wo, vec, ub, cot, hid, slope, normal_ref, inv_ref, low_ref,
             out_ref, grad_ref, grad_low_ref, sums, keep, wd, low):
    tok = att.shape[0]

    @pl.when(step == 0)
    def _():
        sums[...] = jnp.zeros_like(sums)
        for r in range(tok // ROWS):
            rows = slice(r * ROWS, (r + 1) * ROWS)
            branch = nn(att[rows, :], wo().reshape(-1, att.shape[1])) + vec[2:3, :]
            start = inp[rows, :].astype(jnp.float32) + vec[0:1, :] + vec[1:2, :]
            normal, inv = normalize(start + branch)
            normal_ref[rows, :] = normal
            inv_ref[rows, :] = jnp.broadcast_to(inv, (ROWS, 128))
            first = (normal * vec[3:4, :] + vec[4:5, :]).astype(jnp.bfloat16)
            low[rows, :] = first
            low_ref[:, rows] = first.T
            sums[3:4, :] += column_sum(start * start)
            sums[4:5, :] += column_sum(branch * branch)

    @pl.when((step >= 0) & (step < ups))
    def _():
        at = pl.ds(pl.multiple_of(step * FT, FT), FT)
        for r in range(tok // ROWS):
            rows = slice(r * ROWS, (r + 1) * ROWS)
            up = nn(low[rows, :], up_weight()) + ub[0:1, at]
            phi = 0.5 * (1.0 + lax.erf(up * 2.0**-0.5))
            h = (up * phi).astype(jnp.bfloat16)
            hid[:, rows] = h.T
            keep[rows, at] = h
            slope[rows, :] = (phi + up * (jnp.exp(-0.5 * up * up) * 0.3989422804014327)).astype(jnp.bfloat16)

    @pl.when(step == ups)
    def _():
        whole_weight()

    @pl.when(step >= ups)
    def _():
        rows = pl.ds(pl.multiple_of((step - ups) * ROWS, ROWS), ROWS)
        weight = wd[...].reshape(-1, wd.shape[-1])
        branch = nn(keep[rows, :], weight) + vec[5:6, :]
        first = normal_ref[rows, :] * vec[3:4, :] + vec[4:5, :]
        normal, inv = normalize(first + branch)
        out_ref[...] = (normal * vec[6:7, :] + vec[7:8, :]).astype(jnp.bfloat16)
        g = cot[...].astype(jnp.float32)
        grad = normalize_back(g * vec[6:7, :], normal, inv)
        grad_ref[...] = grad
        low_grad = grad.astype(jnp.bfloat16)
        grad_low_ref[...] = low_grad
        sums[0:1, :] += column_sum(g * normal)
        sums[1:2, :] += column_sum(g)
        sums[2:3, :] += column_sum(low_grad.astype(jnp.float32))
        sums[5:6, :] += column_sum(branch * branch)


def ffn_specs(tok, width, wide, wd_shape, begin):
    ups = wide // FT
    f32, low, shape = jnp.float32, jnp.bfloat16, jax.ShapeDtypeStruct
    now = lambda i: lax.max(lax.min(i - begin, ups - 1), 0)
    row = pl.BlockSpec((ROWS, width), lambda i: (lax.max(i - begin - ups, 0), 0))
    ins = [fixed(8, width), fixed(8, wide), row]
    outs = [pl.BlockSpec((FT, tok), lambda i: (now(i), 0)), pl.BlockSpec((tok, FT), lambda i: (0, now(i))),
            fixed(tok, width), fixed(tok, 128), fixed(width, tok), row, row, row, fixed(8, width)]
    shapes = [shape((wide, tok), low), shape((tok, wide), low), shape((tok, width), f32), shape((tok, 128), f32),
              shape((width, tok), low), shape((tok, width), low), shape((tok, width), f32), shape((tok, width), low),
              shape((8, width), f32)]
    scratch = [pltpu.VMEM((tok, wide), low), pltpu.VMEM(wd_shape, low), pltpu.VMEM((tok, width), low)]
    return ins, outs, shapes, scratch


def ffn_kernel(ups, *refs):
    down, att, inp, wo, wu, refs = *refs[:5], refs[5:]
    load, wd = refs[-1], refs[-3]

    def whole_weight():
        copy = pltpu.make_async_copy(down, wd, load)
        copy.start()
        copy.wait()

    ffn_body(pl.program_id(0), ups, whole_weight, lambda: wu[...], att, inp, lambda: wo[...], *refs[:-1])


def ffn_forward(down, att, inp, wo, wu, vec, ub, cot):
    tok, width = att.shape
    wide = wu.shape[1]
    ups = wide // FT
    ins, outs, shapes, scratch = ffn_specs(tok, width, wide, down.shape, 0)
    return pl.pallas_call(
        functools.partial(ffn_kernel, ups),
        grid=(ups + tok // ROWS,),
        in_specs=[pl.BlockSpec(memory_space=pl.ANY), fixed(tok, width), fixed(tok, width), fixed(width, width),
                  pl.BlockSpec((width, FT), lambda i: (0, lax.min(i, ups - 1)))] + ins,
        out_specs=outs, out_shape=shapes, scratch_shapes=scratch + [pltpu.SemaphoreType.DMA],
        compiler_params=pltpu.CompilerParams(vmem_limit_bytes=62 << 20, dimension_semantics=("arbitrary",)),
        name="feed_forward",
    )(down, att, inp, wo, wu, vec, ub, cot)


def layer_kernel(plan, at, ups, tok, lanes, *refs):
    shards, refs = refs[:3], refs[3:]
    attention_in, refs = refs[:9], refs[9:]
    inp, ffn_in, refs = refs[0], refs[1:4], refs[4:]
    fulls, refs = refs[:3], refs[3:]
    attention_out, ffn_out, refs = refs[:3], refs[3:12], refs[12:]
    attention_scratch, ffn_scratch, refs = refs[:4], refs[4:7], refs[7:]
    wo, wu, load, send_sem, recv_sem, local_sem = refs
    step = pl.program_id(0)
    begin = attention_out[1].shape[1] // PAIR
    pos = Place()

    @pl.when(step == 0)
    def _():
        meet(pos, False)

    sends = Sends(send_sem, recv_sem, pos.to)
    place(step, at, gather_job(pos, plan, shards, fulls, sends, local_sem))

    @pl.when(step < begin)
    def _():
        attention_body(step, tok, lanes, *attention_in, *attention_out, *attention_scratch)

    turn = step - begin
    wo_load = Copy(lambda: pltpu.make_async_copy(fulls[0], wo, load.at[2]))
    wd_load = Copy(lambda: pltpu.make_async_copy(fulls[2], ffn_scratch[1], load.at[2]))

    def wu_load(k):
        slot = lax.rem(k, 2)
        columns = pl.ds(pl.multiple_of(k * FT, FT), FT)
        return pltpu.make_async_copy(fulls[1].at[:, :, :, :, :, columns], wu.at[slot], load.at[slot])

    @pl.when(turn == 0)
    def _():
        wo_load.start()
        wu_load(0).start()
        wo_load.wait()

    @pl.when((turn >= 0) & (turn < ups - 1))
    def _():
        wu_load(turn + 1).start()

    @pl.when((turn >= 0) & (turn < ups))
    def _():
        wu_load(turn).wait()

    def whole_weight():
        wd_load.start()
        wd_load.wait()

    ffn_body(turn, ups, whole_weight, lambda: wu[lax.rem(turn, 2)].reshape(-1, FT), attention_out[1], inp,
             lambda: wo[...], *ffn_in, *ffn_out, *ffn_scratch)


def layer_forward(shards, plan, at, edges, shift, start, inproj, bias, qf, kf, lanes, inp, vec, ub, cot, collective):
    tok, width = start.shape
    wide = ub.shape[1]
    ups, begin = wide // FT, width // PAIR
    low = jnp.bfloat16
    ins, outs, shapes, scratch = attention_specs(tok, tok + 2 * (edges.shape[1] - 16), width)
    ffn_ins, ffn_outs, ffn_shapes, ffn_scratch = ffn_specs(tok, width, wide, (2, 2, 4, 2) + shards[2].shape, begin)
    anywhere = pl.BlockSpec(memory_space=pl.ANY)
    rows = shards[0].shape[0]
    return pl.pallas_call(
        functools.partial(layer_kernel, plan, at, ups, tok, lanes),
        grid=(begin + ups + tok // ROWS,),
        in_specs=[anywhere] * 3 + ins + [fixed(tok, width)] + ffn_ins,
        out_specs=[anywhere] * 3 + outs + ffn_outs,
        out_shape=full_shapes(shards) + shapes + ffn_shapes,
        scratch_shapes=scratch + ffn_scratch
        + [pltpu.VMEM((2, 2, 4, 2, rows, width), low), pltpu.VMEM((2, 2, 2, 4, 2, rows, FT), low),
           pltpu.SemaphoreType.DMA((3,))] + semaphores(len(plan) * SENDS, len(plan)),
        compiler_params=pltpu.CompilerParams(
            vmem_limit_bytes=63 << 20, dimension_semantics=("arbitrary",), collective_id=collective, has_side_effects=True
        ),
        name="layer_forward",
    )(*shards, edges, shift, start, inproj, inproj, inproj, bias, qf, kf, inp, vec, ub, cot)


def tn(a, b):
    return lax.dot_general(a, b, (((0,), (0,)), ((), ())), preferred_element_type=jnp.float32)


def back_kernel(plan, count, counts, ups, lanes, *refs):
    hid, gffn, wd, slope, wu, first_low, gsecond, normal_ref, inv_ref, vec, att, wo, feat_ref = refs[:13]
    down, up_grad, out_grad, up_sum, sums, gin_ref, packed, acc, piece, low_grad = refs[13:23]
    refs = refs[23:]
    step = pl.program_id(0)
    tok, width = gffn.shape
    last = 2 * ups + tok // ROWS - 1
    if count:
        dwd, send_sem, recv_sem, local_sem, bufs = *refs[:4], refs[4:]
        pos = Place()

        @pl.when(step == ups)
        def _():
            meet(pos, False)

        sends = Sends(send_sem, recv_sem, pos.to)
        job = scatter_job(pos, plan, counts, [dwd], [down], bufs, sends, local_sem, True)
        place(step, spread(ups, last, len(plan) + 4), job)

    @pl.when(step < ups)
    def _():
        grad = nn(hid[...], gffn[...]).astype(jnp.bfloat16)
        if count:
            each = dwd.shape[4]
            for k in range(FT // each):
                at = step * (FT // each) + k
                dwd[at // 16, lax.rem(at // 8, 2), lax.rem(at // 2, 4), lax.rem(at, 2)] = grad[k * each : (k + 1) * each]
        else:
            down[pl.ds(pl.multiple_of(step * FT, FT), FT), :] = grad

    @pl.when((step >= ups) & (step < 2 * ups))
    def _():
        total = jnp.zeros((1, FT), jnp.float32)
        for r in range(tok // ROWS):
            rows = slice(r * ROWS, (r + 1) * ROWS)
            g = (nt(gffn[rows, :], wd[...]) * slope[rows, :].astype(jnp.float32)).astype(jnp.bfloat16)
            piece[rows, :] = g
            total += column_sum(g.astype(jnp.float32))
            more = nt(g, wu[...])

            @pl.when(step == ups)
            def _():
                acc[rows, :] = more

            @pl.when(step > ups)
            def _():
                acc[rows, :] += more

        up_sum[...] = jnp.broadcast_to(total, (8, FT))
        up_grad[...] = nn(first_low[...], piece[...]).astype(jnp.bfloat16)

    @pl.when(step == 2 * ups)
    def _():
        sums[...] = jnp.zeros_like(sums)

    @pl.when(step >= 2 * ups)
    def _():
        rows = pl.ds(pl.multiple_of((step - 2 * ups) * ROWS, ROWS), ROWS)
        g = gsecond[...] + acc[rows, :]
        normal = normal_ref[...]
        grad = normalize_back(g * vec[3:4, :], normal, inv_ref[:, :1])
        gin_ref[...] = grad
        low = grad.astype(jnp.bfloat16)
        low_grad[rows, :] = low
        sums[0:1, :] += column_sum(g * normal)
        sums[1:2, :] += column_sum(g)
        sums[2:3, :] += column_sum(low.astype(jnp.float32))
        gatt = nt(low, wo[...]).astype(jnp.bfloat16)
        packed[:, :width] = gatt
        both = gatt.astype(jnp.float32) * att[rows, :].astype(jnp.float32)
        lane = lax.broadcasted_iota(jnp.int32, (width, PAIR), 1)
        head = lax.broadcasted_iota(jnp.int32, (width, PAIR), 0) // HD
        pick = (lane >= lanes + 48) & (lane < lanes + 80) & (lax.rem(lane - lanes + 128, 16) == head)
        pick = jnp.where(pick, 1.0, 0.0).astype(jnp.bfloat16)
        high = both.astype(jnp.bfloat16)
        delta = nn(high, pick) + nn((both - high.astype(jnp.float32)).astype(jnp.bfloat16), pick)
        first = delta.astype(jnp.bfloat16)
        second = (delta - first.astype(jnp.float32)).astype(jnp.bfloat16)
        lane = lax.broadcasted_iota(jnp.int32, (ROWS, PAIR), 1)
        feat = feat_ref[...]
        feat = jnp.where((lane >= lanes + 48) & (lane < lanes + 64), first, feat)
        packed[:, width:] = jnp.where((lane >= lanes + 64) & (lane < lanes + 80), second, feat)

    @pl.when(step == last)
    def _():
        for k in range(2):
            cols = slice(k * width // 2, (k + 1) * width // 2)
            out_grad[cols, :] = tn(att[:, cols], low_grad[...]).astype(jnp.bfloat16)


def ffn_backward(hid, gffn, wd, slope, wu, first_low, gsecond, normal, inv, vec, att, wo, feat, lanes, parts=(), share=0.0,
                 collective=None):
    wide, tok = hid.shape
    width = gffn.shape[1]
    ups, downs = wide // FT, tok // ROWS
    count = 1 if parts else 0
    f32, low = jnp.float32, jnp.bfloat16
    shape = jax.ShapeDtypeStruct
    vmem = pl.BlockSpec(memory_space=pltpu.VMEM)
    whole = lambda r, c: pl.BlockSpec((r, c), lambda i: (0, 0), pipeline_mode=pl.Buffered(1))
    middle = lambda i: lax.max(lax.min(i - ups, ups - 1), 0)
    tile = pl.BlockSpec((tok, FT), lambda i: (0, middle(i)))
    row = lambda c: pl.BlockSpec((ROWS, c), lambda i: (lax.max(i - 2 * ups, 0), 0))
    scratch = [pltpu.VMEM((tok, width), f32), pltpu.VMEM((tok, FT), low), pltpu.VMEM((tok, width), low)]
    plan, counts, down, comm = [], [], shape((wide, width), low), {}
    if count:
        rows = wide // 32
        plan = pieces([width], parts, share)
        bufs = [scatter_bufs(rows, w, at, True) for _, _, w, at in plan]
        counts = [len(b) for b in bufs]
        scratch += [pltpu.VMEM((2, 2, 4, 2, rows, width), low)] + semaphores(len(plan) * SENDS, len(plan)) + sum(bufs, [])
        down, comm = shape((rows, width), f32), dict(collective_id=collective, has_side_effects=True)
    return pl.pallas_call(
        functools.partial(back_kernel, plan, count, counts, ups, lanes),
        grid=(2 * ups + downs,),
        in_specs=[pl.BlockSpec((FT, tok), lambda i: (lax.min(i, ups - 1), 0)), whole(tok, width),
                  pl.BlockSpec((FT, width), lambda i: (middle(i), 0)), tile,
                  pl.BlockSpec((width, FT), lambda i: (0, middle(i))), whole(width, tok), row(width), row(width), row(128),
                  whole(8, width), whole(tok, width), whole(width, width), row(PAIR)],
        out_specs=[vmem, pl.BlockSpec((width, FT), lambda i: (0, middle(i))), whole(width, width),
                   pl.BlockSpec((8, FT), lambda i: (0, middle(i))), whole(8, width), row(width), row(width + PAIR)],
        out_shape=[down, shape((width, wide), low), shape((width, width), low), shape((8, wide), f32),
                   shape((8, width), f32), shape((tok, width), f32), shape((tok, width + PAIR), low)],
        scratch_shapes=scratch,
        compiler_params=pltpu.CompilerParams(vmem_limit_bytes=62 << 20, dimension_semantics=("arbitrary",), **comm),
        name="feed_forward_gradients",
    )(hid, gffn, wd, slope, wu, first_low, gsecond, normal, inv, vec, att, wo, feat)


def tail_kernel(plan, counts, *refs):
    gq, gkv, start, wt, gin, near, far, other, out_ref, in_share, small_share, sums = refs[:12]
    held, held_small, send_sem, recv_sem, local_sem, bufs = *refs[12:17], refs[17:]
    step = pl.program_id(0)
    width = start.shape[1]
    pos = Place()

    @pl.when(step == 0)
    def _():
        meet(pos, False)
        sums[...] = jnp.zeros_like(sums)

    sends = Sends(send_sem, recv_sem, pos.to)
    last = 3 + gq.shape[0] // ROWS
    job = scatter_job(pos, plan, counts, [held, held_small], [in_share, small_share], bufs, sends, local_sem, True, [0, 1, 2, 2])

    def keep(k, grad):
        for half in range(2):
            cols = slice(half * width // 2, (half + 1) * width // 2)
            part = tn(start[...], grad[:, cols]).astype(jnp.bfloat16).reshape(held.shape[:5] + (width // 2,))
            held[:, :, :, :, :, k * width + half * width // 2 : k * width + (half + 1) * width // 2] = part

    @pl.when(step == last)
    def _():
        lines = [other[4:5, :] * sums[1:2, :], sums[1:2, :], sums[2:3, :], sums[3:4, :], near[2:3, :], near[0:1, :],
                 near[1:2, :], far[2:3, :], far[0:1, :], far[1:2, :]] + [other[k : k + 1, :] for k in range(4)]
        row = lax.broadcasted_iota(jnp.int32, (128, width), 0)
        total = jnp.zeros((128, width), jnp.float32)
        for k, line in enumerate(lines):
            total = jnp.where(row == k, line, total)
        held_small[...] = total.T.astype(jnp.bfloat16).reshape(held_small.shape)

    place(step, [1, 2] + [last] * 5, job)

    @pl.when(step == 0)
    def _():
        keep(0, gq)

    @pl.when(step == 1)
    def _():
        keep(1, gkv.at[0])

    @pl.when(step == last - 1)
    def _():
        keep(2, gkv.at[1])

    @pl.when((step >= 2) & (step < last - 1))
    def _():
        rows = pl.ds(pl.multiple_of((step - 2) * ROWS, ROWS), ROWS)
        q, k, v = gq[rows, :], gkv[0, rows, :], gkv[1, rows, :]
        total = gin[...] + nt(q, wt[:, :width]) + nt(k, wt[:, width : 2 * width]) + nt(v, wt[:, 2 * width :])
        out_ref[...] = total.astype(jnp.bfloat16)
        sums[1:2, :] += column_sum(total)
        sums[2:3, :] += column_sum(q.astype(jnp.float32))
        sums[3:4, :] += column_sum(v.astype(jnp.float32))


def input_gradients(gq, gkv, start, wt, gin, near, far, other, share, collective):
    tok, width = start.shape
    rows = width // 32
    plan = pieces([3 * width, 128], (3, 1), share)
    bufs = [scatter_bufs(rows, w, at, True) for _, _, w, at in plan]
    f32, low = jnp.float32, jnp.bfloat16
    shape = jax.ShapeDtypeStruct
    vmem = pl.BlockSpec(memory_space=pltpu.VMEM)
    row = pl.BlockSpec((ROWS, width), lambda i: (lax.max(lax.min(i - 2, tok // ROWS - 1), 0), 0))
    fix = lambda *s: pl.BlockSpec(s, lambda i: (0,) * len(s), pipeline_mode=pl.Buffered(1))
    return pl.pallas_call(
        functools.partial(tail_kernel, plan, [len(b) for b in bufs]),
        grid=(4 + tok // ROWS,),
        in_specs=[fix(tok, width), fix(2, tok, width), fix(tok, width), fix(width, 3 * width), row] + [fix(8, width)] * 3,
        out_specs=[row, vmem, vmem],
        out_shape=[shape((tok, width), low), shape((rows, 3 * width), f32), shape((rows, 128), f32)],
        scratch_shapes=[pltpu.VMEM((8, width), f32), pltpu.VMEM((2, 2, 4, 2, rows, 3 * width), low),
                        pltpu.VMEM((2, 2, 4, 2, rows, 128), low)]
        + semaphores(len(plan) * SENDS, len(plan)) + sum(bufs, []),
        compiler_params=pltpu.CompilerParams(
            vmem_limit_bytes=62 << 20, dimension_semantics=("arbitrary",), collective_id=collective, has_side_effects=True
        ),
        name="input_gradients",
    )(gq, gkv, start, wt, gin, near, far, other)


H = 16
MAXLEN = 512
TSTEPS = 5000
AXES = ("seq", "blk")
SMALL = 10


def as_float(value):
    return value.astype(jnp.float32)


def low(value):
    return value.astype(jnp.bfloat16)


def row_dot(left, right):
    return lax.dot_general(left, right, (((0,), (0,)), ((), ())), preferred_element_type=jnp.float32)


def neighbours(low_part, high_part):
    count = lax.axis_size("blk")
    up = [(i, i + 1) for i in range(count - 1)]
    down = [(i + 1, i) for i in range(count - 1)]
    return lax.ppermute(high_part, "blk", up), lax.ppermute(low_part, "blk", down)


def item_of(ends, places):
    return jnp.sum((ends[None, :] <= places[:, None]).astype(jnp.int32), axis=1)


def per_device(fast, inputs, cotangent, timestep, lengths, padding, *shards):
    (time_weight, time_bias, inproj, query_bias, value_bias, outproj, outproj_bias, first_gain, first_shift,
     upward_w, upward_bias, downward_w, downward_bias, second_gain, second_shift) = shards
    small = (time_weight, time_bias, query_bias, value_bias, outproj_bias, first_gain, first_shift,
             downward_bias, second_gain, second_shift)
    tok, width = inputs.shape
    half = MAXLEN
    ext = tok + 2 * half
    hidden = upward_w.shape[1]

    keep_own = low(padding)
    mark = jnp.pad(keep_own.reshape(1, tok), ((0, 15), (0, width - tok)))
    edges = jnp.stack([jnp.concatenate([inputs[:half], mark]), jnp.concatenate([inputs[tok - half :], mark])])

    if fast:
        rows = time_weight.shape[0]
        cols = [v[:, None] for v in small] + [upward_bias.reshape(-1, rows).T]
        cols = jnp.concatenate(cols, axis=1)
        cols = jnp.pad(cols, ((0, 0), (0, 128 - cols.shape[1])))
        *fulls, halo = gather_all(
            (inproj, cols), (1, 1), 0.5, edges, 0
        )
        inproj_f, small_f = [v.reshape(-1, v.shape[-1]) for v in fulls]
        small_f = as_float(small_f.T)
        edges = halo
        upward_bias_f = small_f[SMALL : SMALL + hidden // width]
        upward_bias_f = upward_bias_f.reshape(-1, width // rows, rows).transpose(1, 0, 2).reshape(hidden)
    else:
        edges = jnp.stack(neighbours(*edges))
        whole = lambda v: lax.all_gather(v, AXES, axis=0, tiled=True)
        inproj_f, outproj_f, upward_f, downward_f = map(whole, (inproj, outproj, upward_w, downward_w))
        small_f = [as_float(whole(v)) for v in small]
        upward_bias_f = as_float(whole(upward_bias))
    (time_weight_f, time_bias_f, query_bias_f, value_bias_f, outproj_bias_f, first_gain_f, first_shift_f,
     downward_bias_f, second_gain_f, second_shift_f) = [small_f[i] for i in range(SMALL)]

    offset = lax.axis_index("blk") * tok
    ends = jnp.cumsum(lengths[0]).astype(jnp.int32)
    places = offset - half + jnp.arange(ext, dtype=jnp.int32)
    item = jnp.where(places >= 0, item_of(ends, places), -1)
    keep = jnp.concatenate([edges[0, half, tok - half :], keep_own, edges[1, half, :half]])
    query_feat, key_feat, lane = features(item, places, as_float(keep) > 0.5, lengths.shape[1])

    time_value = as_float(timestep[0]) / TSTEPS
    move = time_value * time_weight_f
    start_vec = as_float(inputs) + move + time_bias_f
    start_low = low(start_vec)
    shift = jnp.pad(jnp.stack([move, time_bias_f]), ((0, 6), (0, 0)))
    bias = jnp.pad(jnp.stack([query_bias_f, jnp.zeros_like(query_bias_f), value_bias_f]), ((0, 5), (0, 0)))
    vec = jnp.stack([move, time_bias_f, outproj_bias_f, first_gain_f, first_shift_f, downward_bias_f, second_gain_f,
                     second_shift_f])
    up_bias = jnp.broadcast_to(upward_bias_f, (8, hidden))
    attention = (edges, shift, start_low, inproj_f, bias, query_feat, key_feat, lane)
    if fast:
        plan = pieces((width, hidden, width), (1, 4, 4), 0.5)
        at = [0, 1, 2, 3, 4, 5, 6, 7, 9, 11, 13, 15, 16]
        results = layer_forward(
            (outproj, upward_w, downward_w), plan, at, *attention, inputs, vec, up_bias, cotangent, 1
        )
        outproj_f, upward_f, downward_f = [v.reshape(-1, v.shape[-1]) for v in results[:3]]
        projected, attended, feat_own, *results = results[3:]
    else:
        projected, attended, feat_own = attn_fwd(*attention)
        results = ffn_forward(downward_f, attended, inputs, outproj_f, upward_f, vec, up_bias, cotangent)
    hidden_low, slope, first_normal, first_inv, first_low, layer_out, grad_second_in, grad_ffn_low, sums = results
    grad_second_gain, grad_second_shift, grad_down_bias = sums[0], sums[1], sums[2]
    sums_forward, sums = sums, jnp.sum(sums[3:6], axis=1)
    backward = functools.partial(
        ffn_backward, hidden_low, grad_ffn_low, downward_f, slope, upward_f, first_low, grad_second_in, first_normal,
        first_inv, vec, attended, outproj_f, feat_own, lane
    )
    grad_down, grad_up_weight, grad_out_weight, grad_up_bias, sums_back, grad_first_in, packed = (
        backward((4,), 0.5, 3) if fast else backward()
    )
    grad_up_bias = grad_up_bias[0]
    grad_first_gain, grad_first_shift, grad_out_bias = sums_back[0], sums_back[1], sums_back[2]
    values = jnp.pad(sums[None], ((0, 7), (0, 125)))
    backward = functools.partial(
        attn_bwd, projected, packed, query_feat, key_feat, delta_key(ext, lane), lane, tok
    )
    if fast:
        edges = packed.reshape(2, half, width + PAIR)
        down_share = grad_down
        out_share, up_share, sums, grad_q, grad_kv = backward(
            edges, values, (grad_out_weight, grad_up_weight), (1, 2), 0.0, 4
        )
    else:
        edges = jnp.stack(neighbours(packed[:half], packed[tok - half :]))
        sums, grad_q, grad_kv = backward(edges, lax.psum(values, AXES))
    sums = sums[0, :3]
    branch_rms = jnp.sqrt(sums / (tok * width * lax.axis_size(AXES)))
    if fast:
        cols = grad_up_bias.reshape(width // rows, -1, rows).transpose(1, 0, 2).reshape(-1, width)
        other = jnp.concatenate([cols, jnp.broadcast_to(time_value, (4, width))])
        input_grad, in_share, last = input_gradients(
            grad_q, grad_kv, start_low, inproj_f, grad_first_in, sums_back, sums_forward, other, 0.5, 5
        )
        small_shares = [last[:, i] for i in range(SMALL)]
        up_bias_share = last[:, SMALL : SMALL + hidden // width].T.reshape(-1)
    else:
        grad_proj_low = jnp.concatenate([grad_q, grad_kv[0], grad_kv[1]], axis=1)
        grad_in_weight = row_dot(start_low, grad_proj_low)
        grad_query_bias = jnp.sum(as_float(grad_q), axis=0)
        grad_value_bias = jnp.sum(as_float(grad_kv[1]), axis=0)
        grad_start = grad_first_in + nt(grad_proj_low, inproj_f)
        grad_time_bias = jnp.sum(grad_start, axis=0)
        grad_time_weight = time_value * grad_time_bias
        input_grad = low(grad_start)
        small_grads = (grad_time_weight, grad_time_bias, grad_query_bias, grad_value_bias, grad_out_bias, grad_first_gain,
                       grad_first_shift, grad_down_bias, grad_second_gain, grad_second_shift)
        share = lambda v: lax.psum_scatter(v, AXES, scatter_dimension=0, tiled=True)
        down_share, up_share, out_share, in_share, up_bias_share = map(
            share, map(as_float, (grad_down, grad_up_weight, grad_out_weight, grad_in_weight, grad_up_bias))
        )
        small_shares = [share(v) for v in small_grads]
    (time_weight_s, time_bias_s, query_bias_s, value_bias_s, out_bias_s, first_gain_s, first_shift_s,
     down_bias_s, second_gain_s, second_shift_s) = small_shares
    return (layer_out, input_grad, time_weight_s, time_bias_s, in_share, query_bias_s, value_bias_s, out_share,
            out_bias_s, first_gain_s, first_shift_s, up_share, up_bias_share, down_share, down_bias_s,
            second_gain_s, second_shift_s, branch_rms)


def solution(mesh):
    both = P(AXES)
    matrix = P(AXES, None)
    in_specs = (matrix, matrix, P("seq"), P("seq", None), both,
                both, both, matrix, both, both, matrix, both, both, both, matrix, both, matrix, both, both, both)
    out_specs = (matrix, matrix, both, both, matrix, both, both, matrix, both, both, both, matrix, both, matrix,
                 both, both, both, P())
    fast = dict(mesh.shape) == {"seq": 4, "blk": 8}
    return jax.shard_map(
        functools.partial(per_device, fast), mesh=mesh, in_specs=in_specs, out_specs=out_specs, check_vma=False
    )
```

```python
import functools

import jax
import jax.numpy as jnp
from jax import lax
from jax.experimental import pallas as pl
from jax.experimental.pallas import tpu as pltpu
from jax.sharding import PartitionSpec as P

HD = 64
TQ = 256
PAIR = 2 * HD
NEG = -(2.0**100)


def nt(a, b):
    return lax.dot_general(a, b, (((1,), (1,)), ((), ())), preferred_element_type=jnp.float32)


def nn(a, b):
    return jnp.dot(a, b, preferred_element_type=jnp.float32)


def spread(first, last, length):
    return [first + (2 * i * (last - first) + length - 1) // (2 * (length - 1)) for i in range(length)]


def place(step, at, job):
    for s in range(at[-1] + 1):
        count = at.count(s)
        if count:

            @pl.when(step == s)
            def _():
                for _ in range(count):
                    next(job)


def attention_body(step, tok, lanes, edges, shift_ref, start_ref, wq, wk, wv, bias_ref, qf_ref, kf_ref,
                   proj_ref, o_ref, f_ref, ka, va, qa, halo):
    half = halo.shape[1]
    ext = tok + 2 * half
    window = 2 * half + TQ
    columns = pl.ds(pl.multiple_of(step * PAIR, PAIR), PAIR)

    @pl.when(step == 0)
    def _():
        for side in range(2):
            for t in range(half // TQ):
                rows = slice(t * TQ, (t + 1) * TQ)
                moved = edges[side, rows, :].astype(jnp.float32) + shift_ref[0:1, :] + shift_ref[1:2, :]
                halo[side, rows, :] = moved.astype(jnp.bfloat16)
        ka[:, PAIR:] = kf_ref[...]
        va[:, PAIR:] = jnp.ones((ext, PAIR), jnp.bfloat16)
        f_ref[...] = qf_ref[half : half + tok, :]

    lane = lax.broadcasted_iota(jnp.int32, (TQ, PAIR), 1)
    left = lane < HD
    for t in range(ext // TQ):
        rows = slice(t * TQ, (t + 1) * TQ)
        if t * TQ < half:
            start = halo[0, rows, :]
        elif t * TQ < half + tok:
            start = start_ref[t * TQ - half : (t + 1) * TQ - half, :]
        else:
            start = halo[1, t * TQ - half - tok : (t + 1) * TQ - half - tok, :]
        q = (nn(start, wq[...]) + bias_ref[0:1, :]).astype(jnp.bfloat16)
        k = (nn(start, wk[...]) + bias_ref[1:2, :]).astype(jnp.bfloat16)
        v = (nn(start, wv[...]) + bias_ref[2:3, :]).astype(jnp.bfloat16)
        proj_ref[0, rows, :] = q
        proj_ref[1, rows, :] = k
        proj_ref[2, rows, :] = v
        ka[rows, :PAIR] = k
        va[rows, :PAIR] = v
        if half <= t * TQ < half + tok:
            own = t - half // TQ
            q = q * jnp.bfloat16(HD**-0.5)
            zero = jnp.zeros_like(q)
            qa[2 * own, :, :PAIR] = jnp.where(left, q, zero)
            qa[2 * own + 1, :, :PAIR] = jnp.where(left, zero, q)
            qa[2 * own, :, PAIR:] = qf_ref[rows, :]
            qa[2 * own + 1, :, PAIR:] = qf_ref[rows, :]
    for t in range(tok // TQ):
        win = slice(t * TQ, t * TQ + window)
        own = slice(t * TQ, (t + 1) * TQ)
        feat = f_ref[own, :]
        out = []
        for side in range(2):
            s = nt(qa[2 * t + side], ka[win, :])
            top = jnp.max(s, axis=1, keepdims=True)
            r = nn(jnp.exp(s - top).astype(jnp.bfloat16), va[win, :])
            total = r[:, PAIR:]
            out.append(r[:, :PAIR] / total)
            rest = top + jnp.log(total)
            for part in range(3):
                piece = rest.astype(jnp.bfloat16)
                rest = rest - piece.astype(jnp.float32)
                feat = jnp.where(lane == lanes + part * 16 + 2 * step + side, piece, feat)
        o_ref[own, columns] = jnp.where(left, out[0], out[1]).astype(jnp.bfloat16)
        f_ref[own, :] = feat


def fwd_kernel(tok, lanes, *refs):
    attention_body(pl.program_id(0), tok, lanes, *refs)


def fixed(*shape):
    return pl.BlockSpec(shape, lambda i: (0,) * len(shape), pipeline_mode=pl.Buffered(1))


def attention_specs(tok, ext, width):
    half, last = (ext - tok) // 2, width // PAIR - 1
    col = lambda base: pl.BlockSpec((width, PAIR), lambda i: (0, base * (last + 1) + lax.min(i, last)))
    ins = [fixed(2, half, width), fixed(8, width), fixed(tok, width), col(0), col(1), col(2),
           pl.BlockSpec((8, PAIR), lambda i: (0, lax.min(i, last))), fixed(ext, PAIR), fixed(ext, PAIR)]
    outs = [pl.BlockSpec((3, ext, PAIR), lambda i: (0, 0, lax.min(i, last))), fixed(tok, width), fixed(tok, PAIR)]
    shape, low = jax.ShapeDtypeStruct, jnp.bfloat16
    shapes = [shape((3, ext, width), low), shape((tok, width), low), shape((tok, PAIR), low)]
    scratch = [pltpu.VMEM((ext, 2 * PAIR), low), pltpu.VMEM((ext, 2 * PAIR), low),
               pltpu.VMEM((2 * tok // TQ, TQ, 2 * PAIR), low), pltpu.VMEM((2, half, width), low)]
    return ins, outs, shapes, scratch


def attn_fwd(edges, shift, start, inproj, bias, qf, kf, lanes):
    tok, width = start.shape
    ins, outs, shapes, scratch = attention_specs(tok, tok + 2 * (edges.shape[1] - 16), width)
    return pl.pallas_call(
        functools.partial(fwd_kernel, tok, lanes),
        grid=(width // PAIR,), in_specs=ins, out_specs=outs, out_shape=shapes, scratch_shapes=scratch,
        compiler_params=pltpu.CompilerParams(vmem_limit_bytes=56 << 20, dimension_semantics=("arbitrary",)),
        name="attention",
    )(edges, shift, start, inproj, inproj, inproj, bias, qf, kf)


def bwd_kernel(plan, count, counts, tok, lanes, *refs):
    grads, refs = refs[:count], refs[count:]
    edges, values, refs = refs[0], refs[1], refs[2:]
    q_ref, k_ref, v_ref, d_ref, qf_ref, own_ref, kf_ref, vf_ref, refs = *refs[:8], refs[8:]
    outs, refs = refs[:count], refs[count:]
    result, gq_ref, gkv_ref, refs = *refs[:3], refs[3:]
    one, two, feats, halo, refs = *refs[:4], refs[4:]
    step = pl.program_id(0)
    ext = k_ref.shape[1]
    half = (ext - tok) // 2
    window = 2 * half + TQ
    pairs = BWD_STEPS // 2
    pair = lax.rem(step, pairs)
    if count:
        send_sem, recv_sem, local_sem, sums, refs = *refs[:4], refs[4:]
        pos = Place()

        @pl.when(step == 0)
        def _():
            meet(pos, True)

        sends = Sends(send_sem, recv_sem, pos.to)

        at = [0, 3, 6, 8, 11, 13, 15]
        ready = max(i for i, s in enumerate(at) if s <= pairs)

        def work():
            neighbour = halo_plan(pos, edges, halo, sends, local_sem, len(plan))
            total = total_plan(values, result, sums, sends)
            next(neighbour)
            for i, _ in enumerate(scatter_job(pos, plan, counts, grads, outs, refs, sends, local_sem)):
                if i < 6:
                    next(total)
                if i == ready:
                    next(neighbour)
                yield

        place(step, at, work())
    else:

        @pl.when(step == 0)
        def _():
            halo[...] = edges[...]
            result[...] = values[...]

    lane = lax.broadcasted_iota(jnp.int32, (TQ, PAIR), 1)
    left = lane < HD

    @pl.when(step == 0)
    def _():
        one[2, :, PAIR:] = kf_ref[...]
        two[2, :, PAIR:] = vf_ref[...]
        feats[half : half + tok, :] = own_ref[...]

    @pl.when(step == pairs)
    def _():
        for t in range(half // TQ):
            for side, base in ((0, 0), (1, half + tok)):
                rows = slice(base + t * TQ, base + (t + 1) * TQ)
                got = halo[side, t * TQ : (t + 1) * TQ, PAIR * pairs :]
                feats[rows, :] = jnp.where(lane < lanes, qf_ref[rows, :], got)

    def sides(tile, rows, d):
        q = q_ref[0, rows, :] * jnp.bfloat16(HD**-0.5)
        feat = feats[rows, :]
        zero = jnp.zeros_like(q)
        for side in range(2):
            mine = left if side == 0 else ~left
            kept = jnp.where((lane < lanes) | (lax.rem(lane - lanes + 128, 16) == 2 * pair + side), feat, zero)
            one[side, rows, :PAIR] = jnp.where(mine, q, zero)
            one[side, rows, PAIR:] = kept
            two[side, rows, :PAIR] = jnp.where(mine, d, zero)
            two[side, rows, PAIR:] = kept

    one[2, :, :PAIR] = k_ref[0]
    two[2, :, :PAIR] = v_ref[0]
    for t in range(tok // TQ):
        sides(t, slice(half + t * TQ, half + (t + 1) * TQ), d_ref[t * TQ : (t + 1) * TQ, :])

    @pl.when(step < pairs)
    def _():
        for t in range(tok // TQ):
            win = slice(t * TQ, t * TQ + window)
            rows = slice(half + t * TQ, half + (t + 1) * TQ)
            parts = []
            for side in range(2):
                p = jnp.exp(nt(one[side, rows, :], one[2, win, :]))
                g = (p * nt(two[side, rows, :], two[2, win, :])).astype(jnp.bfloat16)
                parts.append(nn(g, k_ref[0, win, :]))
            gq_ref[t * TQ : (t + 1) * TQ, :] = (jnp.where(left, *parts) * HD**-0.5).astype(jnp.bfloat16)

    @pl.when(step >= pairs)
    def _():
        at = pl.ds(pl.multiple_of(pair * PAIR, PAIR), PAIR)
        for t in range(half // TQ):
            for side, base in ((0, 0), (1, half + tok)):
                sides(t, slice(base + t * TQ, base + (t + 1) * TQ), halo[side, t * TQ : (t + 1) * TQ, at])
        for t in range(tok // TQ):
            win = slice(t * TQ, t * TQ + window)
            rows = slice(half + t * TQ, half + (t + 1) * TQ)
            dk, dv = 0.0, 0.0
            for side in range(2):
                p = jnp.exp(nt(one[2, rows, :], one[side, win, :]))
                g = (p * nt(two[2, rows, :], two[side, win, :])).astype(jnp.bfloat16)
                dk = dk + nn(g, one[side, win, :PAIR])
                dv = dv + nn(p.astype(jnp.bfloat16), two[side, win, :PAIR])
            gkv_ref[0, t * TQ : (t + 1) * TQ, :] = dk.astype(jnp.bfloat16)
            gkv_ref[1, t * TQ : (t + 1) * TQ, :] = dv.astype(jnp.bfloat16)


BWD_STEPS = 16


def attn_bwd(proj, packed, qf, kf, vf, lanes, tok, edges, values, grads=(), parts=(), share=0.0, collective=None):
    _, ext, width = proj.shape
    pairs = width // PAIR
    half = (ext - tok) // 2
    grads, plan, counts, bufs, shapes = scatter_layout(grads, parts, share)
    count = len(grads)
    anywhere, vmem = pl.BlockSpec(memory_space=pl.ANY), pl.BlockSpec(memory_space=pltpu.VMEM)
    third = lambda k: pl.BlockSpec((1, ext, PAIR), lambda i: (k, 0, lax.rem(i, pairs)))
    fix = lambda rows: pl.BlockSpec((rows, PAIR), lambda i: (0, 0))
    comm = dict(collective_id=collective, has_side_effects=True) if count else {}
    scratch = [
        pltpu.VMEM((3, ext, 2 * PAIR), jnp.bfloat16),
        pltpu.VMEM((3, ext, 2 * PAIR), jnp.bfloat16),
        pltpu.VMEM((ext, PAIR), jnp.bfloat16),
        pltpu.VMEM((2, half, width + PAIR), jnp.bfloat16),
    ]
    if count:
        scratch += semaphores(len(plan) * SENDS + 7, len(plan) + 1) + [pltpu.VMEM((10, 8, 128), jnp.float32)] + bufs
    return pl.pallas_call(
        functools.partial(bwd_kernel, plan, count, counts, tok, lanes),
        grid=(2 * pairs,),
        in_specs=[anywhere] * count
        + [anywhere if count else vmem, vmem, third(0), third(1), third(2),
           pl.BlockSpec((tok, PAIR), lambda i: (0, lax.rem(i, pairs))), fix(ext),
           pl.BlockSpec((tok, PAIR), lambda i: (0, pairs)), fix(ext), fix(ext)],
        out_specs=[vmem] * count
        + [vmem, pl.BlockSpec((tok, PAIR), lambda i: (0, lax.min(i, pairs - 1))),
           pl.BlockSpec((2, tok, PAIR), lambda i: (0, 0, lax.max(i - pairs, 0)))],
        out_shape=shapes
        + [jax.ShapeDtypeStruct(values.shape, jnp.float32), jax.ShapeDtypeStruct((tok, width), jnp.bfloat16),
           jax.ShapeDtypeStruct((2, tok, width), jnp.bfloat16)],
        scratch_shapes=scratch,
        compiler_params=pltpu.CompilerParams(
            vmem_limit_bytes=62 << 20, dimension_semantics=("arbitrary",), **comm
        ),
        name="attention_gradients",
    )(*grads, edges, values, proj, proj, proj, packed, qf, packed, kf, vf)


def features(item, places, keep, n_items):
    ext = item.shape[0]
    nb = (n_items + 1).bit_length()
    pb = (ext - 1).bit_length()
    lanes = 2 * (nb + pb)
    assert lanes + 80 <= PAIR and ext == 1 << pb
    lane = jnp.arange(PAIR, dtype=jnp.int32)
    of_item = lane < 2 * nb
    shift = jnp.where(of_item, lane % nb, (lane - 2 * nb) % pb)
    turned = jnp.where(of_item, lane // nb, (lane - 2 * nb) // pb)
    bit = ((jnp.where(of_item, (item + 1)[:, None], places[:, None]) >> shift) ^ turned) & 1
    used = lane < lanes
    active = of_item == keep[:, None]
    qf = jnp.where(used, bit, 0)
    kf = jnp.where(used, jnp.where(active & (bit == 0), NEG, 0.0), jnp.where(lane < lanes + 48, -1.0, 0.0))
    return qf.astype(jnp.bfloat16), kf.astype(jnp.bfloat16), lanes


def delta_key(ext, lanes):
    lane = jnp.arange(PAIR)
    vf = jnp.where((lane >= lanes + 48) & (lane < lanes + 80), -1.0, 0.0)
    return jnp.broadcast_to(vf[None], (ext, PAIR)).astype(jnp.bfloat16)


MESH = pl.DeviceIdType.MESH


class Place:
    def __init__(self):
        seq, blk = lax.axis_index("seq"), lax.axis_index("blk")
        self.seq, self.blk, self.last = seq, blk, lax.axis_size("blk") - 1
        self.x, self.c, self.z, self.y = x, c, z, y = seq // 2, lax.rem(seq, 2), blk // 2, lax.rem(blk, 2)
        self.nx, self.nc, self.ny = nx, nc, ny = 1 - x, 1 - c, 1 - y
        low_bit, high_bit = lax.rem(z, 2), z // 2
        flips = {1: (1 - low_bit, high_bit), 2: (low_bit, 1 - high_bit), 3: (1 - low_bit, 1 - high_bit)}
        self.nz = {k: high * 2 + bit for k, (bit, high) in flips.items()}
        device = lambda x, c, z, y: (x * 2 + c, z * 2 + y)
        self.to = {"x": device(nx, c, z, y), "y": device(x, c, z, ny), "c": device(x, nc, z, y)}
        for k in (1, 2, 3):
            self.to[k] = device(x, c, self.nz[k], y)
        self.below = (seq, lax.max(blk - 1, 0))
        self.above = (seq, lax.min(blk + 1, self.last))


class Copy:
    def __init__(self, make):
        self.make = make

    def start(self):
        self.make().start()
        return self

    def wait(self):
        self.make().wait()

    def wait_send(self):
        self.make().wait_send()

    def wait_recv(self):
        self.make().wait_recv()


def local_copy(src, dst, sems, at):
    return Copy(lambda: pltpu.make_async_copy(src(), dst(), sems.at[at])).start()


class Sends:
    def __init__(self, send_sem, recv_sem, to):
        self.send_sem, self.recv_sem, self.to, self.used, self.live = send_sem, recv_sem, to, 0, []

    def describe(self, src, dst, device):
        at = self.used
        self.used += 1
        return Copy(
            lambda: pltpu.make_async_remote_copy(
                src_ref=src(), dst_ref=dst(), send_sem=self.send_sem.at[at], recv_sem=self.recv_sem.at[at],
                device_id=device, device_id_type=MESH,
            )
        )

    def start(self, src, dst, partner):
        copy = self.describe(src, dst, self.to[partner]).start()
        self.live.append(copy)
        return copy

    def finish(self):
        for copy in self.live:
            copy.wait_send()


def gather_plan(pos, shard, full, sends, local, number, base, wide, at):
    x, c, z, y, nx, nc, ny = pos.x, pos.c, pos.z, pos.y, pos.nx, pos.nc, pos.ny
    every, one, two = pl.ds(base, wide), pl.ds(base, at), pl.ds(base + at, wide - at)

    def send(partner, *index):
        return sends.start(lambda: full.at[index], lambda: full.at[index], partner)

    rows = slice(None)
    source, target = lambda: shard.at[:, every], lambda: full.at[x, c, z, y, :, every]
    own = local_copy(source, target, local, number)
    line = [sends.start(source, target, k) for k in (1, 2, 3)]
    yield
    own.wait()
    for copy in line:
        copy.wait_recv()
    if at:
        a = send("x", x, c, rows, y, rows, one)
    b = send("y", x, c, rows, y, rows, two)
    core = [send("c", x, c, rows, y, rows, every)]
    yield
    if at:
        a.wait_recv()
        a2 = send("y", rows, c, rows, y, rows, one)
        core.append(send("c", nx, c, rows, y, rows, one))
    b.wait_recv()
    b2 = send("x", x, c, rows, rows, rows, two)
    core.append(send("c", x, c, rows, ny, rows, two))
    yield
    if at:
        a2.wait_recv()
        core.append(send("c", rows, c, rows, ny, rows, one))
    b2.wait_recv()
    core.append(send("c", nx, c, rows, rows, rows, two))
    yield
    for copy in core:
        copy.wait_recv()
    yield


SENDS = 12


def turns(plans, last, begin=None):
    begin = begin or list(range(len(plans)))
    for turn in range(begin[-1] + 5):
        for k in reversed(range(len(plans))):
            if 0 <= turn - begin[k] <= 4:
                next(plans[k])
        if turn == begin[-1] + 4:
            last()
        yield


def pieces(widths, parts, share):
    plan = []
    for k, (whole, count) in enumerate(zip(widths, parts)):
        wide = whole // count
        plan += [(k, p * wide, wide, int(wide * share) // 128 * 128) for p in range(count)]
    return plan


def halo_plan(pos, edges, halo, sends, local, number):
    blk, last = pos.blk, pos.last
    down = sends.describe(lambda: edges.at[0], lambda: halo.at[1], pos.below)
    up = sends.describe(lambda: edges.at[1], lambda: halo.at[0], pos.above)
    fill = [
        Copy(lambda k=k: pltpu.make_async_copy(edges.at[k], halo.at[k], local.at[number])) for k in (0, 1)
    ]

    def where(test, *acts):
        @pl.when(test)
        def _():
            for act in acts:
                act()

    where(blk > 0, down.start)
    where(blk < last, up.start)
    where(blk == 0, fill[0].start)
    where(blk == last, fill[1].start)
    yield
    where(blk > 0, down.wait_send, up.wait_recv)
    where(blk < last, up.wait_send, down.wait_recv)
    where(blk == 0, fill[0].wait)
    where(blk == last, fill[1].wait)
    yield


def meet(pos, halo):
    barrier = pltpu.get_barrier_semaphore()
    for device in pos.to.values():
        pl.semaphore_signal(barrier, inc=1, device_id=device, device_id_type=MESH)
    count = len(pos.to)
    if halo:

        @pl.when(pos.blk > 0)
        def _():
            pl.semaphore_signal(barrier, inc=1, device_id=pos.below, device_id_type=MESH)

        @pl.when(pos.blk < pos.last)
        def _():
            pl.semaphore_signal(barrier, inc=1, device_id=pos.above, device_id_type=MESH)

        count = count + 2 - jnp.where(pos.blk == 0, 1, 0) - jnp.where(pos.blk == pos.last, 1, 0)
    pl.semaphore_wait(barrier, count)


def gather_job(pos, plan, shards, fulls, sends, local):
    yield from turns([
        gather_plan(pos, shards[k], fulls[k], sends, local, i, base, wide, at) for i, (k, base, wide, at) in enumerate(plan)
    ], sends.finish)


def gather_kernel(plan, count, *refs):
    shards, edges, fulls, halo = refs[:count], refs[count], refs[count + 1 : 2 * count + 1], refs[2 * count + 1]
    send_sem, recv_sem, local_sem = refs[2 * count + 2 :]
    pos = Place()
    meet(pos, True)
    sends = Sends(send_sem, recv_sem, pos.to)
    neighbour = halo_plan(pos, edges, halo, sends, local_sem, len(plan))
    next(neighbour)
    for _ in gather_job(pos, plan, shards, fulls, sends, local_sem):
        pass
    next(neighbour)


def semaphores(number, local):
    return [pltpu.SemaphoreType.DMA((number,)), pltpu.SemaphoreType.DMA((number,)), pltpu.SemaphoreType.DMA((local,))]


def full_shapes(shards):
    return [jax.ShapeDtypeStruct((2, 2, 4, 2) + v.shape, jnp.bfloat16) for v in shards]


def gather_all(shards, parts, share, edges, collective):
    count = len(shards)
    plan = pieces([v.shape[1] for v in shards], parts, share)
    anywhere = pl.BlockSpec(memory_space=pl.ANY)
    return pl.pallas_call(
        functools.partial(gather_kernel, plan, count),
        in_specs=[anywhere] * (count + 1),
        out_specs=[anywhere] * (count + 1),
        out_shape=full_shapes(shards) + [jax.ShapeDtypeStruct(edges.shape, edges.dtype)],
        scratch_shapes=semaphores(len(plan) * SENDS + 2, len(plan) + 1),
        compiler_params=pltpu.CompilerParams(collective_id=collective, has_side_effects=True),
        name="gather_weights",
    )(*shards, edges)


def widen(value):
    return value.astype(jnp.float32)


def scatter_plan(pos, grad, out, bufs, sends, local, number, base, wide, at, held=False):
    x, c, z, y, nx, nc, ny = pos.x, pos.c, pos.z, pos.y, pos.nx, pos.nc, pos.ny
    every, one, two = pl.ds(base, wide), pl.ds(0, at), pl.ds(at, wide - at)
    if held:
        own, bufs = lambda: grad.at[:, c, :, :, :, every], (None,) + tuple(bufs)
    else:
        own = lambda: bufs[0]
    got, one1, two1, one2, two2, line, ends = bufs[1:] if at else bufs[1:2] + (None,) + bufs[2:3] + (None,) + bufs[3:]
    if not held:
        load = local_copy(lambda: grad.at[:, c, :, :, :, every], own, local, number)
    cross = sends.start(lambda: grad.at[:, nc, :, :, :, every], lambda: got, "c")
    yield
    if not held:
        load.wait()
    cross.wait_recv()

    @pl.loop(0, 8)
    def _(i):
        mine = own().at[i // 4, lax.rem(i, 4)]
        mine[...] = mine[...] + got[i // 4, lax.rem(i, 4)]

    if at:
        a = sends.start(lambda: own().at[:, :, ny, :, one], lambda: one1, "y")
    b = sends.start(lambda: own().at[nx, :, :, :, two], lambda: two1, "x")
    yield
    if at:
        a.wait_recv()

        @pl.loop(0, 8)
        def _(i):
            one1[i // 4, lax.rem(i, 4)] = own().at[i // 4, lax.rem(i, 4), y, :, one][...] + one1[i // 4, lax.rem(i, 4)]

        a2 = sends.start(lambda: one1.at[nx], lambda: one2, "x")
    b.wait_recv()

    @pl.loop(0, 4)
    def _(i):
        two1[i] = own().at[x, i, :, :, two][...] + two1[i]

    b2 = sends.start(lambda: two1.at[:, ny], lambda: two2, "y")
    yield
    if at:
        a2.wait_recv()
    b2.wait_recv()

    @pl.loop(0, 4)
    def _(i):
        if at:
            line[i, :, :at] = one1[x, i] + one2[i]
        line[i, :, at:] = two1[i, y] + two2[i]

    last = [
        sends.start(lambda k=k: line.at[pos.nz[k]], lambda k=k: ends.at[k - 1], k) for k in (1, 2, 3)
    ]
    yield
    for copy in last:
        copy.wait_recv()
    out[:, base : base + wide] = widen(line[z]) + widen(ends[0]) + widen(ends[1]) + widen(ends[2])
    yield


def scatter_bufs(rows, wide, at, held=False):
    shapes = [(2, 4, 2, rows, wide)] * (1 if held else 2)
    if at:
        shapes += [(2, 4, rows, at), (4, 2, rows, wide - at), (4, rows, at)]
    else:
        shapes += [(4, 2, rows, wide)]
    shapes += [(4, rows, wide - at), (4, rows, wide), (3, rows, wide)]
    return [pltpu.VMEM(s, jnp.bfloat16) for s in shapes]


def total_plan(values, result, bufs, sends):
    partners = ("c", "x", "y", 1, 2)
    for i, partner in enumerate(partners):
        source = (lambda i=i: bufs.at[2 * i - 1]) if i else (lambda: values)
        copy = sends.start(source, lambda i=i: bufs.at[2 * i], partner)
        yield
        copy.wait_recv()
        total = source()[...] + bufs[2 * i]
        if i + 1 < len(partners):
            bufs[2 * i + 1] = total
        else:
            result[...] = total
    yield


def scatter_job(pos, plan, counts, grads, outs, bufs, sends, local, held=False, begin=None):
    plans = []
    for i, (k, base, wide, at) in enumerate(plan):
        first = sum(counts[:i])
        mine = bufs[first : first + counts[i]]
        plans.append(scatter_plan(pos, grads[k], outs[k], mine, sends, local, i, base, wide, at, held))
    yield from turns(plans, sends.finish, begin)


def scatter_layout(grads, parts, share):
    grads = [v.reshape(2, 2, 4, 2, v.shape[0] // 32, v.shape[1]) for v in grads]
    plan = pieces([v.shape[-1] for v in grads], parts, share)
    bufs = [scatter_bufs(grads[k].shape[-2], wide, at) for k, base, wide, at in plan]
    shapes = [jax.ShapeDtypeStruct(v.shape[-2:], jnp.float32) for v in grads]
    return grads, plan, [len(b) for b in bufs], sum(bufs, []), shapes


def scatter_kernel(plan, count, counts, *refs):
    grads, outs, refs = refs[:count], refs[count : 2 * count], refs[2 * count :]
    send_sem, recv_sem, local_sem = refs[:3]
    pos = Place()
    meet(pos, False)
    sends = Sends(send_sem, recv_sem, pos.to)
    for _ in scatter_job(pos, plan, counts, grads, outs, refs[3:], sends, local_sem):
        pass


def scatter_all(grads, parts, share, collective):
    count = len(grads)
    grads, plan, counts, bufs, shapes = scatter_layout(grads, parts, share)
    anywhere, vmem = pl.BlockSpec(memory_space=pl.ANY), pl.BlockSpec(memory_space=pltpu.VMEM)
    return pl.pallas_call(
        functools.partial(scatter_kernel, plan, count, counts),
        in_specs=[anywhere] * count,
        out_specs=[vmem] * count,
        out_shape=shapes,
        scratch_shapes=semaphores(len(plan) * SENDS, len(plan)) + bufs,
        compiler_params=pltpu.CompilerParams(
            collective_id=collective, has_side_effects=True, vmem_limit_bytes=58 << 20
        ),
        name="sum_gradients",
    )(*grads)


FT = 512
ROWS = 256


def normalize(values):
    centered = values - jnp.mean(values, axis=1, keepdims=True)
    inv = lax.rsqrt(jnp.mean(centered * centered, axis=1, keepdims=True) + 1e-05)
    return centered * inv, inv


def normalize_back(grad, normal, inv):
    return inv * (
        grad - jnp.mean(grad, axis=1, keepdims=True) - normal * jnp.mean(grad * normal, axis=1, keepdims=True)
    )


def column_sum(values):
    return jnp.sum(values, axis=0, keepdims=True)


def ffn_body(step, ups, whole_weight, up_weight, att, inp, wo, vec, ub, cot, hid, slope, normal_ref, inv_ref, low_ref,
             out_ref, grad_ref, grad_low_ref, sums, keep, wd, low):
    tok = att.shape[0]

    @pl.when(step == 0)
    def _():
        sums[...] = jnp.zeros_like(sums)
        for r in range(tok // ROWS):
            rows = slice(r * ROWS, (r + 1) * ROWS)
            branch = nn(att[rows, :], wo().reshape(-1, att.shape[1])) + vec[2:3, :]
            start = inp[rows, :].astype(jnp.float32) + vec[0:1, :] + vec[1:2, :]
            normal, inv = normalize(start + branch)
            normal_ref[rows, :] = normal
            inv_ref[rows, :] = jnp.broadcast_to(inv, (ROWS, 128))
            first = (normal * vec[3:4, :] + vec[4:5, :]).astype(jnp.bfloat16)
            low[rows, :] = first
            low_ref[:, rows] = first.T
            sums[3:4, :] += column_sum(start * start)
            sums[4:5, :] += column_sum(branch * branch)

    @pl.when((step >= 0) & (step < ups))
    def _():
        at = pl.ds(pl.multiple_of(step * FT, FT), FT)
        for r in range(tok // ROWS):
            rows = slice(r * ROWS, (r + 1) * ROWS)
            up = nn(low[rows, :], up_weight()) + ub[0:1, at]
            phi = 0.5 * (1.0 + lax.erf(up * 2.0**-0.5))
            h = (up * phi).astype(jnp.bfloat16)
            hid[:, rows] = h.T
            keep[rows, at] = h
            slope[rows, :] = (phi + up * (jnp.exp(-0.5 * up * up) * 0.3989422804014327)).astype(jnp.bfloat16)

    @pl.when(step == ups)
    def _():
        whole_weight()

    @pl.when(step >= ups)
    def _():
        rows = pl.ds(pl.multiple_of((step - ups) * ROWS, ROWS), ROWS)
        weight = wd[...].reshape(-1, wd.shape[-1])
        branch = nn(keep[rows, :], weight) + vec[5:6, :]
        first = normal_ref[rows, :] * vec[3:4, :] + vec[4:5, :]
        normal, inv = normalize(first + branch)
        out_ref[...] = (normal * vec[6:7, :] + vec[7:8, :]).astype(jnp.bfloat16)
        g = cot[...].astype(jnp.float32)
        grad = normalize_back(g * vec[6:7, :], normal, inv)
        grad_ref[...] = grad
        low_grad = grad.astype(jnp.bfloat16)
        grad_low_ref[...] = low_grad
        sums[0:1, :] += column_sum(g * normal)
        sums[1:2, :] += column_sum(g)
        sums[2:3, :] += column_sum(low_grad.astype(jnp.float32))
        sums[5:6, :] += column_sum(branch * branch)


def ffn_specs(tok, width, wide, wd_shape, begin):
    ups = wide // FT
    f32, low, shape = jnp.float32, jnp.bfloat16, jax.ShapeDtypeStruct
    now = lambda i: lax.max(lax.min(i - begin, ups - 1), 0)
    row = pl.BlockSpec((ROWS, width), lambda i: (lax.max(i - begin - ups, 0), 0))
    ins = [fixed(8, width), fixed(8, wide), row]
    outs = [pl.BlockSpec((FT, tok), lambda i: (now(i), 0)), pl.BlockSpec((tok, FT), lambda i: (0, now(i))),
            fixed(tok, width), fixed(tok, 128), fixed(width, tok), row, row, row, fixed(8, width)]
    shapes = [shape((wide, tok), low), shape((tok, wide), low), shape((tok, width), f32), shape((tok, 128), f32),
              shape((width, tok), low), shape((tok, width), low), shape((tok, width), f32), shape((tok, width), low),
              shape((8, width), f32)]
    scratch = [pltpu.VMEM((tok, wide), low), pltpu.VMEM(wd_shape, low), pltpu.VMEM((tok, width), low)]
    return ins, outs, shapes, scratch


def ffn_kernel(ups, *refs):
    down, att, inp, wo, wu, refs = *refs[:5], refs[5:]
    load, wd = refs[-1], refs[-3]

    def whole_weight():
        copy = pltpu.make_async_copy(down, wd, load)
        copy.start()
        copy.wait()

    ffn_body(pl.program_id(0), ups, whole_weight, lambda: wu[...], att, inp, lambda: wo[...], *refs[:-1])


def ffn_forward(down, att, inp, wo, wu, vec, ub, cot):
    tok, width = att.shape
    wide = wu.shape[1]
    ups = wide // FT
    ins, outs, shapes, scratch = ffn_specs(tok, width, wide, down.shape, 0)
    return pl.pallas_call(
        functools.partial(ffn_kernel, ups),
        grid=(ups + tok // ROWS,),
        in_specs=[pl.BlockSpec(memory_space=pl.ANY), fixed(tok, width), fixed(tok, width), fixed(width, width),
                  pl.BlockSpec((width, FT), lambda i: (0, lax.min(i, ups - 1)))] + ins,
        out_specs=outs, out_shape=shapes, scratch_shapes=scratch + [pltpu.SemaphoreType.DMA],
        compiler_params=pltpu.CompilerParams(vmem_limit_bytes=62 << 20, dimension_semantics=("arbitrary",)),
        name="feed_forward",
    )(down, att, inp, wo, wu, vec, ub, cot)


def layer_kernel(plan, at, ups, tok, lanes, *refs):
    shards, refs = refs[:3], refs[3:]
    attention_in, refs = refs[:9], refs[9:]
    inp, ffn_in, refs = refs[0], refs[1:4], refs[4:]
    fulls, refs = refs[:3], refs[3:]
    attention_out, ffn_out, refs = refs[:3], refs[3:12], refs[12:]
    attention_scratch, ffn_scratch, refs = refs[:4], refs[4:7], refs[7:]
    wo, wu, load, send_sem, recv_sem, local_sem = refs
    step = pl.program_id(0)
    begin = attention_out[1].shape[1] // PAIR
    pos = Place()

    @pl.when(step == 0)
    def _():
        meet(pos, False)

    sends = Sends(send_sem, recv_sem, pos.to)
    place(step, at, gather_job(pos, plan, shards, fulls, sends, local_sem))

    @pl.when(step < begin)
    def _():
        attention_body(step, tok, lanes, *attention_in, *attention_out, *attention_scratch)

    turn = step - begin
    wo_load = Copy(lambda: pltpu.make_async_copy(fulls[0], wo, load.at[2]))
    wd_load = Copy(lambda: pltpu.make_async_copy(fulls[2], ffn_scratch[1], load.at[2]))

    def wu_load(k):
        slot = lax.rem(k, 2)
        columns = pl.ds(pl.multiple_of(k * FT, FT), FT)
        return pltpu.make_async_copy(fulls[1].at[:, :, :, :, :, columns], wu.at[slot], load.at[slot])

    @pl.when(turn == 0)
    def _():
        wo_load.start()
        wu_load(0).start()
        wo_load.wait()

    @pl.when((turn >= 0) & (turn < ups - 1))
    def _():
        wu_load(turn + 1).start()

    @pl.when((turn >= 0) & (turn < ups))
    def _():
        wu_load(turn).wait()

    def whole_weight():
        wd_load.start()
        wd_load.wait()

    ffn_body(turn, ups, whole_weight, lambda: wu[lax.rem(turn, 2)].reshape(-1, FT), attention_out[1], inp,
             lambda: wo[...], *ffn_in, *ffn_out, *ffn_scratch)


def layer_forward(shards, plan, at, edges, shift, start, inproj, bias, qf, kf, lanes, inp, vec, ub, cot, collective):
    tok, width = start.shape
    wide = ub.shape[1]
    ups, begin = wide // FT, width // PAIR
    low = jnp.bfloat16
    ins, outs, shapes, scratch = attention_specs(tok, tok + 2 * (edges.shape[1] - 16), width)
    ffn_ins, ffn_outs, ffn_shapes, ffn_scratch = ffn_specs(tok, width, wide, (2, 2, 4, 2) + shards[2].shape, begin)
    anywhere = pl.BlockSpec(memory_space=pl.ANY)
    rows = shards[0].shape[0]
    return pl.pallas_call(
        functools.partial(layer_kernel, plan, at, ups, tok, lanes),
        grid=(begin + ups + tok // ROWS,),
        in_specs=[anywhere] * 3 + ins + [fixed(tok, width)] + ffn_ins,
        out_specs=[anywhere] * 3 + outs + ffn_outs,
        out_shape=full_shapes(shards) + shapes + ffn_shapes,
        scratch_shapes=scratch + ffn_scratch
        + [pltpu.VMEM((2, 2, 4, 2, rows, width), low), pltpu.VMEM((2, 2, 2, 4, 2, rows, FT), low),
           pltpu.SemaphoreType.DMA((3,))] + semaphores(len(plan) * SENDS, len(plan)),
        compiler_params=pltpu.CompilerParams(
            vmem_limit_bytes=63 << 20, dimension_semantics=("arbitrary",), collective_id=collective, has_side_effects=True
        ),
        name="layer_forward",
    )(*shards, edges, shift, start, inproj, inproj, inproj, bias, qf, kf, inp, vec, ub, cot)


def tn(a, b):
    return lax.dot_general(a, b, (((0,), (0,)), ((), ())), preferred_element_type=jnp.float32)


def back_kernel(plan, count, counts, ups, lanes, *refs):
    hid, gffn, wd, slope, wu, first_low, gsecond, normal_ref, inv_ref, vec, att, wo, feat_ref = refs[:13]
    down, up_grad, out_grad, up_sum, sums, gin_ref, packed, acc, piece, low_grad = refs[13:23]
    refs = refs[23:]
    step = pl.program_id(0)
    tok, width = gffn.shape
    last = 2 * ups + tok // ROWS - 1
    if count:
        dwd, send_sem, recv_sem, local_sem, bufs = *refs[:4], refs[4:]
        pos = Place()

        @pl.when(step == ups)
        def _():
            meet(pos, False)

        sends = Sends(send_sem, recv_sem, pos.to)
        job = scatter_job(pos, plan, counts, [dwd], [down], bufs, sends, local_sem, True)
        place(step, spread(ups, last, len(plan) + 4), job)

    @pl.when(step < ups)
    def _():
        grad = nn(hid[...], gffn[...]).astype(jnp.bfloat16)
        if count:
            each = dwd.shape[4]
            for k in range(FT // each):
                at = step * (FT // each) + k
                dwd[at // 16, lax.rem(at // 8, 2), lax.rem(at // 2, 4), lax.rem(at, 2)] = grad[k * each : (k + 1) * each]
        else:
            down[pl.ds(pl.multiple_of(step * FT, FT), FT), :] = grad

    @pl.when((step >= ups) & (step < 2 * ups))
    def _():
        total = jnp.zeros((1, FT), jnp.float32)
        for r in range(tok // ROWS):
            rows = slice(r * ROWS, (r + 1) * ROWS)
            g = (nt(gffn[rows, :], wd[...]) * slope[rows, :].astype(jnp.float32)).astype(jnp.bfloat16)
            piece[rows, :] = g
            total += column_sum(g.astype(jnp.float32))
            more = nt(g, wu[...])

            @pl.when(step == ups)
            def _():
                acc[rows, :] = more

            @pl.when(step > ups)
            def _():
                acc[rows, :] += more

        up_sum[...] = jnp.broadcast_to(total, (8, FT))
        up_grad[...] = nn(first_low[...], piece[...]).astype(jnp.bfloat16)

    @pl.when(step == 2 * ups)
    def _():
        sums[...] = jnp.zeros_like(sums)

    @pl.when(step >= 2 * ups)
    def _():
        rows = pl.ds(pl.multiple_of((step - 2 * ups) * ROWS, ROWS), ROWS)
        g = gsecond[...] + acc[rows, :]
        normal = normal_ref[...]
        grad = normalize_back(g * vec[3:4, :], normal, inv_ref[:, :1])
        gin_ref[...] = grad
        low = grad.astype(jnp.bfloat16)
        low_grad[rows, :] = low
        sums[0:1, :] += column_sum(g * normal)
        sums[1:2, :] += column_sum(g)
        sums[2:3, :] += column_sum(low.astype(jnp.float32))
        gatt = nt(low, wo[...]).astype(jnp.bfloat16)
        packed[:, :width] = gatt
        both = gatt.astype(jnp.float32) * att[rows, :].astype(jnp.float32)
        lane = lax.broadcasted_iota(jnp.int32, (width, PAIR), 1)
        head = lax.broadcasted_iota(jnp.int32, (width, PAIR), 0) // HD
        pick = (lane >= lanes + 48) & (lane < lanes + 80) & (lax.rem(lane - lanes + 128, 16) == head)
        pick = jnp.where(pick, 1.0, 0.0).astype(jnp.bfloat16)
        high = both.astype(jnp.bfloat16)
        delta = nn(high, pick) + nn((both - high.astype(jnp.float32)).astype(jnp.bfloat16), pick)
        first = delta.astype(jnp.bfloat16)
        second = (delta - first.astype(jnp.float32)).astype(jnp.bfloat16)
        lane = lax.broadcasted_iota(jnp.int32, (ROWS, PAIR), 1)
        feat = feat_ref[...]
        feat = jnp.where((lane >= lanes + 48) & (lane < lanes + 64), first, feat)
        packed[:, width:] = jnp.where((lane >= lanes + 64) & (lane < lanes + 80), second, feat)

    @pl.when(step == last)
    def _():
        for k in range(2):
            cols = slice(k * width // 2, (k + 1) * width // 2)
            out_grad[cols, :] = tn(att[:, cols], low_grad[...]).astype(jnp.bfloat16)


def ffn_backward(hid, gffn, wd, slope, wu, first_low, gsecond, normal, inv, vec, att, wo, feat, lanes, parts=(), share=0.0,
                 collective=None):
    wide, tok = hid.shape
    width = gffn.shape[1]
    ups, downs = wide // FT, tok // ROWS
    count = 1 if parts else 0
    f32, low = jnp.float32, jnp.bfloat16
    shape = jax.ShapeDtypeStruct
    vmem = pl.BlockSpec(memory_space=pltpu.VMEM)
    whole = lambda r, c: pl.BlockSpec((r, c), lambda i: (0, 0), pipeline_mode=pl.Buffered(1))
    middle = lambda i: lax.max(lax.min(i - ups, ups - 1), 0)
    tile = pl.BlockSpec((tok, FT), lambda i: (0, middle(i)))
    row = lambda c: pl.BlockSpec((ROWS, c), lambda i: (lax.max(i - 2 * ups, 0), 0))
    scratch = [pltpu.VMEM((tok, width), f32), pltpu.VMEM((tok, FT), low), pltpu.VMEM((tok, width), low)]
    plan, counts, down, comm = [], [], shape((wide, width), low), {}
    if count:
        rows = wide // 32
        plan = pieces([width], parts, share)
        bufs = [scatter_bufs(rows, w, at, True) for _, _, w, at in plan]
        counts = [len(b) for b in bufs]
        scratch += [pltpu.VMEM((2, 2, 4, 2, rows, width), low)] + semaphores(len(plan) * SENDS, len(plan)) + sum(bufs, [])
        down, comm = shape((rows, width), f32), dict(collective_id=collective, has_side_effects=True)
    return pl.pallas_call(
        functools.partial(back_kernel, plan, count, counts, ups, lanes),
        grid=(2 * ups + downs,),
        in_specs=[pl.BlockSpec((FT, tok), lambda i: (lax.min(i, ups - 1), 0)), whole(tok, width),
                  pl.BlockSpec((FT, width), lambda i: (middle(i), 0)), tile,
                  pl.BlockSpec((width, FT), lambda i: (0, middle(i))), whole(width, tok), row(width), row(width), row(128),
                  whole(8, width), whole(tok, width), whole(width, width), row(PAIR)],
        out_specs=[vmem, pl.BlockSpec((width, FT), lambda i: (0, middle(i))), whole(width, width),
                   pl.BlockSpec((8, FT), lambda i: (0, middle(i))), whole(8, width), row(width), row(width + PAIR)],
        out_shape=[down, shape((width, wide), low), shape((width, width), low), shape((8, wide), f32),
                   shape((8, width), f32), shape((tok, width), f32), shape((tok, width + PAIR), low)],
        scratch_shapes=scratch,
        compiler_params=pltpu.CompilerParams(vmem_limit_bytes=62 << 20, dimension_semantics=("arbitrary",), **comm),
        name="feed_forward_gradients",
    )(hid, gffn, wd, slope, wu, first_low, gsecond, normal, inv, vec, att, wo, feat)


def tail_kernel(plan, counts, *refs):
    gq, gkv, start, wt, gin, near, far, other, out_ref, in_share, small_share, sums = refs[:12]
    held, held_small, send_sem, recv_sem, local_sem, bufs = *refs[12:17], refs[17:]
    step = pl.program_id(0)
    width = start.shape[1]
    pos = Place()

    @pl.when(step == 0)
    def _():
        meet(pos, False)
        sums[...] = jnp.zeros_like(sums)

    sends = Sends(send_sem, recv_sem, pos.to)
    last = 3 + gq.shape[0] // ROWS
    job = scatter_job(pos, plan, counts, [held, held_small], [in_share, small_share], bufs, sends, local_sem, True, [0, 1, 3, 3])

    def keep(k, grad):
        for half in range(2):
            cols = slice(half * width // 2, (half + 1) * width // 2)
            part = tn(start[...], grad[:, cols]).astype(jnp.bfloat16).reshape(held.shape[:5] + (width // 2,))
            held[:, :, :, :, :, k * width + half * width // 2 : k * width + (half + 1) * width // 2] = part

    @pl.when(step == last)
    def _():
        lines = [other[4:5, :] * sums[1:2, :], sums[1:2, :], sums[2:3, :], sums[3:4, :], near[2:3, :], near[0:1, :],
                 near[1:2, :], far[2:3, :], far[0:1, :], far[1:2, :]] + [other[k : k + 1, :] for k in range(4)]
        row = lax.broadcasted_iota(jnp.int32, (128, width), 0)
        total = jnp.zeros((128, width), jnp.float32)
        for k, line in enumerate(lines):
            total = jnp.where(row == k, line, total)
        held_small[...] = total.T.astype(jnp.bfloat16).reshape(held_small.shape)

    place(step, [1, 2, 4] + [last] * 5, job)

    @pl.when(step == 0)
    def _():
        keep(0, gq)

    @pl.when(step == 1)
    def _():
        keep(1, gkv.at[0])

    @pl.when(step == last - 1)
    def _():
        keep(2, gkv.at[1])

    @pl.when((step >= 2) & (step < last - 1))
    def _():
        rows = pl.ds(pl.multiple_of((step - 2) * ROWS, ROWS), ROWS)
        q, k, v = gq[rows, :], gkv[0, rows, :], gkv[1, rows, :]
        total = gin[...] + nt(q, wt[:, :width]) + nt(k, wt[:, width : 2 * width]) + nt(v, wt[:, 2 * width :])
        out_ref[...] = total.astype(jnp.bfloat16)
        sums[1:2, :] += column_sum(total)
        sums[2:3, :] += column_sum(q.astype(jnp.float32))
        sums[3:4, :] += column_sum(v.astype(jnp.float32))


def input_gradients(gq, gkv, start, wt, gin, near, far, other, share, collective):
    tok, width = start.shape
    rows = width // 32
    plan = pieces([3 * width, 128], (3, 1), share)
    bufs = [scatter_bufs(rows, w, at, True) for _, _, w, at in plan]
    f32, low = jnp.float32, jnp.bfloat16
    shape = jax.ShapeDtypeStruct
    vmem = pl.BlockSpec(memory_space=pltpu.VMEM)
    row = pl.BlockSpec((ROWS, width), lambda i: (lax.max(lax.min(i - 2, tok // ROWS - 1), 0), 0))
    fix = lambda *s: pl.BlockSpec(s, lambda i: (0,) * len(s), pipeline_mode=pl.Buffered(1))
    return pl.pallas_call(
        functools.partial(tail_kernel, plan, [len(b) for b in bufs]),
        grid=(4 + tok // ROWS,),
        in_specs=[fix(tok, width), fix(2, tok, width), fix(tok, width), fix(width, 3 * width), row] + [fix(8, width)] * 3,
        out_specs=[row, vmem, vmem],
        out_shape=[shape((tok, width), low), shape((rows, 3 * width), f32), shape((rows, 128), f32)],
        scratch_shapes=[pltpu.VMEM((8, width), f32), pltpu.VMEM((2, 2, 4, 2, rows, 3 * width), low),
                        pltpu.VMEM((2, 2, 4, 2, rows, 128), low)]
        + semaphores(len(plan) * SENDS, len(plan)) + sum(bufs, []),
        compiler_params=pltpu.CompilerParams(
            vmem_limit_bytes=62 << 20, dimension_semantics=("arbitrary",), collective_id=collective, has_side_effects=True
        ),
        name="input_gradients",
    )(gq, gkv, start, wt, gin, near, far, other)


H = 16
MAXLEN = 512
TSTEPS = 5000
AXES = ("seq", "blk")
SMALL = 10


def as_float(value):
    return value.astype(jnp.float32)


def low(value):
    return value.astype(jnp.bfloat16)


def row_dot(left, right):
    return lax.dot_general(left, right, (((0,), (0,)), ((), ())), preferred_element_type=jnp.float32)


def neighbours(low_part, high_part):
    count = lax.axis_size("blk")
    up = [(i, i + 1) for i in range(count - 1)]
    down = [(i + 1, i) for i in range(count - 1)]
    return lax.ppermute(high_part, "blk", up), lax.ppermute(low_part, "blk", down)


def item_of(ends, places):
    return jnp.sum((ends[None, :] <= places[:, None]).astype(jnp.int32), axis=1)


def per_device(fast, inputs, cotangent, timestep, lengths, padding, *shards):
    (time_weight, time_bias, inproj, query_bias, value_bias, outproj, outproj_bias, first_gain, first_shift,
     upward_w, upward_bias, downward_w, downward_bias, second_gain, second_shift) = shards
    small = (time_weight, time_bias, query_bias, value_bias, outproj_bias, first_gain, first_shift,
             downward_bias, second_gain, second_shift)
    tok, width = inputs.shape
    half = MAXLEN
    ext = tok + 2 * half
    hidden = upward_w.shape[1]

    keep_own = low(padding)
    mark = jnp.pad(keep_own.reshape(1, tok), ((0, 15), (0, width - tok)))
    edges = jnp.stack([jnp.concatenate([inputs[:half], mark]), jnp.concatenate([inputs[tok - half :], mark])])

    if fast:
        rows = time_weight.shape[0]
        cols = [v[:, None] for v in small] + [upward_bias.reshape(-1, rows).T]
        cols = jnp.concatenate(cols, axis=1)
        cols = jnp.pad(cols, ((0, 0), (0, 128 - cols.shape[1])))
        *fulls, halo = gather_all(
            (inproj, cols), (1, 1), 0.5, edges, 0
        )
        inproj_f, small_f = [v.reshape(-1, v.shape[-1]) for v in fulls]
        small_f = as_float(small_f.T)
        edges = halo
        upward_bias_f = small_f[SMALL : SMALL + hidden // width]
        upward_bias_f = upward_bias_f.reshape(-1, width // rows, rows).transpose(1, 0, 2).reshape(hidden)
    else:
        edges = jnp.stack(neighbours(*edges))
        whole = lambda v: lax.all_gather(v, AXES, axis=0, tiled=True)
        inproj_f, outproj_f, upward_f, downward_f = map(whole, (inproj, outproj, upward_w, downward_w))
        small_f = [as_float(whole(v)) for v in small]
        upward_bias_f = as_float(whole(upward_bias))
    (time_weight_f, time_bias_f, query_bias_f, value_bias_f, outproj_bias_f, first_gain_f, first_shift_f,
     downward_bias_f, second_gain_f, second_shift_f) = [small_f[i] for i in range(SMALL)]

    offset = lax.axis_index("blk") * tok
    ends = jnp.cumsum(lengths[0]).astype(jnp.int32)
    places = offset - half + jnp.arange(ext, dtype=jnp.int32)
    item = jnp.where(places >= 0, item_of(ends, places), -1)
    keep = jnp.concatenate([edges[0, half, tok - half :], keep_own, edges[1, half, :half]])
    query_feat, key_feat, lane = features(item, places, as_float(keep) > 0.5, lengths.shape[1])

    time_value = as_float(timestep[0]) / TSTEPS
    move = time_value * time_weight_f
    start_vec = as_float(inputs) + move + time_bias_f
    start_low = low(start_vec)
    shift = jnp.pad(jnp.stack([move, time_bias_f]), ((0, 6), (0, 0)))
    bias = jnp.pad(jnp.stack([query_bias_f, jnp.zeros_like(query_bias_f), value_bias_f]), ((0, 5), (0, 0)))
    vec = jnp.stack([move, time_bias_f, outproj_bias_f, first_gain_f, first_shift_f, downward_bias_f, second_gain_f,
                     second_shift_f])
    up_bias = jnp.broadcast_to(upward_bias_f, (8, hidden))
    attention = (edges, shift, start_low, inproj_f, bias, query_feat, key_feat, lane)
    if fast:
        plan = pieces((width, hidden, width), (1, 4, 4), 0.5)
        at = [0, 1, 2, 3, 4, 5, 7, 8, 9, 11, 13, 15, 16]
        results = layer_forward(
            (outproj, upward_w, downward_w), plan, at, *attention, inputs, vec, up_bias, cotangent, 1
        )
        outproj_f, upward_f, downward_f = [v.reshape(-1, v.shape[-1]) for v in results[:3]]
        projected, attended, feat_own, *results = results[3:]
    else:
        projected, attended, feat_own = attn_fwd(*attention)
        results = ffn_forward(downward_f, attended, inputs, outproj_f, upward_f, vec, up_bias, cotangent)
    hidden_low, slope, first_normal, first_inv, first_low, layer_out, grad_second_in, grad_ffn_low, sums = results
    grad_second_gain, grad_second_shift, grad_down_bias = sums[0], sums[1], sums[2]
    sums_forward, sums = sums, jnp.sum(sums[3:6], axis=1)
    backward = functools.partial(
        ffn_backward, hidden_low, grad_ffn_low, downward_f, slope, upward_f, first_low, grad_second_in, first_normal,
        first_inv, vec, attended, outproj_f, feat_own, lane
    )
    grad_down, grad_up_weight, grad_out_weight, grad_up_bias, sums_back, grad_first_in, packed = (
        backward((4,), 0.5, 3) if fast else backward()
    )
    grad_up_bias = grad_up_bias[0]
    grad_first_gain, grad_first_shift, grad_out_bias = sums_back[0], sums_back[1], sums_back[2]
    values = jnp.pad(sums[None], ((0, 7), (0, 125)))
    backward = functools.partial(
        attn_bwd, projected, packed, query_feat, key_feat, delta_key(ext, lane), lane, tok
    )
    if fast:
        edges = packed.reshape(2, half, width + PAIR)
        down_share = grad_down
        out_share, up_share, sums, grad_q, grad_kv = backward(
            edges, values, (grad_out_weight, grad_up_weight), (1, 2), 0.0, 4
        )
    else:
        edges = jnp.stack(neighbours(packed[:half], packed[tok - half :]))
        sums, grad_q, grad_kv = backward(edges, lax.psum(values, AXES))
    sums = sums[0, :3]
    branch_rms = jnp.sqrt(sums / (tok * width * lax.axis_size(AXES)))
    if fast:
        cols = grad_up_bias.reshape(width // rows, -1, rows).transpose(1, 0, 2).reshape(-1, width)
        other = jnp.concatenate([cols, jnp.broadcast_to(time_value, (4, width))])
        input_grad, in_share, last = input_gradients(
            grad_q, grad_kv, start_low, inproj_f, grad_first_in, sums_back, sums_forward, other, 0.5, 5
        )
        small_shares = [last[:, i] for i in range(SMALL)]
        up_bias_share = last[:, SMALL : SMALL + hidden // width].T.reshape(-1)
    else:
        grad_proj_low = jnp.concatenate([grad_q, grad_kv[0], grad_kv[1]], axis=1)
        grad_in_weight = row_dot(start_low, grad_proj_low)
        grad_query_bias = jnp.sum(as_float(grad_q), axis=0)
        grad_value_bias = jnp.sum(as_float(grad_kv[1]), axis=0)
        grad_start = grad_first_in + nt(grad_proj_low, inproj_f)
        grad_time_bias = jnp.sum(grad_start, axis=0)
        grad_time_weight = time_value * grad_time_bias
        input_grad = low(grad_start)
        small_grads = (grad_time_weight, grad_time_bias, grad_query_bias, grad_value_bias, grad_out_bias, grad_first_gain,
                       grad_first_shift, grad_down_bias, grad_second_gain, grad_second_shift)
        share = lambda v: lax.psum_scatter(v, AXES, scatter_dimension=0, tiled=True)
        down_share, up_share, out_share, in_share, up_bias_share = map(
            share, map(as_float, (grad_down, grad_up_weight, grad_out_weight, grad_in_weight, grad_up_bias))
        )
        small_shares = [share(v) for v in small_grads]
    (time_weight_s, time_bias_s, query_bias_s, value_bias_s, out_bias_s, first_gain_s, first_shift_s,
     down_bias_s, second_gain_s, second_shift_s) = small_shares
    return (layer_out, input_grad, time_weight_s, time_bias_s, in_share, query_bias_s, value_bias_s, out_share,
            out_bias_s, first_gain_s, first_shift_s, up_share, up_bias_share, down_share, down_bias_s,
            second_gain_s, second_shift_s, branch_rms)


def solution(mesh):
    both = P(AXES)
    matrix = P(AXES, None)
    in_specs = (matrix, matrix, P("seq"), P("seq", None), both,
                both, both, matrix, both, both, matrix, both, both, both, matrix, both, matrix, both, both, both)
    out_specs = (matrix, matrix, both, both, matrix, both, both, matrix, both, both, both, matrix, both, matrix,
                 both, both, both, P())
    fast = dict(mesh.shape) == {"seq": 4, "blk": 8}
    return jax.shard_map(
        functools.partial(per_device, fast), mesh=mesh, in_specs=in_specs, out_specs=out_specs, check_vma=False
    )
```
